32 devices in a mesh: ctx: 16 (over z, y, core), fsdp: 2 (over x).
Axes of the slice: x: 2, y: 2, z: 4, core: 2. Of those that a mesh axis runs over, the one named last changes fastest.
Arguments:
- tokens: bfloat16 [2, 2048, 768], P('fsdp', 'ctx'), may hold values from -6 to 6
- cotangent: bfloat16 [2, 2048, 768], P('fsdp', 'ctx'), may hold values from -6 to 6
- lengths: int32 [2, 4], P('fsdp'), may hold values from 1 to 1024, 2048 in all within a row
- dealing: int32 [2, 2048], P('fsdp', 'ctx'), may hold values from 0 to 2047, each once within a row
- gain_one: bfloat16 [768], P('fsdp'), may hold values from 0.25 to 1.75
- w_query: bfloat16 [768, 768], P('fsdp'), may hold values from -0.109375 to 0.109375
- w_key: bfloat16 [768, 768], P('fsdp'), may hold values from -0.109375 to 0.109375
- w_value: bfloat16 [768, 768], P('fsdp'), may hold values from -0.21875 to 0.21875
- w_out: bfloat16 [768, 768], P('fsdp'), may hold values from -0.875 to 0.875
- gain_two: bfloat16 [768], P('fsdp'), may hold values from 0.25 to 1.75
- w_in: bfloat16 [768, 3072], P('fsdp'), may hold values from -0.21875 to 0.21875
- w_ff: bfloat16 [3072, 768], P('fsdp'), may hold values from -0.15625 to 0.15625
- rel_table: bfloat16 [32, 12], P('fsdp'), may hold values from -4 to 4
Outputs:
- output: bfloat16 [2, 2048, 768], P('fsdp', 'ctx')
- grad_tokens: float32 [2, 2048, 768], P('fsdp', 'ctx')
- grad_gain_one: float32 [768], P('fsdp')
- grad_w_query: float32 [768, 768], P('fsdp')
- grad_w_key: float32 [768, 768], P('fsdp')
- grad_w_value: float32 [768, 768], P('fsdp')
- grad_w_out: float32 [768, 768], P('fsdp')
- grad_gain_two: float32 [768], P('fsdp')
- grad_w_in: float32 [768, 3072], P('fsdp')
- grad_w_ff: float32 [3072, 768], P('fsdp')
- grad_rel_table: float32 [32, 12], P('fsdp')
The draws below stay inside these ranges and needn't reach their ends.
Inputs may be any that keep to these rules, and one draw needn't show every extreme that they name: Each group's 4 lengths add up to 2048 and the longest is 1024. `dealing`: each group's row is a permutation of the packed places 0 to 2047.
All inputs are finite; a program needn't handle non-finite values.
Results may differ from the reference program's by a relative error of at most 0.018.
Values may be sent and summed in bfloat16 or wider, within the bound.
No kernel may reach another device: no remote copies, remote signals or barrier semaphores. Data moves between devices by JAX's collectives and lax.ppermute only.
A program may use at most 256 MiB of HBM per device.

```python
import math
import jax
import jax.numpy as jnp
import numpy as np
from jax import lax

D = 768
H = 12
DH = 64
FF = 3072
BUCKETS = 32
SEQS = 4
GROUP_TOK = 2048
MOST = 1024
N_FSDP = 2


def block_scale(stream_key, dims, pieces, smallest, high):
    factor_of, own = 1.0, jax.random.fold_in(stream_key, 6)
    for dim, parts in pieces:
        steps = jnp.exp(jax.random.uniform(jax.random.fold_in(own, dim), (parts,), jnp.float32, smallest / len(pieces), high / len(pieces)))
        factor_of = factor_of * jnp.repeat(steps, dims[dim] // parts).reshape([-1 if axis == dim else 1 for axis in range(len(dims))])
    return factor_of


def split_up(number_of, total, reach, lean):
    portions = [(1 << 20) // math.isqrt(standing ** lean) + 1 for standing in range(2, number_of + 1)]
    surplus, holding = total - reach - (number_of - 1), [1] * (number_of - 1)
    while surplus > 0:
        candidates = [i for i in range(number_of - 1) if holding[i] < reach]
        mass, remaining = sum([portions[i] for i in candidates]), surplus
        for i in candidates:
            addition = min(reach - holding[i], max(1, remaining * portions[i] // mass), surplus)
            holding[i] = holding[i] + addition
            surplus = surplus - addition
    return np.array([reach] + holding)


def uneven_parts(key, number_of, total, most, lean):
    if number_of == 2:
        one = jax.random.randint(key, (), max(1, total - most), min(most, total - 1) + 1)
        return jnp.stack([one, total - one])
    tallies = jnp.asarray(split_up(number_of, total, most, lean), jnp.int32)
    pairs = (number_of - 1) // 2
    source_of, sink = tallies[1:1 + 2 * pairs:2], tallies[2:2 + 2 * pairs:2]
    slack = jnp.minimum(source_of - 1, most - sink)
    shifted = jax.random.randint(jax.random.fold_in(key, 1), (pairs,), 0, 1 << 20) % (slack + 1)
    tallies = tallies.at[1:1 + 2 * pairs:2].set(source_of - shifted).at[2:2 + 2 * pairs:2].set(sink + shifted)
    return tallies[jax.random.permutation(jax.random.fold_in(key, 2), number_of)]


def scatter_about(stream_key, dims, scale, most, cuts=(), kind=jnp.bfloat16):
    drawn = jax.random.normal(stream_key, dims, jnp.float32) * scale
    if len(cuts) > 0:
        drawn = block_scale(stream_key, dims, cuts, -0.22, 0.18) * drawn
    return jnp.clip(drawn, min=-most, max=most).astype(kind)


def setup_inputs(seed: int = 0) -> dict:
    streams_of = jax.random.split(jax.random.key(seed), 14)
    tokens = scatter_about(streams_of[0], (N_FSDP, GROUP_TOK, D), 1.0, 6.0, ((0, 2), (1, 16)))
    cotangent = scatter_about(streams_of[1], (N_FSDP, GROUP_TOK, D), 1.0, 6.0, ((0, 2), (1, 16)))
    lengths = jax.vmap(lambda own: uneven_parts(own, SEQS, GROUP_TOK, MOST, 2))(jax.random.split(streams_of[2], N_FSDP)).reshape((N_FSDP, SEQS)).astype(jnp.int32)
    dealing = jax.vmap(lambda own: jax.random.permutation(own, GROUP_TOK))(jax.random.split(streams_of[3], N_FSDP)).reshape((N_FSDP, GROUP_TOK)).astype(jnp.int32)
    gain_one = jnp.clip(1.0 + 0.15 * jax.random.normal(streams_of[4], (D,), jnp.float32), 0.25, 1.75).astype(jnp.bfloat16)
    w_query = scatter_about(streams_of[5], (D, D), 0.018, 0.109375, ((0, 2),))
    w_key = scatter_about(streams_of[6], (D, D), 0.018, 0.109375, ((0, 2),))
    w_value = scatter_about(streams_of[7], (D, D), D ** -0.5, 0.21875, ((0, 2),))
    w_out = scatter_about(streams_of[8], (D, D), (D // 16) ** -0.5, 0.875, ((0, 2),))
    gain_two = jnp.clip(1.0 + 0.15 * jax.random.normal(streams_of[9], (D,), jnp.float32), 0.25, 1.75).astype(jnp.bfloat16)
    w_in = scatter_about(streams_of[10], (D, FF), D ** -0.5, 0.21875, ((0, 2),))
    w_ff = scatter_about(streams_of[11], (FF, D), (FF // 2) ** -0.5, 0.15625, ((0, 2),))
    rel_table = scatter_about(streams_of[12], (BUCKETS, H), 1.0, 4.0, ((0, 2),))
    return dict(tokens=tokens, cotangent=cotangent, lengths=lengths, dealing=dealing, gain_one=gain_one, w_query=w_query, w_key=w_key, w_value=w_value, w_out=w_out, gain_two=gain_two, w_in=w_in, w_ff=w_ff, rel_table=rel_table)


@jax.custom_vjp
def low(v):
    return lax.optimization_barrier(v.astype(jnp.bfloat16)).astype(jnp.float32)

@jax.custom_vjp
def low_back(v):
    return v

def low_keep(v):
    return (low(v), None)

def low_pass(kept, grad):
    return (grad,)

def back_keep(v):
    return (v, None)

def back_low(kept, grad):
    return (low(grad),)
low.defvjp(low_keep, low_pass)
low_back.defvjp(back_keep, back_low)
EPS = 1e-06
NEG = -1000000000.0
THRESHOLDS = (1, 2, 3, 4, 5, 6, 7, 8, 12, 16, 23, 32, 46, 64, 91)

def bucket_of(offset):
    distance = jnp.abs(offset).astype(jnp.int32)
    counted = jnp.zeros(offset.shape, jnp.int32)
    for threshold in THRESHOLDS:
        counted = counted + (distance >= threshold).astype(jnp.int32)
    return (counted + BUCKETS // 2 * (offset > 0).astype(jnp.int32)).astype(jnp.int32)

def places(packed, seq_lengths):
    seq_ends = jnp.cumsum(seq_lengths.astype(jnp.int32), dtype=jnp.int32).astype(jnp.int32)
    passed = (packed[:, None] >= seq_ends[None, :]).astype(jnp.int32)
    segment = lax.optimization_barrier(jnp.sum(passed, axis=1, dtype=jnp.int32)).astype(jnp.int32)
    starts = lax.optimization_barrier(jnp.sum(passed * seq_lengths[None, :].astype(jnp.int32), axis=1, dtype=jnp.int32)).astype(jnp.int32)
    return ((packed.astype(jnp.int32) - starts).astype(jnp.int32), segment)

def normalize(values, scale_gain):
    return values * lax.rsqrt(lax.optimization_barrier(jnp.mean(values * values, axis=-1, keepdims=True)) + EPS) * scale_gain

def matmul(left, right):
    return jnp.dot(left, right, precision=lax.Precision.HIGHEST)

def attention(queries, keys_all, values_all, rel_table, position, segment):
    total_rows = queries.shape[0]
    block_rows = math.gcd(total_rows, 512)
    bucket_ids = jnp.arange(BUCKETS, dtype=jnp.int32)

    def one_block(block_index):
        first_row = (block_index * block_rows).astype(jnp.int32)
        query_blk = lax.dynamic_slice_in_dim(queries, first_row, block_rows, 0)
        pos_blk = lax.dynamic_slice_in_dim(position, first_row, block_rows, 0)
        seg_blk = lax.dynamic_slice_in_dim(segment, first_row, block_rows, 0)
        scores = jnp.einsum('qhd,khd->hqk', query_blk, keys_all, precision=lax.Precision.HIGHEST)
        bucket = bucket_of(position[None, :] - pos_blk[:, None])
        one_hot = (bucket[:, :, None] == bucket_ids[None, None, :]).astype(jnp.float32)
        bias = jnp.einsum('qkb,bh->hqk', one_hot, rel_table, precision=lax.Precision.HIGHEST)
        scores = low_back(scores + bias)
        allowed = (seg_blk[:, None] == segment[None, :])[None]
        probs = jax.nn.softmax(jnp.where(allowed, scores, NEG), axis=-1)
        return jnp.einsum('hqk,khd->qhd', probs, values_all, precision=lax.Precision.HIGHEST)
    checked = jax.checkpoint(one_block)

    def step(carry, block_index):
        return (carry, checked(block_index))
    unused, blocks = lax.scan(step, jnp.zeros((), jnp.int32), jnp.arange(total_rows // block_rows, dtype=jnp.int32))
    return blocks.reshape(total_rows, -1)

def layer(tokens32, gain_one, w_query, w_key, w_value, w_out, gain_two, w_in, w_ff, rel_table, positions, segments):
    results = []
    for group_index in range(N_FSDP):
        inputs = tokens32[group_index]
        head_split = (inputs.shape[0], H, DH)
        normed_one = low(normalize(inputs, gain_one))
        queries = low(low_back(matmul(normed_one, w_query))).reshape(head_split)
        keys_all = low(low_back(matmul(normed_one, w_key))).reshape(head_split)
        values_all = low(low_back(matmul(normed_one, w_value))).reshape(head_split)
        mixed = attention(queries, keys_all, values_all, rel_table, positions[group_index], segments[group_index])
        mixed = low(low_back(mixed))
        resid = inputs + low_back(matmul(mixed, w_out))
        normed_two = low(normalize(resid, gain_two))
        gate_pre = low_back(matmul(normed_two, w_in))
        active = low(jax.nn.gelu(gate_pre, approximate=True))
        results.append(resid + matmul(active, w_ff))
    return jnp.stack(results)

def reference(tokens, cotangent, lengths, dealing, gain_one, w_query, w_key, w_value, w_out, gain_two, w_in, w_ff, rel_table):
    pos_list = []
    seg_list = []
    for group_index in range(N_FSDP):
        position, segment = places(dealing[group_index], lengths[group_index])
        pos_list.append(position)
        seg_list.append(segment)
    positions = jnp.stack(pos_list).astype(jnp.int32)
    segments = jnp.stack(seg_list).astype(jnp.int32)
    floats = tuple((member.astype(jnp.float32) for member in (tokens, gain_one, w_query, w_key, w_value, w_out, gain_two, w_in, w_ff, rel_table)))

    def forward(*values):
        return layer(*values, positions, segments)
    output, pullback = jax.vjp(forward, *floats)
    grads = pullback(cotangent.astype(jnp.float32))
    return (output.astype(jnp.bfloat16), grads[0], grads[1], grads[2], grads[3], grads[4], grads[5], grads[6], grads[7], grads[8], grads[9])
```

```python
import functools
import jax
import jax.numpy as jnp
from jax import lax
from jax.experimental import pallas as pl
from jax.experimental.pallas import tpu as pltpu
from jax.sharding import PartitionSpec as P

BUCKETS = 32
EPS = 1e-06
NEG = -1000000000.0
THRESHOLDS = (1, 2, 3, 4, 5, 6, 7, 8, 12, 16, 23, 32, 46, 64, 91)
VMEM_BYTES = 50 * 1024 * 1024


def dot_nt(left, right):
    return lax.dot_general(left, right, (((1,), (1,)), ((), ())), preferred_element_type=jnp.float32)


def dot_tn(left, right):
    return lax.dot_general(left, right, (((0,), (0,)), ((), ())), preferred_element_type=jnp.float32)


def pair_rows(block, half):
    lane = lax.broadcasted_iota(jnp.int32, block.shape, 1)
    zero = jnp.zeros_like(block)
    return jnp.concatenate(
        [jnp.where(lane < half, block, zero), jnp.where(lane < half, zero, block)], axis=0
    )


def pair_blocks(acc, half, rows):
    return jnp.concatenate([acc[:half, :rows], acc[half:, rows:]], axis=0)


def bias_of(row, index):
    return jnp.take_along_axis(jnp.broadcast_to(row, index.shape), index, axis=1)


def attend_kernel(tile, q_ref, k_ref, v_ref, idx_ref, tab_ref, o_ref, lse_ref, m_out, p_ref, s_scr, m_scr, l_scr, acc_scr):
    chunk, n_chunks = pl.program_id(1), pl.num_programs(1)
    rows = q_ref.shape[0]
    half = q_ref.shape[1] // 2
    keys = k_ref.shape[0]

    @pl.when(chunk == 0)
    def _():
        m_scr[...] = jnp.full_like(m_scr, -3.0e38)
        l_scr[...] = jnp.zeros_like(l_scr)
        acc_scr[...] = jnp.zeros_like(acc_scr)

    q_cat = pair_rows(q_ref[...], half)
    m_old = m_scr[...]
    m_tiles = jnp.full((8, 2 * rows), -3.0e38, jnp.float32)
    for t in range(keys // tile):
        rng = slice(t * tile, (t + 1) * tile)
        s = dot_nt(k_ref[rng, :], q_cat)
        index = idx_ref[rng, :]
        s = s + jnp.concatenate(
            [bias_of(tab_ref[0, j : j + 1, :], index) for j in range(2)], axis=1
        )
        s_scr[rng, :] = s
        m_tiles = jnp.maximum(m_tiles, jnp.max(s.reshape(tile // 8, 8, 2 * rows), axis=0))
    m_new = jnp.maximum(m_old, jnp.max(m_tiles, axis=0, keepdims=True))
    fade = jnp.exp(m_old - m_new)
    sums = jnp.zeros((8, 2 * rows), jnp.float32)
    acc = acc_scr[...] * fade
    for t in range(keys // tile):
        rng = slice(t * tile, (t + 1) * tile)
        p = jnp.exp(s_scr[rng, :] - m_new)
        sums = sums + jnp.sum(p.reshape(tile // 8, 8, 2 * rows), axis=0)
        p_low = p.astype(jnp.bfloat16)
        p_ref[0, rng, :] = p_low[:, :rows]
        p_ref[1, rng, :] = p_low[:, rows:]
        acc = acc + dot_tn(v_ref[rng, :], p_low)
    acc_scr[...] = acc
    l_new = l_scr[...] * fade + jnp.sum(sums, axis=0, keepdims=True)
    l_scr[...] = l_new
    m_scr[...] = m_new
    m_out[0, 0] = m_new

    @pl.when(chunk == n_chunks - 1)
    def _():
        lse_ref[0] = m_new + jnp.log(l_new)
        o_ref[...] = jnp.transpose(pair_blocks(acc / l_new, half, rows))


def attend(projected, index, table, rows, chunk_keys, tile=512):
    total, width = projected.shape[0], projected.shape[1] // 3
    heads = table.shape[0] * 2
    pairs = table.shape[0]
    wide = width // pairs
    n_chunks = total // chunk_keys
    return pl.pallas_call(
        functools.partial(attend_kernel, tile),
        grid=(pairs, n_chunks),
        in_specs=[
            pl.BlockSpec((rows, wide), lambda p, c: (0, p)),
            pl.BlockSpec((chunk_keys, wide), lambda p, c: (c, pairs + p)),
            pl.BlockSpec((chunk_keys, wide), lambda p, c: (c, 2 * pairs + p)),
            pl.BlockSpec((chunk_keys, rows), lambda p, c: (c, 0)),
            pl.BlockSpec((1, 2, 128), lambda p, c: (p, 0, 0)),
        ],
        out_specs=[
            pl.BlockSpec((rows, wide), lambda p, c: (0, p)),
            pl.BlockSpec((1, 1, 2 * rows), lambda p, c: (p, 0, 0)),
            pl.BlockSpec((1, 1, 1, 2 * rows), lambda p, c: (p, c, 0, 0)),
            pl.BlockSpec((2, chunk_keys, rows), lambda p, c: (p, c, 0)),
        ],
        out_shape=[
            jax.ShapeDtypeStruct((rows, width), jnp.float32),
            jax.ShapeDtypeStruct((pairs, 1, 2 * rows), jnp.float32),
            jax.ShapeDtypeStruct((pairs, n_chunks, 1, 2 * rows), jnp.float32),
            jax.ShapeDtypeStruct((heads, total, rows), jnp.bfloat16),
        ],
        scratch_shapes=[
            pltpu.VMEM((chunk_keys, 2 * rows), jnp.float32),
            pltpu.VMEM((1, 2 * rows), jnp.float32),
            pltpu.VMEM((1, 2 * rows), jnp.float32),
            pltpu.VMEM((wide, 2 * rows), jnp.float32),
        ],
        compiler_params=pltpu.CompilerParams(vmem_limit_bytes=VMEM_BYTES),
        name="attend",
    )(projected, projected, projected, index, table)


def query_back_kernel(tile, p_ref, v_ref, k_ref, da_ref, delta_ref, lse_ref, m_ref, ds_ref, dq_ref, acc_scr):
    chunk, n_chunks = pl.program_id(1), pl.num_programs(1)
    rows = da_ref.shape[0]
    half = da_ref.shape[1] // 2
    keys = v_ref.shape[0]

    @pl.when(chunk == 0)
    def _():
        acc_scr[...] = jnp.zeros_like(acc_scr)

    factor = jnp.exp(m_ref[0, 0] - lse_ref[0])
    delta = delta_ref[0]
    da_cat = pair_rows(da_ref[...], half)
    acc = acc_scr[...]
    for t in range(keys // tile):
        rng = slice(t * tile, (t + 1) * tile)
        dp = dot_nt(v_ref[rng, :], da_cat)
        p = jnp.concatenate([p_ref[0, rng, :], p_ref[1, rng, :]], axis=1).astype(jnp.float32)
        ds = ((p * factor) * (dp - delta)).astype(jnp.bfloat16)
        ds_ref[0, rng, :] = ds[:, :rows]
        ds_ref[1, rng, :] = ds[:, rows:]
        acc = acc + dot_tn(k_ref[rng, :], ds)
    acc_scr[...] = acc

    @pl.when(chunk == n_chunks - 1)
    def _():
        dq_ref[...] = jnp.transpose(pair_blocks(acc, half, rows)).astype(jnp.bfloat16)


def query_back(probs, projected, grad_attn, delta, lse, lows, chunk_keys, tile=512):
    heads, total, rows = probs.shape
    pairs = heads // 2
    width = grad_attn.shape[1]
    wide = width // pairs
    n_chunks = total // chunk_keys
    return pl.pallas_call(
        functools.partial(query_back_kernel, tile),
        grid=(pairs, n_chunks),
        in_specs=[
            pl.BlockSpec((2, chunk_keys, rows), lambda p, c: (p, c, 0)),
            pl.BlockSpec((chunk_keys, wide), lambda p, c: (c, 2 * pairs + p)),
            pl.BlockSpec((chunk_keys, wide), lambda p, c: (c, pairs + p)),
            pl.BlockSpec((rows, wide), lambda p, c: (0, p)),
            pl.BlockSpec((1, 1, 2 * rows), lambda p, c: (p, 0, 0)),
            pl.BlockSpec((1, 1, 2 * rows), lambda p, c: (p, 0, 0)),
            pl.BlockSpec((1, 1, 1, 2 * rows), lambda p, c: (p, c, 0, 0)),
        ],
        out_specs=[
            pl.BlockSpec((2, chunk_keys, rows), lambda p, c: (p, c, 0)),
            pl.BlockSpec((rows, wide), lambda p, c: (0, p)),
        ],
        out_shape=[
            jax.ShapeDtypeStruct((heads, total, rows), jnp.bfloat16),
            jax.ShapeDtypeStruct((rows, width), jnp.bfloat16),
        ],
        scratch_shapes=[pltpu.VMEM((wide, 2 * rows), jnp.float32)],
        input_output_aliases={0: 0},
        compiler_params=pltpu.CompilerParams(vmem_limit_bytes=VMEM_BYTES),
        name="query_back",
    )(probs, projected, projected, grad_attn, delta, lse, lows)


def key_back_kernel(tile, q_ref, da_ref, aux_ref, idx_ref, k_ref, v_ref, tab_ref, dk_ref, dv_ref, dk_scr, dv_scr):
    pair, chunk, n_chunks = pl.program_id(0), pl.program_id(1), pl.num_programs(1)
    rows = k_ref.shape[0]
    wide = k_ref.shape[1]
    half = wide // 2
    queries = q_ref.shape[0]

    @pl.when(chunk == 0)
    def _():
        dk_scr[...] = jnp.zeros_like(dk_scr)
        dv_scr[...] = jnp.zeros_like(dv_scr)

    lane = lax.broadcasted_iota(jnp.int32, (2 * rows, 128), 1)
    head = 2 * pair + (lax.broadcasted_iota(jnp.int32, (2 * rows, 128), 0) >= rows).astype(jnp.int32)
    first = (lane >= 2 * head) & (lane < 2 * head + 2)
    second = (lane >= 64 + 2 * head) & (lane < 64 + 2 * head + 2)
    take_lse = jnp.where(first, -1.0, 0.0).astype(jnp.bfloat16)
    take_delta = jnp.where(second, -1.0, 0.0).astype(jnp.bfloat16)
    k_cat = jnp.concatenate([pair_rows(k_ref[...], half), take_lse], axis=1)
    v_cat = jnp.concatenate([pair_rows(v_ref[...], half), take_delta], axis=1)
    dk, dv = dk_scr[...], dv_scr[...]
    for t in range(queries // tile):
        rng = slice(t * tile, (t + 1) * tile)
        q, da, aux = q_ref[rng, :], da_ref[rng, :], aux_ref[rng, :]
        index = idx_ref[rng, :]
        s = dot_nt(jnp.concatenate([q, aux], axis=1), k_cat)
        bias = jnp.concatenate(
            [bias_of(tab_ref[0, j : j + 1, :], index) for j in range(2)], axis=1
        )
        p = jnp.exp(s + bias)
        ds = p * dot_nt(jnp.concatenate([da, aux], axis=1), v_cat)
        dv = dv + dot_tn(da, p.astype(jnp.bfloat16))
        dk = dk + dot_tn(q, ds.astype(jnp.bfloat16))
    dk_scr[...] = dk
    dv_scr[...] = dv

    @pl.when(chunk == n_chunks - 1)
    def _():
        dk_ref[...] = jnp.transpose(pair_blocks(dk, half, rows)).astype(jnp.bfloat16)
        dv_ref[...] = jnp.transpose(pair_blocks(dv, half, rows)).astype(jnp.bfloat16)


def key_back(projected, grads_aux, index, table, rows, chunk_keys, tile=512):
    total, width = projected.shape[0], projected.shape[1] // 3
    pairs = table.shape[0]
    wide = width // pairs
    n_chunks = total // chunk_keys
    return pl.pallas_call(
        functools.partial(key_back_kernel, tile),
        grid=(pairs, n_chunks),
        in_specs=[
            pl.BlockSpec((chunk_keys, wide), lambda p, c: (c, p)),
            pl.BlockSpec((chunk_keys, wide), lambda p, c: (c, p)),
            pl.BlockSpec((chunk_keys, 128), lambda p, c: (c, pairs)),
            pl.BlockSpec((chunk_keys, rows), lambda p, c: (c, 0)),
            pl.BlockSpec((rows, wide), lambda p, c: (0, pairs + p)),
            pl.BlockSpec((rows, wide), lambda p, c: (0, 2 * pairs + p)),
            pl.BlockSpec((1, 2, 128), lambda p, c: (p, 0, 0)),
        ],
        out_specs=[
            pl.BlockSpec((rows, wide), lambda p, c: (0, p)),
            pl.BlockSpec((rows, wide), lambda p, c: (0, p)),
        ],
        out_shape=[
            jax.ShapeDtypeStruct((rows, width), jnp.bfloat16),
            jax.ShapeDtypeStruct((rows, width), jnp.bfloat16),
        ],
        scratch_shapes=[
            pltpu.VMEM((wide, 2 * rows), jnp.float32),
            pltpu.VMEM((wide, 2 * rows), jnp.float32),
        ],
        compiler_params=pltpu.CompilerParams(vmem_limit_bytes=VMEM_BYTES),
        name="key_back",
    )(projected, grads_aux, grads_aux, index, projected, projected, table)


def bucket_of(offset):
    distance = jnp.abs(offset)
    counted = jnp.zeros(offset.shape, jnp.int32)
    for threshold in THRESHOLDS:
        counted = counted + (distance >= threshold).astype(jnp.int32)
    return counted + BUCKETS // 2 * (offset > 0).astype(jnp.int32)


def places(packed, seq_lengths):
    seq_ends = jnp.cumsum(seq_lengths)
    passed = (packed[:, None] >= seq_ends[None, :]).astype(jnp.int32)
    segment = jnp.sum(passed, axis=1)
    starts = jnp.sum(passed * seq_lengths[None, :], axis=1)
    return (packed - starts, segment)


def norm_back(values, inverse, scale_gain, grad_normed):
    grad_gain = jnp.sum(grad_normed * values * inverse, axis=0)
    scaled = grad_normed * scale_gain
    grad_values = inverse * (
        scaled - values * inverse * inverse * jnp.mean(scaled * values, axis=1, keepdims=True)
    )
    return (grad_gain, grad_values)


def smooth_gate(values):
    return jax.nn.gelu(values, approximate=True)


def dot_f32(left, right):
    return jnp.dot(left, right, preferred_element_type=jnp.float32)


def swap_ctx(values, distance):
    size = lax.axis_size("ctx")
    return lax.ppermute(values, "ctx", [(i, i ^ distance) for i in range(size)])


def swap_pair(values):
    return lax.ppermute(values, "fsdp", [(0, 1), (1, 0)])


def in_order(where, mine, other, axis=0):
    return jnp.where(
        where == 0,
        jnp.concatenate([mine, other], axis=axis),
        jnp.concatenate([other, mine], axis=axis),
    )


def part_of(values, index, parts, axis):
    size = values.shape[axis] // parts
    return lax.dynamic_slice_in_dim(values, index * size, size, axis)


def gather_group(block):
    size = lax.axis_size("ctx")
    quarter = size // 4
    pieces = [block] + [swap_ctx(block, quarter * j) for j in (1, 2, 3)]
    pieces = [piece[None] for piece in pieces]
    distance = quarter // 2
    while distance > 1:
        if len(pieces) > 4:
            pieces = [jnp.concatenate(pieces, axis=0)]
        pieces = pieces + [swap_ctx(piece, distance) for piece in pieces]
        distance //= 2
    most = jnp.concatenate(pieces, axis=0)
    return jnp.concatenate([most, swap_ctx(most, 1)], axis=0)


def bits_of(size):
    return size.bit_length() - 1


def scatter_sum(blocks, order):
    here = lax.axis_index("ctx")
    for bit in order:
        mine = (here >> bit) & 1
        keep = part_of(blocks, mine, 2, 0)
        got = swap_ctx(part_of(blocks, 1 - mine, 2, 0), 1 << bit)
        blocks = (keep.astype(jnp.float32) + got.astype(jnp.float32)).astype(jnp.bfloat16)
    return blocks


def gather_back(blocks, order):
    here = lax.axis_index("ctx")
    for bit in reversed(order):
        mine = (here >> bit) & 1
        blocks = in_order(mine, blocks, swap_ctx(blocks, 1 << bit))
    return blocks


def pair_weights(rows):
    core = lax.axis_index("ctx") & 1
    got = swap_pair(part_of(rows, core, 2, 0))
    return in_order(core, got, swap_ctx(got, 1))


def shards(
    tokens,
    cotangent,
    lengths,
    dealing,
    gain_one,
    w_query,
    w_key,
    w_value,
    w_out,
    gain_two,
    w_in,
    w_ff,
    rel_table,
):
    bf16, f32 = jnp.bfloat16, jnp.float32
    size = lax.axis_size("ctx")
    pair = lax.axis_index("fsdp")
    rows, width = tokens.shape[1], tokens.shape[2]
    heads = rel_table.shape[1]
    head_size = width // heads
    pairs = heads // 2
    total = size * rows
    half_ff = w_ff.shape[0]
    half_width = w_query.shape[0]
    chunk_keys = min(total, 2048)

    dealt = dealing[0]
    place_row = jnp.concatenate([dealt // 128, dealt % 128]).astype(bf16)
    place_rows = jnp.pad(place_row[None], ((0, 7), (0, width - 2 * rows)))
    gathered = gather_group(jnp.concatenate([tokens[0], place_rows], axis=0))

    small = jnp.concatenate([gain_one, gain_two, rel_table.reshape(-1)])
    small = jnp.pad(small, (0, 1024 - small.shape[0])).reshape(8, 128)
    small_other = swap_pair(small)
    small_full = jnp.stack([small.reshape(-1), small_other.reshape(-1)])
    small_full = jnp.where(pair == 0, small_full, small_full[::-1])
    gain32_one = small_full[:, :half_width].reshape(width).astype(f32)
    gain32_two = small_full[:, half_width : 2 * half_width].reshape(width).astype(f32)
    full_table = small_full[:, 2 * half_width : 2 * half_width + rel_table.size]
    full_table = full_table.reshape(2 * rel_table.shape[0], heads).astype(f32)
    first_rows = jnp.concatenate([w_query, w_key, w_value], axis=1)
    w_qkv = in_order(pair, first_rows, pair_weights(first_rows))
    mine_in = part_of(w_in, pair, 2, 1)
    second_rows = jnp.concatenate([w_out, part_of(w_in, 1 - pair, 2, 1)], axis=1)
    second_other = pair_weights(second_rows)
    full_out = in_order(pair, w_out, second_other[:, :width])
    half_in = in_order(pair, mine_in, second_other[:, width:])
    grad_out = cotangent[0]
    grad_out_pair = jnp.concatenate([grad_out, swap_pair(grad_out)], axis=0)

    packed = gathered[:, rows, : 2 * rows].astype(jnp.int32)
    packed = (packed[:, :rows] * 128 + packed[:, rows:]).reshape(total)
    pos, seg = places(packed, lengths[0])
    index = jnp.where(
        seg[:, None] == seg[None, :rows],
        bucket_of(pos[:, None] - pos[None, :rows]),
        BUCKETS,
    )
    table_t = jnp.transpose(full_table)
    back_t = jnp.concatenate(
        [table_t[:, :1], table_t[:, 17:], table_t[:, :1], table_t[:, 1:16]], axis=1
    )
    tables = [
        jnp.pad(tab, ((0, 0), (0, 128 - BUCKETS)), constant_values=NEG).reshape(pairs, 2, 128)
        for tab in (table_t, back_t)
    ]
    all_tokens = gathered[:, :rows].reshape(total, width).astype(f32)
    inv_all = lax.rsqrt(jnp.mean(all_tokens * all_tokens, axis=1, keepdims=True) + EPS)
    normed_all = (all_tokens * inv_all * gain32_one).astype(bf16)
    projected = dot_f32(normed_all, w_qkv).astype(bf16)
    attn_f32, lse, lows, probs = attend(projected, index, tables[0], rows, chunk_keys)
    attn_b = attn_f32.astype(bf16)

    inputs = tokens[0].astype(f32)
    inv_one = lax.rsqrt(jnp.mean(inputs * inputs, axis=1, keepdims=True) + EPS)
    normed_one = (inputs * inv_one * gain32_one).astype(bf16)
    resid = inputs + dot_f32(attn_b, full_out)
    inv_two = lax.rsqrt(jnp.mean(resid * resid, axis=1, keepdims=True) + EPS)
    normed_two = (resid * inv_two * gain32_two).astype(bf16)
    normed_pair = jnp.concatenate([normed_two, swap_pair(normed_two)], axis=0)
    gate_pre = dot_f32(normed_pair, half_in)
    gate_val, gate_pull = jax.vjp(smooth_gate, gate_pre)
    active = gate_val.astype(bf16)
    grad_active = jnp.einsum("td,fd->tf", grad_out_pair, w_ff, preferred_element_type=f32)
    grad_pre = gate_pull(grad_active)[0].astype(bf16)
    grad_normed_part = jnp.einsum("tf,df->td", grad_pre, half_in, preferred_element_type=f32)
    grad_normed_two = grad_normed_part[:rows] + swap_pair(
        grad_normed_part[rows:].astype(bf16)
    ).astype(f32)
    grad_gain_two, grad_resid_norm = norm_back(resid, inv_two, gain32_two, grad_normed_two)
    grad_resid = grad_out.astype(f32) + grad_resid_norm
    grad_branch = grad_resid.astype(bf16)
    grad_attn = jnp.einsum("td,ed->te", grad_branch, full_out, preferred_element_type=f32)
    grad_attn = grad_attn.astype(bf16)
    delta = jnp.sum((grad_attn.astype(f32) * attn_f32).reshape(rows, heads, head_size), axis=2)
    out_part = dot_f32(active, w_ff)
    output = resid + out_part[:rows] + swap_pair(out_part[rows:].astype(bf16)).astype(f32)

    def two_parts(values):
        high = lax.reduce_precision(values, 8, 7)
        both = jnp.stack([high, values - high], axis=2).reshape(rows, 2 * heads)
        return jnp.pad(both.astype(bf16), ((0, 0), (0, 64 - 2 * heads)))

    lse_t = jnp.transpose(lse.reshape(heads, rows))
    grads_aux = gather_group(
        jnp.concatenate([grad_attn, two_parts(lse_t), two_parts(delta)], axis=1)
    ).reshape(total, width + 128)
    delta_rows = jnp.transpose(delta).reshape(pairs, 1, 2 * rows)
    grad_scores, grad_q = query_back(probs, projected, grad_attn, delta_rows, lse, lows, chunk_keys)
    one_hot = (index[:, :, None] == jnp.arange(BUCKETS, dtype=jnp.int32)).astype(bf16)
    grad_tab = jnp.einsum("hkq,kqb->hb", grad_scores, one_hot, preferred_element_type=f32)
    grad_k, grad_v = key_back(projected, grads_aux, index, tables[1], rows, chunk_keys)

    def halves(values):
        other = swap_pair(part_of(values, 1 - pair, 2, 1))
        return jnp.concatenate([part_of(values, pair, 2, 1), other], axis=0)

    def both(values):
        return jnp.concatenate([values, swap_pair(values)], axis=0)

    def by_rows(left, right):
        return jnp.einsum("td,te->de", left, right, preferred_element_type=f32).astype(bf16)

    def blocks_of(values):
        return [
            values[:, j : j + width].reshape(size, values.shape[0] // size, width)
            for j in range(0, values.shape[1], width)
        ]

    order = list(range(bits_of(size)))
    grad_ff_part = by_rows(active, grad_out_pair)
    grad_in_part = by_rows(normed_pair, grad_pre)
    grad_out_part = by_rows(halves(attn_b), both(grad_branch))
    ff_sum = scatter_sum(grad_ff_part.reshape(size, half_ff // size, width), order)
    in_blocks = blocks_of(part_of(grad_in_part, pair, 2, 0)) + blocks_of(
        part_of(grad_in_part, 1 - pair, 2, 0)
    )
    in_sum = scatter_sum(
        jnp.concatenate(in_blocks + blocks_of(grad_out_part), axis=1),
        order,
    )
    ff_full = gather_back(ff_sum, order)
    tall = half_width // size
    moved = swap_pair(in_sum[:, 2 * tall : 4 * tall])
    in_sum = jnp.concatenate([in_sum[:, : 2 * tall], moved, in_sum[:, 4 * tall :]], axis=1)
    in_full = gather_back(in_sum, order)

    grads_qkv = jnp.concatenate([grad_q, grad_k, grad_v], axis=1)
    grad_qkv_part = by_rows(halves(normed_one), both(grads_qkv))
    qkv_full = gather_back(
        scatter_sum(jnp.concatenate(blocks_of(grad_qkv_part), axis=1), order), order
    )
    grad_normed_one = jnp.einsum("te,de->td", grads_qkv, w_qkv, preferred_element_type=f32)
    grad_gain_one, grad_input_norm = norm_back(inputs, inv_one, gain32_one, grad_normed_one)
    grad_tokens = grad_resid + grad_input_norm

    small_grads = jnp.concatenate(
        [
            grad_gain_one.reshape(2, half_width),
            grad_gain_two.reshape(2, half_width),
            jnp.transpose(grad_tab).reshape(2, rel_table.size),
        ],
        axis=1,
    )
    small_grads = lax.psum(small_grads, ("ctx", "fsdp"))
    small_mine = part_of(small_grads, pair, 2, 0)[0]

    def whole(full, block, count=1):
        return full[:, block * tall : (block + count) * tall].astype(f32)

    def joined(full, first):
        return whole(full, first).reshape(half_width, width)

    in_low, in_high = (
        jnp.concatenate([joined(in_full, j), joined(in_full, j + 1)], axis=1) for j in (0, 2)
    )
    return (
        output.astype(bf16)[None],
        grad_tokens[None],
        small_mine[:half_width],
        joined(qkv_full, 0),
        joined(qkv_full, 1),
        joined(qkv_full, 2),
        joined(in_full, 4),
        small_mine[half_width : 2 * half_width],
        in_order(pair, in_low, in_high, axis=1),
        ff_full.astype(f32).reshape(half_ff, width),
        small_mine[2 * half_width :].reshape(rel_table.shape),
    )


def solution(mesh):
    spread = P("fsdp", "ctx", None)
    rows_of = P("fsdp", None)
    return jax.shard_map(
        shards,
        mesh=mesh,
        in_specs=(
            spread,
            spread,
            rows_of,
            P("fsdp", "ctx"),
            P("fsdp"),
            rows_of,
            rows_of,
            rows_of,
            rows_of,
            P("fsdp"),
            rows_of,
            rows_of,
            rows_of,
        ),
        out_specs=(
            spread,
            spread,
            P("fsdp"),
            rows_of,
            rows_of,
            rows_of,
            rows_of,
            P("fsdp"),
            rows_of,
            rows_of,
            rows_of,
        ),
        check_vma=False,
    )
```

```python
import functools
import jax
import jax.numpy as jnp
from jax import lax
from jax.experimental import pallas as pl
from jax.experimental.pallas import tpu as pltpu
from jax.sharding import PartitionSpec as P

BUCKETS = 32
PIECES = 16
EPS = 1e-06
NEG = -1000000000.0
THRESHOLDS = (1, 2, 3, 4, 5, 6, 7, 8, 12, 16, 23, 32, 46, 64, 91)
VMEM_BYTES = 50 * 1024 * 1024


def cost_of(micros):
    return pl.CostEstimate(flops=int(micros * 8e8), bytes_accessed=int(micros * 2.5e6), transcendentals=0)


def dot_nt(left, right):
    return lax.dot_general(left, right, (((1,), (1,)), ((), ())), preferred_element_type=jnp.float32)


def dot_tn(left, right):
    return lax.dot_general(left, right, (((0,), (0,)), ((), ())), preferred_element_type=jnp.float32)


def pair_rows(block, half):
    lane = lax.broadcasted_iota(jnp.int32, block.shape, 1)
    zero = jnp.zeros_like(block)
    return jnp.concatenate(
        [jnp.where(lane < half, block, zero), jnp.where(lane < half, zero, block)], axis=0
    )


def pair_blocks(acc, half, rows):
    return jnp.concatenate([acc[:half, :rows], acc[half:, rows:]], axis=0)


def bias_of(row, index):
    return jnp.take_along_axis(jnp.broadcast_to(row, index.shape), index, axis=1)


def fill_rows(out_ref, j, own, got, more, spot_ref):
    rows, part = own.shape[0], got.shape[0]
    other = (1 - spot_ref[0]) * rows
    out_ref[j, pl.ds(pl.multiple_of(spot_ref[0] * rows, 64), rows), :] = own
    out_ref[j, pl.ds(pl.multiple_of(other + spot_ref[1] * part, 64), part), :] = got
    out_ref[j, pl.ds(pl.multiple_of(other + (1 - spot_ref[1]) * part, 64), part), :] = more


def project_kernel(count, total, seqs, spot_ref, *refs):
    pieces, refs = refs[:PIECES], refs[PIECES:]
    gain_ref, wq_ref, wk_ref, wv_ref, got_ref, more_ref = refs[:6]
    made_ref, idx_ref, normed_ref, full_ref, rows_scr, place_scr, own_scr = refs[6:]
    width = gain_ref.shape[1]
    rows = normed_ref.shape[0]
    outer, inner = pl.program_id(0), pl.program_id(1)

    for group in range(PIECES // count):

        @pl.when(inner == group)
        def _():
            for j in range(count):
                held = pieces[group * count + j][0]
                rows_scr[j * rows : (j + 1) * rows, :] = held[:rows]
                place_scr[j : j + 1, :] = held[rows:].astype(jnp.float32)[:1, : 2 * rows]

    spots = place_scr[...]
    spots = spots[:, :rows] * 128.0 + spots[:, rows:]
    end = 0
    begin, segment = jnp.zeros_like(spots), jnp.zeros_like(spots)
    for j in range(seqs):
        end = end + spot_ref[2 + j]
        passed = spots >= end.astype(jnp.float32)
        begin = jnp.where(passed, end.astype(jnp.float32), begin)
        segment = jnp.where(passed, segment + 1.0, segment)
    marks = spots - begin + segment * (2.0 * total)

    @pl.when((outer == 0) & (inner == 0))
    def _():
        own_scr[...] = marks[:1, :]
        for j, ref in enumerate((wq_ref, wk_ref, wv_ref)):
            fill_rows(full_ref, j, ref[...], got_ref[j], more_ref[j], spot_ref)

    values = rows_scr[...].astype(jnp.float32)
    inverse = lax.rsqrt(jnp.mean(values * values, axis=1, keepdims=True) + EPS)
    normed = (values * inverse * gain_ref[...]).astype(jnp.bfloat16)
    shape = (count, rows, width)
    for j in range(3):
        made = jnp.dot(normed, full_ref[j], preferred_element_type=jnp.float32)
        made_ref[:, :, j * width : (j + 1) * width] = made.astype(jnp.bfloat16).reshape(shape)

    @pl.when((outer == 0) & (inner == 0))
    def _():
        normed_ref[...] = normed[:rows]

    turned = jnp.transpose(marks)
    for j in range(count):
        offset = turned[:, j : j + 1] - own_scr[...]
        distance = jnp.abs(offset)
        bucket = jnp.where(offset > 0, BUCKETS // 2, 0)
        for threshold in THRESHOLDS:
            bucket = bucket + (distance >= threshold).astype(jnp.int32)
        idx_ref[j] = jnp.where(distance >= total, BUCKETS, bucket)


def project(spot, pieces, gain, weights, got, more, rows, total, seqs, count=4):
    devices, tall, width = pieces[0].shape
    held, part = weights[0].shape[0], got.shape[1]
    fixed = lambda i, j, spot: (0, 0)
    fixed3 = lambda i, j, spot: (0, 0, 0)
    moving = lambda i, j, spot: (j, i, 0)
    return pl.pallas_call(
        functools.partial(project_kernel, count, total, seqs),
        grid_spec=pltpu.PrefetchScalarGridSpec(
            num_scalar_prefetch=1,
            grid=(devices, PIECES // count),
            in_specs=[pl.BlockSpec((1, tall, width), lambda i, j, spot: (i, 0, 0))] * PIECES
            + [
                pl.BlockSpec((1, width), fixed),
                pl.BlockSpec((held, width), fixed),
                pl.BlockSpec((held, width), fixed),
                pl.BlockSpec((held, width), fixed),
                pl.BlockSpec((3, part, width), fixed3),
                pl.BlockSpec((3, part, width), fixed3),
            ],
            out_specs=[
                pl.BlockSpec((count, rows, 3 * width), moving),
                pl.BlockSpec((count, rows, rows), moving),
                pl.BlockSpec((rows, width), fixed),
                pl.BlockSpec((3, width, width), fixed3),
            ],
            scratch_shapes=[
                pltpu.VMEM((count * rows, width), jnp.bfloat16),
                pltpu.VMEM((8, 2 * rows), jnp.float32),
                pltpu.VMEM((1, rows), jnp.float32),
            ],
        ),
        out_shape=[
            jax.ShapeDtypeStruct((PIECES, devices * rows, 3 * width), jnp.bfloat16),
            jax.ShapeDtypeStruct((PIECES, devices * rows, rows), jnp.int32),
            jax.ShapeDtypeStruct((rows, width), jnp.bfloat16),
            jax.ShapeDtypeStruct((3, width, width), jnp.bfloat16),
        ],
        compiler_params=pltpu.CompilerParams(vmem_limit_bytes=VMEM_BYTES),
        cost_estimate=cost_of(0.7 * PIECES * devices),
        name="project",
    )(spot, *pieces, gain, *weights, got, more)


def close_kernel(spot_ref, attn_ref, x_ref, gain_ref, w_ref, got_ref, more_ref, resid_ref, normed_ref, attn_b_ref, full_ref):
    fill_rows(full_ref, 0, w_ref[...], got_ref[0], more_ref[0], spot_ref)
    attn = attn_ref[...].astype(jnp.bfloat16)
    attn_b_ref[...] = attn
    resid = x_ref[...].astype(jnp.float32) + jnp.dot(
        attn, full_ref[0], preferred_element_type=jnp.float32
    )
    resid_ref[...] = resid
    inverse = lax.rsqrt(jnp.mean(resid * resid, axis=1, keepdims=True) + EPS)
    normed_ref[...] = (resid * inverse * gain_ref[...]).astype(jnp.bfloat16)


def close(spot, attn, tokens, gain, weight, got, more):
    rows, width = attn.shape
    held, part = weight.shape[0], got.shape[1]
    whole = lambda i, spot: (0, 0)
    first = lambda i, spot: (0, 0, 0)
    return pl.pallas_call(
        close_kernel,
        grid_spec=pltpu.PrefetchScalarGridSpec(
            num_scalar_prefetch=1,
            grid=(1,),
            in_specs=[
                pl.BlockSpec((rows, width), whole),
                pl.BlockSpec((rows, width), whole),
                pl.BlockSpec((1, width), whole),
                pl.BlockSpec((held, width), whole),
                pl.BlockSpec((1, part, width), first),
                pl.BlockSpec((1, part, width), first),
            ],
            out_specs=[
                pl.BlockSpec((rows, width), whole),
                pl.BlockSpec((rows, width), whole),
                pl.BlockSpec((rows, width), whole),
                pl.BlockSpec((1, width, width), first),
            ],
        ),
        out_shape=[
            jax.ShapeDtypeStruct((rows, width), jnp.float32),
            jax.ShapeDtypeStruct((rows, width), jnp.bfloat16),
            jax.ShapeDtypeStruct((rows, width), jnp.bfloat16),
            jax.ShapeDtypeStruct((1, width, width), jnp.bfloat16),
        ],
        compiler_params=pltpu.CompilerParams(vmem_limit_bytes=VMEM_BYTES),
        cost_estimate=cost_of(2),
        name="close",
    )(spot, attn, tokens, gain, weight, got, more)


def branch_kernel(part_ref, got_ref, resid_ref, cot_ref, gain_ref, out_ref, attn_ref, lse_ref, payload_ref, delta_ref, grad_ref, branch_ref, gain_grad_ref):
    f32, bf16 = jnp.float32, jnp.bfloat16
    rows, width = resid_ref.shape
    heads = lse_ref.shape[0]
    size = width // heads
    resid = resid_ref[...]
    normed_grad = part_ref[...] + got_ref[...].astype(f32)
    inverse = lax.rsqrt(jnp.mean(resid * resid, axis=1, keepdims=True) + EPS)
    gain_grad_ref[...] = jnp.sum(normed_grad * resid * inverse, axis=0, keepdims=True)
    scaled = normed_grad * gain_ref[...]
    mean = jnp.mean(scaled * resid, axis=1, keepdims=True)
    grad = cot_ref[...].astype(f32) + inverse * (scaled - resid * (inverse * inverse * mean))
    grad_ref[...] = grad
    branch = grad.astype(bf16)
    branch_ref[...] = branch
    attn_grad = dot_nt(branch, out_ref[0]).astype(bf16)
    payload_ref[:, :width] = attn_grad
    product = attn_grad.astype(f32) * attn_ref[...]
    high = product.astype(bf16)
    low = (product - high.astype(f32)).astype(bf16)

    def member(shape, at_row, at_col):
        row = lax.broadcasted_iota(jnp.int32, shape, 0)
        col = lax.broadcasted_iota(jnp.int32, shape, 1)
        return jnp.where(at_row(row) == at_col(col), 1.0, 0.0).astype(bf16)

    padded = 16
    by_head = member((padded, width), lambda r: r, lambda c: c // size)
    delta = (dot_nt(by_head, high) + dot_nt(by_head, low))[:heads]
    delta_ref[...] = delta
    col = lax.broadcasted_iota(jnp.int32, (rows, 128), 1)
    aux = jnp.zeros((rows, 128), f32)
    for first, values in ((0, lse_ref[...]), (64, delta)):
        values = jnp.concatenate([values, jnp.zeros((padded - heads, rows), f32)], axis=0)
        high = values.astype(bf16)
        low = (values - high.astype(f32)).astype(bf16)
        for odd, half in ((0, high), (1, low)):
            to_col = member((padded, 128), lambda r: first + odd + 2 * r, lambda c: c)
            aux = aux + dot_tn(half, to_col)
    payload_ref[:, width:] = aux.astype(bf16)


def branch(part, got, resid, cotangent, gain, full_out, attn, lse):
    rows, width = resid.shape
    heads = lse.shape[0]
    return pl.pallas_call(
        branch_kernel,
        grid=(1,),
        in_specs=[
            pl.BlockSpec((rows, width), lambda i: (0, 0)),
            pl.BlockSpec((rows, width), lambda i: (0, 0)),
            pl.BlockSpec((rows, width), lambda i: (0, 0)),
            pl.BlockSpec((rows, width), lambda i: (0, 0)),
            pl.BlockSpec((1, width), lambda i: (0, 0)),
            pl.BlockSpec((1, width, width), lambda i: (0, 0, 0)),
            pl.BlockSpec((rows, width), lambda i: (0, 0)),
            pl.BlockSpec((heads, rows), lambda i: (0, 0)),
        ],
        out_specs=[
            pl.BlockSpec((rows, width + 128), lambda i: (0, 0)),
            pl.BlockSpec((heads, rows), lambda i: (0, 0)),
            pl.BlockSpec((rows, width), lambda i: (0, 0)),
            pl.BlockSpec((rows, width), lambda i: (0, 0)),
            pl.BlockSpec((1, width), lambda i: (0, 0)),
        ],
        out_shape=[
            jax.ShapeDtypeStruct((rows, width + 128), jnp.bfloat16),
            jax.ShapeDtypeStruct((heads, rows), jnp.float32),
            jax.ShapeDtypeStruct((rows, width), jnp.float32),
            jax.ShapeDtypeStruct((rows, width), jnp.bfloat16),
            jax.ShapeDtypeStruct((1, width), jnp.float32),
        ],
        compiler_params=pltpu.CompilerParams(vmem_limit_bytes=VMEM_BYTES),
        cost_estimate=cost_of(3),
        name="branch",
    )(part, got, resid, cotangent, gain, full_out, attn, lse)


def unpack_kernel(tall, spot_ref, near_ref, far_ref, *out_refs):
    values = jnp.where(pl.program_id(0) == 0, near_ref[...], far_ref[...]).astype(jnp.float32)
    for j, ref in enumerate(out_refs):
        ref[...] = values[:, j * tall : (j + 1) * tall, :]


def unpack(spot, near, far, tall, outputs):
    half, high, width = near.shape
    step = min(4, half)
    steps = half // step

    def place(j, i, spot):
        return (jnp.bitwise_xor(j, spot[1]) * steps + i, 0, 0)

    return pl.pallas_call(
        functools.partial(unpack_kernel, tall),
        grid_spec=pltpu.PrefetchScalarGridSpec(
            num_scalar_prefetch=1,
            grid=(2, steps),
            in_specs=[
                pl.BlockSpec(
                    (step, high, width), lambda j, i, spot: (jnp.where(j == 0, i, steps - 1), 0, 0)
                ),
                pl.BlockSpec(
                    (step, high, width), lambda j, i, spot: (jnp.where(j == 0, 0, i), 0, 0)
                ),
            ],
            out_specs=[pl.BlockSpec((step, tall, width), place)] * outputs,
        ),
        out_shape=[jax.ShapeDtypeStruct((2 * half, tall, width), jnp.float32)] * outputs,
        compiler_params=pltpu.CompilerParams(vmem_limit_bytes=VMEM_BYTES),
        cost_estimate=cost_of(4),
        name="unpack",
    )(spot, near, far)


def spread_kernel(tall_ff, tall, spot_ref, full_ref, ff_ref, in_ref, out_ref):
    width = out_ref.shape[2]
    values = full_ref[...].astype(jnp.float32)
    ff_ref[...] = values[:, :tall_ff, :]
    parts = [values[:, tall_ff + j * tall : tall_ff + (j + 1) * tall, :] for j in range(5)]
    for j in range(2):
        in_ref[:, :, j * width : (j + 1) * width] = jnp.where(
            spot_ref[0] == 0, parts[j], parts[2 + j]
        )
        in_ref[:, :, (2 + j) * width : (3 + j) * width] = jnp.where(
            spot_ref[0] == 0, parts[2 + j], parts[j]
        )
    out_ref[...] = parts[4]


def spread(spot, full, tall_ff, tall):
    size, high, width = full.shape
    step = 2
    return pl.pallas_call(
        functools.partial(spread_kernel, tall_ff, tall),
        grid_spec=pltpu.PrefetchScalarGridSpec(
            num_scalar_prefetch=1,
            grid=(size // step,),
            in_specs=[pl.BlockSpec((step, high, width), lambda i, spot: (i, 0, 0))],
            out_specs=[
                pl.BlockSpec((step, tall_ff, width), lambda i, spot: (i, 0, 0)),
                pl.BlockSpec((step, tall, 4 * width), lambda i, spot: (i, 0, 0)),
                pl.BlockSpec((step, tall, width), lambda i, spot: (i, 0, 0)),
            ],
        ),
        out_shape=[
            jax.ShapeDtypeStruct((size, tall_ff, width), jnp.float32),
            jax.ShapeDtypeStruct((size, tall, 4 * width), jnp.float32),
            jax.ShapeDtypeStruct((size, tall, width), jnp.float32),
        ],
        compiler_params=pltpu.CompilerParams(vmem_limit_bytes=VMEM_BYTES),
        cost_estimate=cost_of(6),
        name="spread",
    )(spot, full)


def attend_kernel(tile, q_ref, k_ref, v_ref, idx_ref, tab_ref, o_ref, lse_ref, m_out, p_ref, s_scr, m_scr, l_scr, acc_scr):
    chunk, n_chunks = pl.program_id(1), pl.num_programs(1)
    rows = q_ref.shape[0]
    half = q_ref.shape[1] // 2
    keys = k_ref.shape[0]

    @pl.when(chunk == 0)
    def _():
        m_scr[...] = jnp.full_like(m_scr, -3.0e38)
        l_scr[...] = jnp.zeros_like(l_scr)
        acc_scr[...] = jnp.zeros_like(acc_scr)

    q_cat = pair_rows(q_ref[...], half)
    m_old = m_scr[...]
    m_tiles = jnp.full((8, 2 * rows), -3.0e38, jnp.float32)
    for t in range(keys // tile):
        rng = slice(t * tile, (t + 1) * tile)
        s = dot_nt(k_ref[rng, :], q_cat)
        index = idx_ref[rng, :]
        s = s + jnp.concatenate(
            [bias_of(tab_ref[0, j : j + 1, :], index) for j in range(2)], axis=1
        )
        s_scr[rng, :] = s
        m_tiles = jnp.maximum(m_tiles, jnp.max(s.reshape(tile // 8, 8, 2 * rows), axis=0))
    m_new = jnp.maximum(m_old, jnp.max(m_tiles, axis=0, keepdims=True))
    fade = jnp.exp(m_old - m_new)
    sums = jnp.zeros((8, 2 * rows), jnp.float32)
    acc = acc_scr[...] * fade
    for t in range(keys // tile):
        rng = slice(t * tile, (t + 1) * tile)
        p = jnp.exp(s_scr[rng, :] - m_new)
        sums = sums + jnp.sum(p.reshape(tile // 8, 8, 2 * rows), axis=0)
        p_low = p.astype(jnp.bfloat16)
        p_ref[0, rng, :] = p_low[:, :rows]
        p_ref[1, rng, :] = p_low[:, rows:]
        acc = acc + dot_tn(v_ref[rng, :], p_low)
    acc_scr[...] = acc
    l_new = l_scr[...] * fade + jnp.sum(sums, axis=0, keepdims=True)
    l_scr[...] = l_new
    m_scr[...] = m_new
    m_out[0, 0] = m_new

    @pl.when(chunk == n_chunks - 1)
    def _():
        lse_ref[0] = m_new + jnp.log(l_new)
        o_ref[...] = jnp.transpose(pair_blocks(acc / l_new, half, rows))


def attend(made, index, table, chunk_keys, tile=512):
    total, rows = index.shape
    width = made.shape[1] // 3
    heads = table.shape[0] * 2
    pairs = table.shape[0]
    wide = width // pairs
    n_chunks = total // chunk_keys
    return pl.pallas_call(
        functools.partial(attend_kernel, tile),
        grid=(pairs, n_chunks),
        in_specs=[
            pl.BlockSpec((rows, wide), lambda p, c: (0, p)),
            pl.BlockSpec((chunk_keys, wide), lambda p, c: (c, pairs + p)),
            pl.BlockSpec((chunk_keys, wide), lambda p, c: (c, 2 * pairs + p)),
            pl.BlockSpec((chunk_keys, rows), lambda p, c: (c, 0)),
            pl.BlockSpec((1, 2, 128), lambda p, c: (p, 0, 0)),
        ],
        out_specs=[
            pl.BlockSpec((rows, wide), lambda p, c: (0, p)),
            pl.BlockSpec((1, 1, 2 * rows), lambda p, c: (p, 0, 0)),
            pl.BlockSpec((1, 1, 1, 2 * rows), lambda p, c: (p, c, 0, 0)),
            pl.BlockSpec((2, chunk_keys, rows), lambda p, c: (p, c, 0)),
        ],
        out_shape=[
            jax.ShapeDtypeStruct((rows, width), jnp.float32),
            jax.ShapeDtypeStruct((pairs, 1, 2 * rows), jnp.float32),
            jax.ShapeDtypeStruct((pairs, n_chunks, 1, 2 * rows), jnp.float32),
            jax.ShapeDtypeStruct((heads, total, rows), jnp.bfloat16),
        ],
        scratch_shapes=[
            pltpu.VMEM((chunk_keys, 2 * rows), jnp.float32),
            pltpu.VMEM((1, 2 * rows), jnp.float32),
            pltpu.VMEM((1, 2 * rows), jnp.float32),
            pltpu.VMEM((wide, 2 * rows), jnp.float32),
        ],
        compiler_params=pltpu.CompilerParams(vmem_limit_bytes=VMEM_BYTES),
        cost_estimate=cost_of(0.008 * total),
        name="attend",
    )(made, made, made, index, table)


def query_back_kernel(tile, p_ref, v_ref, k_ref, da_ref, delta_ref, lse_ref, m_ref, ds_ref, dq_ref, acc_scr):
    chunk, n_chunks = pl.program_id(1), pl.num_programs(1)
    rows = da_ref.shape[0]
    half = da_ref.shape[1] // 2
    keys = v_ref.shape[0]

    @pl.when(chunk == 0)
    def _():
        acc_scr[...] = jnp.zeros_like(acc_scr)

    factor = jnp.exp(m_ref[0, 0] - lse_ref[0])
    delta = delta_ref[0]
    da_cat = pair_rows(da_ref[...], half)
    acc = acc_scr[...]
    for t in range(keys // tile):
        rng = slice(t * tile, (t + 1) * tile)
        dp = dot_nt(v_ref[rng, :], da_cat)
        p = jnp.concatenate([p_ref[0, rng, :], p_ref[1, rng, :]], axis=1).astype(jnp.float32)
        ds = ((p * factor) * (dp - delta)).astype(jnp.bfloat16)
        ds_ref[0, rng, :] = ds[:, :rows]
        ds_ref[1, rng, :] = ds[:, rows:]
        acc = acc + dot_tn(k_ref[rng, :], ds)
    acc_scr[...] = acc

    @pl.when(chunk == n_chunks - 1)
    def _():
        dq_ref[...] = jnp.transpose(pair_blocks(acc, half, rows)).astype(jnp.bfloat16)


def query_back(probs, made, payload, delta, lse, lows, chunk_keys, tile=512):
    heads, total, rows = probs.shape
    pairs = heads // 2
    width = made.shape[1] // 3
    wide = width // pairs
    n_chunks = total // chunk_keys
    return pl.pallas_call(
        functools.partial(query_back_kernel, tile),
        grid=(pairs, n_chunks),
        in_specs=[
            pl.BlockSpec((2, chunk_keys, rows), lambda p, c: (p, c, 0)),
            pl.BlockSpec((chunk_keys, wide), lambda p, c: (c, 2 * pairs + p)),
            pl.BlockSpec((chunk_keys, wide), lambda p, c: (c, pairs + p)),
            pl.BlockSpec((rows, wide), lambda p, c: (0, p)),
            pl.BlockSpec((1, 1, 2 * rows), lambda p, c: (p, 0, 0)),
            pl.BlockSpec((1, 1, 2 * rows), lambda p, c: (p, 0, 0)),
            pl.BlockSpec((1, 1, 1, 2 * rows), lambda p, c: (p, c, 0, 0)),
        ],
        out_specs=[
            pl.BlockSpec((2, chunk_keys, rows), lambda p, c: (p, c, 0)),
            pl.BlockSpec((rows, wide), lambda p, c: (0, p)),
        ],
        out_shape=[
            jax.ShapeDtypeStruct((heads, total, rows), jnp.bfloat16),
            jax.ShapeDtypeStruct((rows, width), jnp.bfloat16),
        ],
        scratch_shapes=[pltpu.VMEM((wide, 2 * rows), jnp.float32)],
        input_output_aliases={0: 0},
        compiler_params=pltpu.CompilerParams(vmem_limit_bytes=VMEM_BYTES),
        cost_estimate=cost_of(0.005 * total),
        name="query_back",
    )(probs, made, made, payload, delta, lse, lows)


def key_back_kernel(count, *refs):
    grads, auxes, refs = refs[:PIECES], refs[PIECES : 2 * PIECES], refs[2 * PIECES :]
    q_ref, idx_ref, k_ref, v_ref, tab_ref, dk_ref, dv_ref, dk_scr, dv_scr = refs
    pair, chunk, n_chunks = pl.program_id(0), pl.program_id(1), pl.num_programs(1)
    rows = k_ref.shape[0]
    wide = k_ref.shape[1]
    half = wide // 2

    @pl.when(chunk == 0)
    def _():
        dk_scr[...] = jnp.zeros_like(dk_scr)
        dv_scr[...] = jnp.zeros_like(dv_scr)

    lane = lax.broadcasted_iota(jnp.int32, (2 * rows, 128), 1)
    head = 2 * pair + (lax.broadcasted_iota(jnp.int32, (2 * rows, 128), 0) >= rows).astype(jnp.int32)
    first = (lane >= 2 * head) & (lane < 2 * head + 2)
    second = (lane >= 64 + 2 * head) & (lane < 64 + 2 * head + 2)
    take_lse = jnp.where(first, -1.0, 0.0).astype(jnp.bfloat16)
    take_delta = jnp.where(second, -1.0, 0.0).astype(jnp.bfloat16)
    k_cat = jnp.concatenate([pair_rows(k_ref[...], half), take_lse], axis=1)
    v_cat = jnp.concatenate([pair_rows(v_ref[...], half), take_delta], axis=1)
    dk, dv = dk_scr[...], dv_scr[...]
    for t in range(0, PIECES, count):
        da = jnp.concatenate([ref[...] for ref in grads[t : t + count]], axis=0)
        aux = jnp.concatenate([ref[...] for ref in auxes[t : t + count]], axis=0)
        q = q_ref[t : t + count].reshape(count * rows, wide)
        index = idx_ref[t : t + count].reshape(count * rows, rows)
        s = dot_nt(jnp.concatenate([q, aux], axis=1), k_cat)
        bias = jnp.concatenate(
            [bias_of(tab_ref[0, j : j + 1, :], index) for j in range(2)], axis=1
        )
        p = jnp.exp(s + bias)
        ds = p * dot_nt(jnp.concatenate([da, aux], axis=1), v_cat)
        dv = dv + dot_tn(da, p.astype(jnp.bfloat16))
        dk = dk + dot_tn(q, ds.astype(jnp.bfloat16))
    dk_scr[...] = dk
    dv_scr[...] = dv

    @pl.when(chunk == n_chunks - 1)
    def _():
        dk_ref[...] = jnp.transpose(pair_blocks(dk, half, rows)).astype(jnp.bfloat16)
        dv_ref[...] = jnp.transpose(pair_blocks(dv, half, rows)).astype(jnp.bfloat16)


def key_back(pieces, made, index, table, count=4):
    rows = index.shape[2]
    side, width = made.shape[1], made.shape[2] // 3
    pairs = table.shape[0]
    wide = width // pairs
    n_chunks = side // rows
    return pl.pallas_call(
        functools.partial(key_back_kernel, count),
        grid=(pairs, n_chunks),
        in_specs=[pl.BlockSpec((rows, wide), lambda p, c: (c, p))] * PIECES
        + [pl.BlockSpec((rows, 128), lambda p, c: (c, pairs))] * PIECES
        + [
            pl.BlockSpec((PIECES, rows, wide), lambda p, c: (0, c, p)),
            pl.BlockSpec((PIECES, rows, rows), lambda p, c: (0, c, 0)),
            pl.BlockSpec((rows, wide), lambda p, c: (0, pairs + p)),
            pl.BlockSpec((rows, wide), lambda p, c: (0, 2 * pairs + p)),
            pl.BlockSpec((1, 2, 128), lambda p, c: (p, 0, 0)),
        ],
        out_specs=[
            pl.BlockSpec((rows, wide), lambda p, c: (0, p)),
            pl.BlockSpec((rows, wide), lambda p, c: (0, p)),
        ],
        out_shape=[
            jax.ShapeDtypeStruct((rows, width), jnp.bfloat16),
            jax.ShapeDtypeStruct((rows, width), jnp.bfloat16),
        ],
        scratch_shapes=[
            pltpu.VMEM((wide, 2 * rows), jnp.float32),
            pltpu.VMEM((wide, 2 * rows), jnp.float32),
        ],
        compiler_params=pltpu.CompilerParams(vmem_limit_bytes=VMEM_BYTES),
        cost_estimate=cost_of(15 * n_chunks),
        name="key_back",
    )(*pieces, *pieces, made, index, made[0], made[0], table)


def norm_back(values, inverse, scale_gain, grad_normed):
    grad_gain = jnp.sum(grad_normed * values * inverse, axis=0)
    scaled = grad_normed * scale_gain
    grad_values = inverse * (
        scaled - values * inverse * inverse * jnp.mean(scaled * values, axis=1, keepdims=True)
    )
    return (grad_gain, grad_values)


def smooth_gate(values):
    return jax.nn.gelu(values, approximate=True)


def dot_f32(left, right):
    return jnp.dot(left, right, preferred_element_type=jnp.float32)


def swap_ctx(values, distance):
    size = lax.axis_size("ctx")
    return lax.ppermute(values, "ctx", [(i, i ^ distance) for i in range(size)])


def swap_pair(values):
    return lax.ppermute(values, "fsdp", [(0, 1), (1, 0)])


def in_order(where, mine, other, axis=0):
    return jnp.where(
        where == 0,
        jnp.concatenate([mine, other], axis=axis),
        jnp.concatenate([other, mine], axis=axis),
    )


def part_of(values, index, parts, axis):
    size = values.shape[axis] // parts
    return lax.dynamic_slice_in_dim(values, index * size, size, axis)


def tied(*members):
    return lax.optimization_barrier(members)


def gather_group(block, ties=(None, None, None, None)):
    size = lax.axis_size("ctx")
    quarter = size // 4
    ties = list(ties)
    block = block[None]
    distance = 2 * 2
    while distance < quarter:
        block = jnp.concatenate([block, swap_ctx(block, distance)], axis=0)
        distance *= 2
    far = [swap_ctx(block, quarter * j) for j in (1, 2, 3)]
    near = [block, swap_ctx(block, 2)]
    for j in range(3):
        if ties[j] is not None:
            far[j], ties[j] = tied(far[j], ties[j])
        near += [far[j], swap_ctx(far[j], 2)]
    if ties[3] is not None:
        near[-1], ties[3] = tied(near[-1], ties[3])
    return near + [swap_ctx(piece, 1) for piece in near], ties


def scatter_sum(blocks, tie):
    here, size = lax.axis_index("ctx"), lax.axis_size("ctx")
    low, f32 = blocks.dtype, jnp.float32
    distance = 1
    while distance < size // 4:
        mine = (here // distance) % 2
        got = swap_ctx(part_of(blocks, 1 - mine, 2, 0), distance)
        blocks = (part_of(blocks, mine, 2, 0).astype(f32) + got.astype(f32)).astype(low)
        if distance == 1:
            blocks, tie = tied(blocks, tie)
        distance *= 2
    mine = here // distance
    got = [swap_ctx(part_of(blocks, mine ^ j, 4, 0), distance * j) for j in (1, 2, 3)]
    added = part_of(blocks, mine, 4, 0).astype(f32) + sum(member.astype(f32) for member in got)
    return added.astype(low), tie


def gather_back(block):
    here, size = lax.axis_index("ctx"), lax.axis_size("ctx")
    distance = size // 4
    got = [swap_ctx(block, distance * j) for j in (1, 2, 3)]
    low_bit, high_bit = (here // distance) % 2, here // (2 * distance)
    blocks = in_order(high_bit, in_order(low_bit, block, got[0]), in_order(low_bit, got[1], got[2]))
    while distance > 2:
        distance //= 2
        blocks = in_order((here // distance) % 2, blocks, swap_ctx(blocks, distance))
    return blocks, swap_ctx(blocks, 1)


def sent_weights(*members):
    core = lax.axis_index("ctx") % 2
    return swap_pair(jnp.stack([part_of(member, core, 2, 0) for member in members]))


def shards(
    tokens,
    cotangent,
    lengths,
    dealing,
    gain_one,
    w_query,
    w_key,
    w_value,
    w_out,
    gain_two,
    w_in,
    w_ff,
    rel_table,
):
    bf16, f32 = jnp.bfloat16, jnp.float32
    size = lax.axis_size("ctx")
    pair = lax.axis_index("fsdp")
    rows, width = tokens.shape[1], tokens.shape[2]
    heads = rel_table.shape[1]
    head_size = width // heads
    pairs = heads // 2
    total = size * rows
    half_ff = w_ff.shape[0]
    half_width = w_query.shape[0]
    chunk_keys = min(total, 2048)

    spot = jnp.concatenate(
        [jnp.stack([pair, lax.axis_index("ctx") % 2]).astype(jnp.int32), lengths[0]]
    )

    dealt = dealing[0]
    place_row = jnp.concatenate([dealt // 128, dealt % 128]).astype(bf16)
    place_rows = jnp.pad(place_row[None], ((0, 7), (0, width - 2 * rows)))
    pieces = gather_group(jnp.concatenate([tokens[0], place_rows], axis=0))[0]

    small = jnp.concatenate([gain_one, gain_two, rel_table.reshape(-1)])
    small = jnp.pad(small, (0, 1024 - small.shape[0])).reshape(8, 128)
    small_other = swap_pair(small)
    small_full = jnp.stack([small.reshape(-1), small_other.reshape(-1)])
    small_full = jnp.where(pair == 0, small_full, small_full[::-1])
    gain32_one = small_full[:, :half_width].reshape(width).astype(f32)
    gain32_two = small_full[:, half_width : 2 * half_width].reshape(width).astype(f32)
    full_table = small_full[:, 2 * half_width : 2 * half_width + rel_table.size]
    full_table = full_table.reshape(2 * rel_table.shape[0], heads).astype(f32)
    got_one = sent_weights(w_query, w_key, w_value)
    more_one = swap_ctx(got_one, 1)
    pieces[4], w_out, w_in, cotangent = tied(pieces[4], w_out, w_in, cotangent)
    mine_in, other_in = (part_of(w_in, index, 2, 1) for index in (pair, 1 - pair))
    got_two = sent_weights(w_out, other_in[:, :width], other_in[:, width:])
    grad_out = cotangent[0]
    grad_out_pair = jnp.concatenate([grad_out, swap_pair(grad_out)], axis=0)

    table_t = jnp.transpose(full_table)
    back_t = jnp.concatenate(
        [table_t[:, :1], table_t[:, 17:], table_t[:, :1], table_t[:, 1:16]], axis=1
    )
    tables = [
        jnp.pad(tab, ((0, 0), (0, 128 - BUCKETS)), constant_values=NEG).reshape(pairs, 2, 128)
        for tab in (table_t, back_t)
    ]
    made, index, normed_one, w_qkv = project(
        spot,
        pieces,
        gain32_one[None],
        (w_query, w_key, w_value),
        got_one,
        more_one,
        rows,
        total,
        lengths.shape[1],
    )
    made, got_two = tied(made, got_two)
    more_two = swap_ctx(got_two, 1)
    flat_made, flat_index = made.reshape(total, 3 * width), index.reshape(total, rows)
    attn_f32, lse, lows, probs = attend(flat_made, flat_index, tables[0], chunk_keys)

    resid, normed_two, attn_b, full_out = close(
        spot, attn_f32, tokens[0], gain32_two[None], w_out, got_two, more_two
    )
    normed_pair = jnp.concatenate([normed_two, swap_pair(normed_two)], axis=0)
    core = lax.axis_index("ctx") % 2
    half_in = jnp.concatenate(
        [
            in_order(
                pair,
                mine_in[:, j * width : (j + 1) * width],
                in_order(core, got_two[1 + j], more_two[1 + j]),
            )
            for j in range(2)
        ],
        axis=1,
    )
    gate_pre = dot_f32(normed_pair, half_in)
    gate_val, gate_pull = jax.vjp(smooth_gate, gate_pre)
    active = gate_val.astype(bf16)
    grad_active = jnp.einsum("td,fd->tf", grad_out_pair, w_ff, preferred_element_type=f32)
    grad_pre = gate_pull(grad_active)[0].astype(bf16)
    grad_normed_part = jnp.einsum("tf,df->td", grad_pre, half_in, preferred_element_type=f32)
    payload, delta, grad_resid, grad_branch, grad_gain_two = branch(
        grad_normed_part[:rows],
        swap_pair(grad_normed_part[rows:].astype(bf16)),
        resid,
        grad_out,
        gain32_two[None],
        full_out,
        attn_f32,
        lse.reshape(heads, rows),
    )
    payload, active, normed_pair, grad_pre, attn_b = tied(
        payload, active, normed_pair, grad_pre, attn_b
    )

    def halves(values):
        other = swap_pair(part_of(values, 1 - pair, 2, 1))
        return jnp.concatenate([part_of(values, pair, 2, 1), other], axis=0)

    def both(values):
        return jnp.concatenate([values, swap_pair(values)], axis=0)

    def by_rows(left, right):
        return jnp.einsum("td,te->de", left, right, preferred_element_type=f32).astype(bf16)

    def blocks_of(values):
        return [
            values[:, j : j + width].reshape(size, values.shape[0] // size, width)
            for j in range(0, values.shape[1], width)
        ]

    tall = half_width // size
    tall_ff = half_ff // size
    grad_ff_part = by_rows(active, grad_out_pair)
    grad_in_part = by_rows(normed_pair, grad_pre)
    branch_other = swap_pair(
        jnp.concatenate([part_of(attn_b, 1 - pair, 2, 1), grad_branch], axis=1)
    )
    attn_pair = jnp.concatenate([part_of(attn_b, pair, 2, 1), branch_other[:, :half_width]], axis=0)
    branch_pair = jnp.concatenate([grad_branch, branch_other[:, half_width:]], axis=0)
    grad_out_part = by_rows(attn_pair, branch_pair)
    in_blocks = blocks_of(part_of(grad_in_part, pair, 2, 0)) + blocks_of(
        part_of(grad_in_part, 1 - pair, 2, 0)
    )
    ff_blocks = jnp.concatenate(
        blocks_of(grad_ff_part) + in_blocks + blocks_of(grad_out_part), axis=1
    )
    ff_tall = ff_blocks.shape[1]

    grad_scores, grad_q = query_back(
        probs, flat_made, payload, delta.reshape(pairs, 1, 2 * rows), lse, lows, chunk_keys
    )
    one_hot = (flat_index[:, :, None] == jnp.arange(BUCKETS, dtype=jnp.int32)).astype(bf16)
    grad_tab = jnp.einsum("hkq,kqb->hb", grad_scores, one_hot, preferred_element_type=f32)
    grad_pieces, ties = gather_group(
        payload, ((grad_ff_part, grad_in_part), ff_blocks, grad_q, grad_tab)
    )
    ff_blocks, grad_q, grad_tab = ties[1:]
    ff_sum = lax.psum_scatter(
        ff_blocks.reshape(size * ff_tall, width), "ctx", scatter_dimension=0, tiled=True
    )
    grad_k, grad_v = key_back(
        [piece.reshape(-1, width + 128) for piece in grad_pieces], made, index, tables[1]
    )
    out_part = dot_f32(active, w_ff)
    output = resid + out_part[:rows] + swap_pair(out_part[rows:].astype(bf16)).astype(f32)

    grads_kv = jnp.concatenate([grad_k, grad_v], axis=1)
    normed_halves = halves(normed_one)
    grad_q_part = by_rows(normed_halves, both(grad_q))
    grad_kv_part = by_rows(normed_halves, both(grads_kv))
    inputs = tokens[0].astype(f32)
    inv_one = lax.rsqrt(jnp.mean(inputs * inputs, axis=1, keepdims=True) + EPS)
    grad_normed_one = sum(
        jnp.einsum("te,de->td", member, w_qkv[j], preferred_element_type=f32)
        for j, member in enumerate((grad_q, grad_k, grad_v))
    )
    grad_gain_one, grad_input_norm = norm_back(inputs, inv_one, gain32_one, grad_normed_one)
    grad_tokens = grad_resid + grad_input_norm

    small_grads = jnp.concatenate(
        [
            grad_gain_one.reshape(2, half_width),
            grad_gain_two.reshape(2, half_width),
            jnp.transpose(grad_tab).reshape(2, rel_table.size),
        ],
        axis=1,
    )
    n_small = small_grads.shape[1]
    each = -(-n_small // size)
    small_grads = jnp.pad(small_grads, ((0, 0), (0, size * each - n_small)))
    small_pair = part_of(small_grads, pair, 2, 0) + swap_pair(part_of(small_grads, 1 - pair, 2, 0))
    small_blocks = jnp.pad(
        small_pair.astype(bf16).reshape(size, 1, each), ((0, 0), (0, 7), (0, width - each))
    )
    qkv_sum, ff_sum = scatter_sum(
        jnp.concatenate(
            blocks_of(grad_q_part) + blocks_of(grad_kv_part) + [small_blocks], axis=1
        ),
        ff_sum,
    )
    first_in, last_in = tall_ff, tall_ff + 4 * tall
    moved = swap_pair(ff_sum[tall_ff + 2 * tall : last_in])
    ff_sum = jnp.concatenate([ff_sum[: tall_ff + 2 * tall], moved, ff_sum[last_in:]], axis=0)
    ff_full = lax.all_gather(ff_sum, "ctx", axis=0, tiled=True).reshape(size, ff_tall, width)
    near_sum, far_sum = gather_back(qkv_sum)
    small_halves = [member[:, 3 * tall, :each].reshape(-1) for member in (near_sum, far_sum)]
    small_mine = in_order(spot[1], *small_halves).astype(f32)
    grad_qkv = [
        member.reshape(half_width, width) for member in unpack(spot, near_sum, far_sum, tall, 3)
    ]
    grad_ff, grad_in, grad_out_w = spread(spot, ff_full, tall_ff, tall)
    return (
        output.astype(bf16)[None],
        grad_tokens[None],
        small_mine[:half_width],
        *grad_qkv,
        grad_out_w.reshape(half_width, width),
        small_mine[half_width : 2 * half_width],
        grad_in.reshape(half_width, 4 * width),
        grad_ff.reshape(half_ff, width),
        small_mine[2 * half_width : n_small].reshape(rel_table.shape),
    )


def solution(mesh):
    spread = P("fsdp", "ctx", None)
    rows_of = P("fsdp", None)
    return jax.shard_map(
        shards,
        mesh=mesh,
        in_specs=(
            spread,
            spread,
            rows_of,
            P("fsdp", "ctx"),
            P("fsdp"),
            rows_of,
            rows_of,
            rows_of,
            rows_of,
            P("fsdp"),
            rows_of,
            rows_of,
            rows_of,
        ),
        out_specs=(
            spread,
            spread,
            P("fsdp"),
            rows_of,
            rows_of,
            rows_of,
            rows_of,
            P("fsdp"),
            rows_of,
            rows_of,
            rows_of,
        ),
        check_vma=False,
    )
```

```python
import functools
import jax
import jax.numpy as jnp
from jax import lax
from jax.experimental import pallas as pl
from jax.experimental.pallas import tpu as pltpu
from jax.sharding import PartitionSpec as P

BUCKETS = 32
PIECES = 8
EPS = 1e-06
NEG = -1000000000.0
THRESHOLDS = (1, 2, 3, 4, 5, 6, 7, 8, 12, 16, 23, 32, 46, 64, 91)
VMEM_BYTES = 50 * 1024 * 1024
VMEM_MOST = 63 * 1024 * 1024


def cost_of(micros):
    return pl.CostEstimate(flops=int(micros * 8e8), bytes_accessed=int(micros * 2.5e6), transcendentals=0)


def dot_nt(left, right):
    return lax.dot_general(left, right, (((1,), (1,)), ((), ())), preferred_element_type=jnp.float32)


def dot_tn(left, right):
    return lax.dot_general(left, right, (((0,), (0,)), ((), ())), preferred_element_type=jnp.float32)


def pair_rows(block, half):
    lane = lax.broadcasted_iota(jnp.int32, block.shape, 1)
    zero = jnp.zeros_like(block)
    return jnp.concatenate(
        [jnp.where(lane < half, block, zero), jnp.where(lane < half, zero, block)], axis=0
    )


def pair_blocks(acc, half, rows):
    return jnp.concatenate([acc[:half, :rows], acc[half:, rows:]], axis=0)


def bias_of(row, index):
    return jnp.take_along_axis(jnp.broadcast_to(row, index.shape), index, axis=1)


def fill_rows(out_ref, j, own, got, more, spot_ref):
    rows, part = own.shape[0], got.shape[0]
    other = (1 - spot_ref[0]) * rows
    out_ref[j, pl.ds(pl.multiple_of(spot_ref[0] * rows, 64), rows), :] = own
    out_ref[j, pl.ds(pl.multiple_of(other + spot_ref[1] * part, 64), part), :] = got
    out_ref[j, pl.ds(pl.multiple_of(other + (1 - spot_ref[1]) * part, 64), part), :] = more


def marks_of(places, total, seqs, spot_ref):
    rows = places.shape[1] // 2
    spots = places[:, :rows] * 128.0 + places[:, rows:]
    end = 0
    begin, segment = jnp.zeros_like(spots), jnp.zeros_like(spots)
    for j in range(seqs):
        end = end + spot_ref[2 + j]
        passed = spots >= end.astype(jnp.float32)
        begin = jnp.where(passed, end.astype(jnp.float32), begin)
        segment = jnp.where(passed, segment + 1.0, segment)
    return spots - begin + segment * (2.0 * total)


def project_kernel(count, total, seqs, first, spot_ref, *refs):
    pieces, refs = refs[:PIECES], refs[PIECES:]
    if first:
        gain_ref, place_ref, wq_ref, wk_ref, wv_ref, got_ref, more_ref = refs[:7]
        made_ref, idx_ref, full_ref, normed_ref, rows_scr, place_scr = refs[7:]
    else:
        gain_ref, place_ref, full_ref, made_ref, idx_ref, rows_scr, place_scr = refs
    width = gain_ref.shape[1]
    rows = idx_ref.shape[2]
    outer, inner = pl.program_id(0), pl.program_id(1)

    for group in range(PIECES // count):

        @pl.when(inner == group)
        def _():
            for j in range(count):
                held = pieces[group * count + j][0]
                rows_scr[j * rows : (j + 1) * rows, :] = held[:rows]
                place_scr[j : j + 1, :] = held[rows:].astype(jnp.float32)[:1, : 2 * rows]

    if first:

        @pl.when((outer == 0) & (inner == 0))
        def _():
            for j, ref in enumerate((wq_ref, wk_ref, wv_ref)):
                fill_rows(full_ref, j, ref[...], got_ref[j], more_ref[j], spot_ref)

    values = rows_scr[...].astype(jnp.float32)
    inverse = lax.rsqrt(jnp.mean(values * values, axis=1, keepdims=True) + EPS)
    normed = (values * inverse * gain_ref[...]).astype(jnp.bfloat16)
    shape = (count, rows, width)
    for j in range(3):
        made = jnp.dot(normed, full_ref[j], preferred_element_type=jnp.float32)
        made_ref[:, :, j * width : (j + 1) * width] = made.astype(jnp.bfloat16).reshape(shape)

    if first:

        @pl.when((outer == 0) & (inner == 0))
        def _():
            normed_ref[...] = normed[:rows]

    own = marks_of(place_ref[...].astype(jnp.float32)[:1, : 2 * rows], total, seqs, spot_ref)
    turned = jnp.transpose(marks_of(place_scr[...], total, seqs, spot_ref))
    for j in range(count):
        offset = turned[:, j : j + 1] - own
        distance = jnp.abs(offset)
        bucket = jnp.where(offset > 0, BUCKETS // 2, 0)
        for threshold in THRESHOLDS:
            bucket = bucket + (distance >= threshold).astype(jnp.int32)
        idx_ref[j] = jnp.where(distance >= total, BUCKETS, bucket)


def project(spot, pieces, gain, places, weights, rows, total, seqs, count=4):
    devices, tall, width = pieces[0].shape
    first = len(weights) > 1
    fixed = lambda rank: (lambda i, j, spot: (0,) * rank)
    moving = lambda i, j, spot: (j, i, 0)
    outputs = [
        (
            pl.BlockSpec((count, rows, 3 * width), moving),
            jax.ShapeDtypeStruct((PIECES, devices * rows, 3 * width), jnp.bfloat16),
        ),
        (
            pl.BlockSpec((count, rows, rows), moving),
            jax.ShapeDtypeStruct((PIECES, devices * rows, rows), jnp.int32),
        ),
    ]
    if first:
        outputs += [
            (
                pl.BlockSpec((3, width, width), fixed(3)),
                jax.ShapeDtypeStruct((3, width, width), jnp.bfloat16),
            ),
            (
                pl.BlockSpec((rows, width), fixed(2)),
                jax.ShapeDtypeStruct((rows, width), jnp.bfloat16),
            ),
        ]
    operands = (gain, places) + tuple(weights)
    return pl.pallas_call(
        functools.partial(project_kernel, count, total, seqs, first),
        grid_spec=pltpu.PrefetchScalarGridSpec(
            num_scalar_prefetch=1,
            grid=(devices, PIECES // count),
            in_specs=[pl.BlockSpec((1, tall, width), lambda i, j, spot: (i, 0, 0))] * PIECES
            + [pl.BlockSpec(member.shape, fixed(member.ndim)) for member in operands],
            out_specs=[spec for spec, _ in outputs],
            scratch_shapes=[
                pltpu.VMEM((count * rows, width), jnp.bfloat16),
                pltpu.VMEM((8, 2 * rows), jnp.float32),
            ],
        ),
        out_shape=[shape for _, shape in outputs],
        compiler_params=pltpu.CompilerParams(vmem_limit_bytes=VMEM_BYTES),
        cost_estimate=cost_of(0.7 * PIECES * devices),
        name="project",
    )(spot, *pieces, *operands)


def close_kernel(spot_ref, attn_ref, x_ref, gain_ref, w_ref, got_ref, more_ref, resid_ref, normed_ref, attn_b_ref, full_ref):
    fill_rows(full_ref, 0, w_ref[...], got_ref[0], more_ref[0], spot_ref)
    attn = attn_ref[...].astype(jnp.bfloat16)
    attn_b_ref[...] = attn
    resid = x_ref[...].astype(jnp.float32) + jnp.dot(
        attn, full_ref[0], preferred_element_type=jnp.float32
    )
    resid_ref[...] = resid
    inverse = lax.rsqrt(jnp.mean(resid * resid, axis=1, keepdims=True) + EPS)
    normed_ref[...] = (resid * inverse * gain_ref[...]).astype(jnp.bfloat16)


def close(spot, attn, tokens, gain, weight, got, more):
    rows, width = attn.shape
    held, part = weight.shape[0], got.shape[1]
    whole = lambda i, spot: (0, 0)
    first = lambda i, spot: (0, 0, 0)
    return pl.pallas_call(
        close_kernel,
        grid_spec=pltpu.PrefetchScalarGridSpec(
            num_scalar_prefetch=1,
            grid=(1,),
            in_specs=[
                pl.BlockSpec((rows, width), whole),
                pl.BlockSpec((rows, width), whole),
                pl.BlockSpec((1, width), whole),
                pl.BlockSpec((held, width), whole),
                pl.BlockSpec((1, part, width), first),
                pl.BlockSpec((1, part, width), first),
            ],
            out_specs=[
                pl.BlockSpec((rows, width), whole),
                pl.BlockSpec((rows, width), whole),
                pl.BlockSpec((rows, width), whole),
                pl.BlockSpec((1, width, width), first),
            ],
        ),
        out_shape=[
            jax.ShapeDtypeStruct((rows, width), jnp.float32),
            jax.ShapeDtypeStruct((rows, width), jnp.bfloat16),
            jax.ShapeDtypeStruct((rows, width), jnp.bfloat16),
            jax.ShapeDtypeStruct((1, width, width), jnp.bfloat16),
        ],
        compiler_params=pltpu.CompilerParams(vmem_limit_bytes=VMEM_BYTES),
        cost_estimate=cost_of(2),
        name="close",
    )(spot, attn, tokens, gain, weight, got, more)


def branch_kernel(part_ref, got_ref, resid_ref, cot_ref, gain_ref, out_ref, attn_ref, lse_ref, payload_ref, delta_ref, grad_ref, branch_ref, gain_grad_ref):
    f32, bf16 = jnp.float32, jnp.bfloat16
    rows, width = resid_ref.shape
    heads = lse_ref.shape[0]
    size = width // heads
    resid = resid_ref[...]
    normed_grad = part_ref[...] + got_ref[...].astype(f32)
    inverse = lax.rsqrt(jnp.mean(resid * resid, axis=1, keepdims=True) + EPS)
    gain_grad_ref[...] = jnp.sum(normed_grad * resid * inverse, axis=0, keepdims=True)
    scaled = normed_grad * gain_ref[...]
    mean = jnp.mean(scaled * resid, axis=1, keepdims=True)
    grad = cot_ref[...].astype(f32) + inverse * (scaled - resid * (inverse * inverse * mean))
    grad_ref[...] = grad
    branch = grad.astype(bf16)
    branch_ref[...] = branch
    attn_grad = dot_nt(branch, out_ref[0]).astype(bf16)
    payload_ref[:, :width] = attn_grad
    product = attn_grad.astype(f32) * attn_ref[...]
    high = product.astype(bf16)
    low = (product - high.astype(f32)).astype(bf16)

    def member(shape, at_row, at_col):
        row = lax.broadcasted_iota(jnp.int32, shape, 0)
        col = lax.broadcasted_iota(jnp.int32, shape, 1)
        return jnp.where(at_row(row) == at_col(col), 1.0, 0.0).astype(bf16)

    padded = 16
    by_head = member((padded, width), lambda r: r, lambda c: c // size)
    delta = (dot_nt(by_head, high) + dot_nt(by_head, low))[:heads]
    delta_ref[...] = delta
    col = lax.broadcasted_iota(jnp.int32, (rows, 128), 1)
    aux = jnp.zeros((rows, 128), f32)
    for first, values in ((0, lse_ref[...]), (64, delta)):
        values = jnp.concatenate([values, jnp.zeros((padded - heads, rows), f32)], axis=0)
        high = values.astype(bf16)
        low = (values - high.astype(f32)).astype(bf16)
        for odd, half in ((0, high), (1, low)):
            to_col = member((padded, 128), lambda r: first + odd + 2 * r, lambda c: c)
            aux = aux + dot_tn(half, to_col)
    payload_ref[:, width:] = aux.astype(bf16)


def branch(part, got, resid, cotangent, gain, full_out, attn, lse):
    rows, width = resid.shape
    heads = lse.shape[0]
    return pl.pallas_call(
        branch_kernel,
        grid=(1,),
        in_specs=[
            pl.BlockSpec((rows, width), lambda i: (0, 0)),
            pl.BlockSpec((rows, width), lambda i: (0, 0)),
            pl.BlockSpec((rows, width), lambda i: (0, 0)),
            pl.BlockSpec((rows, width), lambda i: (0, 0)),
            pl.BlockSpec((1, width), lambda i: (0, 0)),
            pl.BlockSpec((1, width, width), lambda i: (0, 0, 0)),
            pl.BlockSpec((rows, width), lambda i: (0, 0)),
            pl.BlockSpec((heads, rows), lambda i: (0, 0)),
        ],
        out_specs=[
            pl.BlockSpec((rows, width + 128), lambda i: (0, 0)),
            pl.BlockSpec((heads, rows), lambda i: (0, 0)),
            pl.BlockSpec((rows, width), lambda i: (0, 0)),
            pl.BlockSpec((rows, width), lambda i: (0, 0)),
            pl.BlockSpec((1, width), lambda i: (0, 0)),
        ],
        out_shape=[
            jax.ShapeDtypeStruct((rows, width + 128), jnp.bfloat16),
            jax.ShapeDtypeStruct((heads, rows), jnp.float32),
            jax.ShapeDtypeStruct((rows, width), jnp.float32),
            jax.ShapeDtypeStruct((rows, width), jnp.bfloat16),
            jax.ShapeDtypeStruct((1, width), jnp.float32),
        ],
        compiler_params=pltpu.CompilerParams(vmem_limit_bytes=VMEM_BYTES),
        cost_estimate=cost_of(3),
        name="branch",
    )(part, got, resid, cotangent, gain, full_out, attn, lse)


def unpack_kernel(tall, spot_ref, near_ref, far_ref, *out_refs):
    values = jnp.where(pl.program_id(0) == 0, near_ref[...], far_ref[...]).astype(jnp.float32)
    for j, ref in enumerate(out_refs[:-1]):
        ref[...] = values[:, j * tall : (j + 1) * tall, :]
    out_refs[-1][...] = values[:, (len(out_refs) - 1) * tall :, :128]


def unpack(spot, near, far, tall, outputs):
    half, high, width = near.shape
    step = min(4, half)
    steps = half // step

    def place(j, i, spot):
        return (jnp.bitwise_xor(j, spot[1]) * steps + i, 0, 0)

    return pl.pallas_call(
        functools.partial(unpack_kernel, tall),
        grid_spec=pltpu.PrefetchScalarGridSpec(
            num_scalar_prefetch=1,
            grid=(2, steps),
            in_specs=[
                pl.BlockSpec(
                    (step, high, width), lambda j, i, spot: (jnp.where(j == 0, i, steps - 1), 0, 0)
                ),
                pl.BlockSpec(
                    (step, high, width), lambda j, i, spot: (jnp.where(j == 0, 0, i), 0, 0)
                ),
            ],
            out_specs=[pl.BlockSpec((step, tall, width), place)] * outputs
            + [pl.BlockSpec((step, high - outputs * tall, 128), place)],
        ),
        out_shape=[jax.ShapeDtypeStruct((2 * half, tall, width), jnp.float32)] * outputs
        + [jax.ShapeDtypeStruct((2 * half, high - outputs * tall, 128), jnp.float32)],
        compiler_params=pltpu.CompilerParams(vmem_limit_bytes=VMEM_BYTES),
        cost_estimate=cost_of(4),
        name="unpack",
    )(spot, near, far)


def spread_kernel(tall_ff, tall, spot_ref, full_ref, ff_ref, in_ref, out_ref):
    width = out_ref.shape[2]
    values = full_ref[...].astype(jnp.float32)
    ff_ref[...] = values[:, :tall_ff, :]
    parts = [values[:, tall_ff + j * tall : tall_ff + (j + 1) * tall, :] for j in range(5)]
    for j in range(2):
        in_ref[:, :, j * width : (j + 1) * width] = jnp.where(
            spot_ref[0] == 0, parts[j], parts[2 + j]
        )
        in_ref[:, :, (2 + j) * width : (3 + j) * width] = jnp.where(
            spot_ref[0] == 0, parts[2 + j], parts[j]
        )
    out_ref[...] = parts[4]


def spread(spot, full, tall_ff, tall):
    size, high, width = full.shape
    step = 4
    return pl.pallas_call(
        functools.partial(spread_kernel, tall_ff, tall),
        grid_spec=pltpu.PrefetchScalarGridSpec(
            num_scalar_prefetch=1,
            grid=(size // step,),
            in_specs=[pl.BlockSpec((step, high, width), lambda i, spot: (i, 0, 0))],
            out_specs=[
                pl.BlockSpec((step, tall_ff, width), lambda i, spot: (i, 0, 0)),
                pl.BlockSpec((step, tall, 4 * width), lambda i, spot: (i, 0, 0)),
                pl.BlockSpec((step, tall, width), lambda i, spot: (i, 0, 0)),
            ],
        ),
        out_shape=[
            jax.ShapeDtypeStruct((size, tall_ff, width), jnp.float32),
            jax.ShapeDtypeStruct((size, tall, 4 * width), jnp.float32),
            jax.ShapeDtypeStruct((size, tall, width), jnp.float32),
        ],
        compiler_params=pltpu.CompilerParams(vmem_limit_bytes=VMEM_BYTES),
        cost_estimate=cost_of(6),
        name="spread",
    )(spot, full)


def attend_kernel(tile, first, q_ref, k_ref, v_ref, idx_ref, tab_ref, *refs):
    if first:
        outs, m_out, p_ref, s_scr, m_scr, l_scr, acc_scr = refs[:3], *refs[3:]
    else:
        kept, outs, m_out, p_ref, s_scr, m_scr, l_scr, acc_scr = refs[:3], refs[3:5], *refs[5:]
    chunk, n_chunks = pl.program_id(1), pl.num_programs(1)
    rows = q_ref.shape[0]
    half = q_ref.shape[1] // 2
    keys = k_ref.shape[0]

    @pl.when(chunk == 0)
    def _():
        if first:
            m_scr[...] = jnp.full_like(m_scr, -3.0e38)
            l_scr[...] = jnp.zeros_like(l_scr)
            acc_scr[...] = jnp.zeros_like(acc_scr)
        else:
            m_scr[...] = kept[0][0]
            l_scr[...] = kept[1][0]
            acc_scr[...] = kept[2][0]

    q_cat = pair_rows(q_ref[...], half)
    m_old = m_scr[...]
    m_tiles = jnp.full((8, 2 * rows), -3.0e38, jnp.float32)
    for t in range(keys // tile):
        rng = slice(t * tile, (t + 1) * tile)
        s = dot_nt(k_ref[rng, :], q_cat)
        index = idx_ref[rng, :]
        s = s + jnp.concatenate(
            [bias_of(tab_ref[0, j : j + 1, :], index) for j in range(2)], axis=1
        )
        s_scr[rng, :] = s
        m_tiles = jnp.maximum(m_tiles, jnp.max(s.reshape(tile // 8, 8, 2 * rows), axis=0))
    m_new = jnp.maximum(m_old, jnp.max(m_tiles, axis=0, keepdims=True))
    fade = jnp.exp(m_old - m_new)
    sums = jnp.zeros((8, 2 * rows), jnp.float32)
    acc = acc_scr[...] * fade
    for t in range(keys // tile):
        rng = slice(t * tile, (t + 1) * tile)
        p = jnp.exp(s_scr[rng, :] - m_new)
        sums = sums + jnp.sum(p.reshape(tile // 8, 8, 2 * rows), axis=0)
        p_low = p.astype(jnp.bfloat16)
        p_ref[0, rng, :] = p_low[:, :rows]
        p_ref[1, rng, :] = p_low[:, rows:]
        acc = acc + dot_tn(v_ref[rng, :], p_low)
    acc_scr[...] = acc
    l_new = l_scr[...] * fade + jnp.sum(sums, axis=0, keepdims=True)
    l_scr[...] = l_new
    m_scr[...] = m_new
    m_out[0, 0] = m_new

    @pl.when(chunk == n_chunks - 1)
    def _():
        if first:
            outs[0][0], outs[1][0], outs[2][0] = m_new, l_new, acc
        else:
            outs[0][...] = jnp.transpose(pair_blocks(acc / l_new, half, rows))
            outs[1][0] = m_new + jnp.log(l_new)


def attend(made_own, made, index, table, chunk_keys, kept=None, tile=512):
    total, rows = index.shape
    width = made.shape[1] // 3
    heads = table.shape[0] * 2
    pairs = table.shape[0]
    wide = width // pairs
    n_chunks = total // chunk_keys
    first = kept is None
    line = (
        pl.BlockSpec((1, 1, 2 * rows), lambda p, c: (p, 0, 0)),
        jax.ShapeDtypeStruct((pairs, 1, 2 * rows), jnp.float32),
    )
    square = (
        pl.BlockSpec((1, wide, 2 * rows), lambda p, c: (p, 0, 0)),
        jax.ShapeDtypeStruct((pairs, wide, 2 * rows), jnp.float32),
    )
    result = (
        pl.BlockSpec((rows, wide), lambda p, c: (0, p)),
        jax.ShapeDtypeStruct((rows, width), jnp.float32),
    )
    outputs = [line, line, square] if first else [result, line]
    outputs += [
        (
            pl.BlockSpec((1, 1, 1, 2 * rows), lambda p, c: (p, c, 0, 0)),
            jax.ShapeDtypeStruct((pairs, n_chunks, 1, 2 * rows), jnp.float32),
        ),
        (
            pl.BlockSpec((2, chunk_keys, rows), lambda p, c: (p, c, 0)),
            jax.ShapeDtypeStruct((heads, total, rows), jnp.bfloat16),
        ),
    ]
    return pl.pallas_call(
        functools.partial(attend_kernel, tile, first),
        grid=(pairs, n_chunks),
        in_specs=[
            pl.BlockSpec((rows, wide), lambda p, c: (0, p)),
            pl.BlockSpec((chunk_keys, wide), lambda p, c: (c, pairs + p)),
            pl.BlockSpec((chunk_keys, wide), lambda p, c: (c, 2 * pairs + p)),
            pl.BlockSpec((chunk_keys, rows), lambda p, c: (c, 0)),
            pl.BlockSpec((1, 2, 128), lambda p, c: (p, 0, 0)),
        ]
        + ([] if first else [line[0], line[0], square[0]]),
        out_specs=[spec for spec, _ in outputs],
        out_shape=[shape for _, shape in outputs],
        scratch_shapes=[
            pltpu.VMEM((chunk_keys, 2 * rows), jnp.float32),
            pltpu.VMEM((1, 2 * rows), jnp.float32),
            pltpu.VMEM((1, 2 * rows), jnp.float32),
            pltpu.VMEM((wide, 2 * rows), jnp.float32),
        ],
        compiler_params=pltpu.CompilerParams(vmem_limit_bytes=VMEM_BYTES),
        cost_estimate=cost_of(0.008 * total),
        name="attend",
    )(made_own, made, made, index, table, *([] if first else kept))


def query_back_kernel(tile, *refs):
    groups, refs = (refs[0:4], refs[4:8]), refs[8:]
    da_ref, delta_ref, lse_ref, dq_ref, acc_scr = refs[:3] + refs[5:]
    chunk, n_chunks = pl.program_id(1), pl.num_programs(1)
    rows = da_ref.shape[0]
    half = da_ref.shape[1] // 2

    @pl.when(chunk == 0)
    def _():
        acc_scr[...] = jnp.zeros_like(acc_scr)

    delta = delta_ref[0]
    da_cat = pair_rows(da_ref[...], half)
    acc = acc_scr[...]
    for (p_ref, v_ref, k_ref, m_ref), ds_ref in zip(groups, refs[3:5]):
        factor = jnp.exp(m_ref[0, 0] - lse_ref[0])
        for t in range(v_ref.shape[0] // tile):
            rng = slice(t * tile, (t + 1) * tile)
            dp = dot_nt(v_ref[rng, :], da_cat)
            p = jnp.concatenate([p_ref[0, rng, :], p_ref[1, rng, :]], axis=1).astype(jnp.float32)
            ds = ((p * factor) * (dp - delta)).astype(jnp.bfloat16)
            ds_ref[0, rng, :] = ds[:, :rows]
            ds_ref[1, rng, :] = ds[:, rows:]
            acc = acc + dot_tn(k_ref[rng, :], ds)
    acc_scr[...] = acc

    @pl.when(chunk == n_chunks - 1)
    def _():
        dq_ref[...] = jnp.transpose(pair_blocks(acc, half, rows)).astype(jnp.bfloat16)


def query_back(probs, mades, lows, payload, delta, lse, chunk_keys, tile=512):
    heads, total, rows = probs[0].shape
    pairs = heads // 2
    width = mades[0].shape[1] // 3
    wide = width // pairs
    n_chunks = total // chunk_keys
    prob = pl.BlockSpec((2, chunk_keys, rows), lambda p, c: (p, c, 0))
    line = pl.BlockSpec((1, 1, 2 * rows), lambda p, c: (p, 0, 0))
    group = [
        prob,
        pl.BlockSpec((chunk_keys, wide), lambda p, c: (c, 2 * pairs + p)),
        pl.BlockSpec((chunk_keys, wide), lambda p, c: (c, pairs + p)),
        pl.BlockSpec((1, 1, 1, 2 * rows), lambda p, c: (p, c, 0, 0)),
    ]
    members = [(probs[j], mades[j], mades[j], lows[j]) for j in range(2)]
    return pl.pallas_call(
        functools.partial(query_back_kernel, tile),
        grid=(pairs, n_chunks),
        in_specs=group + group + [pl.BlockSpec((rows, wide), lambda p, c: (0, p)), line, line],
        out_specs=[prob, prob, pl.BlockSpec((rows, wide), lambda p, c: (0, p))],
        out_shape=[
            jax.ShapeDtypeStruct((heads, total, rows), jnp.bfloat16),
            jax.ShapeDtypeStruct((heads, total, rows), jnp.bfloat16),
            jax.ShapeDtypeStruct((rows, width), jnp.bfloat16),
        ],
        scratch_shapes=[pltpu.VMEM((wide, 2 * rows), jnp.float32)],
        input_output_aliases={0: 0, 4: 1},
        compiler_params=pltpu.CompilerParams(vmem_limit_bytes=VMEM_BYTES),
        cost_estimate=cost_of(0.01 * total),
        name="query_back",
    )(*members[0], *members[1], payload, delta, lse)


def key_back_kernel(count, *refs):
    n_pieces = 2 * PIECES
    grads, auxes, refs = refs[:n_pieces], refs[n_pieces : 2 * n_pieces], refs[2 * n_pieces :]
    q_refs, idx_refs, refs = refs[:2], refs[2:4], refs[4:]
    k_ref, v_ref, tab_ref, out_ref, dk_scr, dv_scr = refs
    pair, chunk, n_chunks = pl.program_id(0), pl.program_id(1), pl.num_programs(1)
    rows = k_ref.shape[0]
    wide = k_ref.shape[1]
    half = wide // 2

    @pl.when(chunk == 0)
    def _():
        dk_scr[...] = jnp.zeros_like(dk_scr)
        dv_scr[...] = jnp.zeros_like(dv_scr)

    lane = lax.broadcasted_iota(jnp.int32, (2 * rows, 128), 1)
    head = 2 * pair + (lax.broadcasted_iota(jnp.int32, (2 * rows, 128), 0) >= rows).astype(jnp.int32)
    early = (lane >= 2 * head) & (lane < 2 * head + 2)
    late = (lane >= 64 + 2 * head) & (lane < 64 + 2 * head + 2)
    take_lse = jnp.where(early, -1.0, 0.0).astype(jnp.bfloat16)
    take_delta = jnp.where(late, -1.0, 0.0).astype(jnp.bfloat16)
    k_cat = jnp.concatenate([pair_rows(k_ref[...], half), take_lse], axis=1)
    v_cat = jnp.concatenate([pair_rows(v_ref[...], half), take_delta], axis=1)
    dk, dv = dk_scr[...], dv_scr[...]
    for t in range(0, n_pieces, count):
        group, at = t // PIECES, t % PIECES
        da = jnp.concatenate([ref[...] for ref in grads[t : t + count]], axis=0)
        aux = jnp.concatenate([ref[...] for ref in auxes[t : t + count]], axis=0)
        q = q_refs[group][at : at + count].reshape(count * rows, wide)
        index = idx_refs[group][at : at + count].reshape(count * rows, rows)
        s = dot_nt(jnp.concatenate([q, aux], axis=1), k_cat)
        bias = jnp.concatenate(
            [bias_of(tab_ref[0, j : j + 1, :], index) for j in range(2)], axis=1
        )
        p = jnp.exp(s + bias)
        ds = p * dot_nt(jnp.concatenate([da, aux], axis=1), v_cat)
        dv = dv + dot_tn(da, p.astype(jnp.bfloat16))
        dk = dk + dot_tn(q, ds.astype(jnp.bfloat16))
    dk_scr[...] = dk
    dv_scr[...] = dv

    @pl.when(chunk == n_chunks - 1)
    def _():
        for j, acc in enumerate((dk, dv)):
            out_ref[j] = jnp.transpose(pair_blocks(acc, half, rows)).astype(jnp.bfloat16)


def key_back(pieces, mades, indexes, table, count=4):
    rows = indexes[0].shape[2]
    side, width = mades[0].shape[1], mades[0].shape[2] // 3
    pairs = table.shape[0]
    wide = width // pairs
    n_chunks = side // rows
    return pl.pallas_call(
        functools.partial(key_back_kernel, count),
        grid=(pairs, n_chunks),
        in_specs=[pl.BlockSpec((rows, wide), lambda p, c: (c, p))] * len(pieces)
        + [pl.BlockSpec((rows, 128), lambda p, c: (c, pairs))] * len(pieces)
        + [pl.BlockSpec((PIECES, rows, wide), lambda p, c: (0, c, p))] * 2
        + [pl.BlockSpec((PIECES, rows, rows), lambda p, c: (0, c, 0))] * 2
        + [
            pl.BlockSpec((None, rows, wide), lambda p, c: (0, 0, pairs + p)),
            pl.BlockSpec((None, rows, wide), lambda p, c: (0, 0, 2 * pairs + p)),
            pl.BlockSpec((1, 2, 128), lambda p, c: (p, 0, 0)),
        ],
        out_specs=pl.BlockSpec((2, rows, wide), lambda p, c: (0, 0, p)),
        out_shape=jax.ShapeDtypeStruct((2, rows, width), jnp.bfloat16),
        scratch_shapes=[pltpu.VMEM((wide, 2 * rows), jnp.float32)] * 2,
        compiler_params=pltpu.CompilerParams(vmem_limit_bytes=VMEM_MOST),
        cost_estimate=cost_of(15 * n_chunks),
        name="key_back",
    )(*pieces, *pieces, *mades, *indexes, mades[0], mades[0], table)


def norm_back(values, inverse, scale_gain, grad_normed):
    grad_gain = jnp.sum(grad_normed * values * inverse, axis=0)
    scaled = grad_normed * scale_gain
    grad_values = inverse * (
        scaled - values * inverse * inverse * jnp.mean(scaled * values, axis=1, keepdims=True)
    )
    return (grad_gain, grad_values)


def smooth_gate(values):
    return jax.nn.gelu(values, approximate=True)


def dot_f32(left, right):
    return jnp.dot(left, right, preferred_element_type=jnp.float32)


def swap_ctx(values, distance):
    size = lax.axis_size("ctx")
    return lax.ppermute(values, "ctx", [(i, i ^ distance) for i in range(size)])


def swap_pair(values):
    return lax.ppermute(values, "fsdp", [(0, 1), (1, 0)])


def in_order(where, mine, other, axis=0):
    return jnp.where(
        where == 0,
        jnp.concatenate([mine, other], axis=axis),
        jnp.concatenate([other, mine], axis=axis),
    )


def part_of(values, index, parts, axis):
    size = values.shape[axis] // parts
    return lax.dynamic_slice_in_dim(values, index * size, size, axis)


def tied(*members):
    return lax.optimization_barrier(members)


def gather_far(block):
    size = lax.axis_size("ctx")
    quarter = size // 4
    block = block[None]
    distance = 2 * 2
    while distance < quarter:
        block = jnp.concatenate([block, swap_ctx(block, distance)], axis=0)
        distance *= 2
    return [block] + [swap_ctx(block, quarter * j) for j in (1, 2, 3)]


def with_other_core(members):
    return members + [swap_ctx(piece, 1) for piece in members]


def scatter_sum(keep, send, tie):
    here, size = lax.axis_index("ctx"), lax.axis_size("ctx")
    f32, low, distance = jnp.float32, keep.dtype, 1
    got = swap_ctx(send, distance)
    while distance < size // 8:
        blocks = (keep.astype(f32) + got.astype(f32)).astype(low)
        distance *= 2
        mine = (here // distance) % 2
        send = part_of(blocks, 1 - mine, 2, 0)
        if distance == 2:
            send, tie = tied(send, tie)
        got = swap_ctx(send, distance)
        keep = part_of(blocks, mine, 2, 0)
    blocks = (keep.astype(f32) + got.astype(f32)).astype(low)
    distance *= 2
    mine = here // distance
    got = [swap_ctx(part_of(blocks, mine ^ j, 4, 0), distance * j) for j in (1, 2, 3)]
    added = part_of(blocks, mine, 4, 0).astype(f32) + sum(member.astype(f32) for member in got)
    return added.astype(low), tie


def gather_back(block):
    here, size = lax.axis_index("ctx"), lax.axis_size("ctx")
    distance = size // 4
    got = [swap_ctx(block, distance * j) for j in (1, 2, 3)]
    low_bit, high_bit = (here // distance) % 2, here // (2 * distance)
    blocks = in_order(high_bit, in_order(low_bit, block, got[0]), in_order(low_bit, got[1], got[2]))
    while distance > 2:
        distance //= 2
        blocks = in_order((here // distance) % 2, blocks, swap_ctx(blocks, distance))
    return blocks, swap_ctx(blocks, 1)


def sent_weights(*members):
    core = lax.axis_index("ctx") % 2
    return swap_pair(jnp.stack([part_of(member, core, 2, 0) for member in members]))


def shards(
    tokens,
    cotangent,
    lengths,
    dealing,
    gain_one,
    w_query,
    w_key,
    w_value,
    w_out,
    gain_two,
    w_in,
    w_ff,
    rel_table,
):
    bf16, f32 = jnp.bfloat16, jnp.float32
    size = lax.axis_size("ctx")
    pair = lax.axis_index("fsdp")
    rows, width = tokens.shape[1], tokens.shape[2]
    heads = rel_table.shape[1]
    head_size = width // heads
    pairs = heads // 2
    total = size * rows
    half_ff = w_ff.shape[0]
    half_width = w_query.shape[0]
    chunk_keys = min(total // 2, 1024)

    spot = jnp.concatenate(
        [jnp.stack([pair, lax.axis_index("ctx") % 2]).astype(jnp.int32), lengths[0]]
    )

    dealt = dealing[0]
    place_row = jnp.concatenate([dealt // 128, dealt % 128]).astype(bf16)
    place_rows = jnp.pad(place_row[None], ((0, 7), (0, width - 2 * rows)))
    far = gather_far(jnp.concatenate([tokens[0], place_rows], axis=0))
    *far, above = tied(*far, swap_ctx(far[0], 2))
    above = [above] + [swap_ctx(piece, 2) for piece in far[1:]]

    small = jnp.concatenate([gain_one, gain_two, rel_table.reshape(-1)])
    small = jnp.pad(small, (0, 1024 - small.shape[0])).reshape(8, 128)
    small_other = swap_pair(small)
    small_full = jnp.stack([small.reshape(-1), small_other.reshape(-1)])
    small_full = jnp.where(pair == 0, small_full, small_full[::-1])
    gain32_one = small_full[:, :half_width].reshape(width).astype(f32)
    gain32_two = small_full[:, half_width : 2 * half_width].reshape(width).astype(f32)
    full_table = small_full[:, 2 * half_width : 2 * half_width + rel_table.size]
    full_table = full_table.reshape(2 * rel_table.shape[0], heads).astype(f32)
    got_one = sent_weights(w_query, w_key, w_value)
    got_one, above[1] = tied(got_one, above[1])
    more_one = swap_ctx(got_one, 1)
    more_one, w_out, w_in, cotangent = tied(more_one, w_out, w_in, cotangent)
    mine_in, other_in = (part_of(w_in, index, 2, 1) for index in (pair, 1 - pair))
    got_two = sent_weights(w_out, other_in[:, :width], other_in[:, width:])
    grad_out = cotangent[0]
    grad_out_pair = jnp.concatenate([grad_out, swap_pair(grad_out)], axis=0)

    table_t = jnp.transpose(full_table)
    back_t = jnp.concatenate(
        [table_t[:, :1], table_t[:, 17:], table_t[:, :1], table_t[:, 1:16]], axis=1
    )
    tables = [
        jnp.pad(tab, ((0, 0), (0, 128 - BUCKETS)), constant_values=NEG).reshape(pairs, 2, 128)
        for tab in (table_t, back_t)
    ]
    fixed = (rows, total, lengths.shape[1])
    weights = (w_query, w_key, w_value, got_one, more_one)
    gain_row = gain32_one[None]
    made_one, index_one, w_qkv, normed_one = project(
        spot, with_other_core(far[:2] + above[:2]), gain_row, place_rows, weights, *fixed
    )
    above[2], above[3], made_one = tied(above[2], above[3], made_one)
    pieces = with_other_core(far[2:] + above[2:])
    mades, indexes = [made_one.reshape(total // 2, -1)], [index_one.reshape(total // 2, rows)]
    *kept, low_one, prob_one = attend(mades[0], mades[0], indexes[0], tables[0], chunk_keys)
    pieces, kept, got_two = tied(pieces, kept, got_two)
    more_two = swap_ctx(got_two, 1)
    made_two, index_two = project(spot, pieces, gain_row, place_rows, (w_qkv,), *fixed)
    mades.append(made_two.reshape(total // 2, -1))
    indexes.append(index_two.reshape(total // 2, rows))
    attn_f32, lse, low_two, prob_two = attend(
        mades[0], mades[1], indexes[1], tables[0], chunk_keys, kept
    )
    lows, probs = (low_one, low_two), (prob_one, prob_two)

    resid, normed_two, attn_b, full_out = close(
        spot, attn_f32, tokens[0], gain32_two[None], w_out, got_two, more_two
    )
    normed_pair = jnp.concatenate([normed_two, swap_pair(normed_two)], axis=0)
    core = lax.axis_index("ctx") % 2
    half_in = jnp.concatenate(
        [
            in_order(
                pair,
                mine_in[:, j * width : (j + 1) * width],
                in_order(core, got_two[1 + j], more_two[1 + j]),
            )
            for j in range(2)
        ],
        axis=1,
    )
    gate_pre = dot_f32(normed_pair, half_in)
    gate_val, gate_pull = jax.vjp(smooth_gate, gate_pre)
    active = gate_val.astype(bf16)
    grad_active = jnp.einsum("td,fd->tf", grad_out_pair, w_ff, preferred_element_type=f32)
    grad_pre = gate_pull(grad_active)[0].astype(bf16)
    grad_normed_part = jnp.einsum("tf,df->td", grad_pre, half_in, preferred_element_type=f32)
    payload, delta, grad_resid, grad_branch, grad_gain_two = branch(
        grad_normed_part,
        swap_pair(grad_normed_part[rows:].astype(bf16)),
        resid,
        grad_out,
        gain32_two[None],
        full_out,
        attn_f32,
        lse.reshape(heads, rows),
    )
    payload, active, normed_pair, grad_pre, attn_b = tied(
        payload, active, normed_pair, grad_pre, attn_b
    )

    def halves(values):
        other = swap_pair(part_of(values, 1 - pair, 2, 1))
        return jnp.concatenate([part_of(values, pair, 2, 1), other], axis=0)

    def both(values):
        return jnp.concatenate([values, swap_pair(values)], axis=0)

    def by_rows(left, right):
        return jnp.einsum("td,te->de", left, right, preferred_element_type=f32).astype(bf16)

    def blocks_of(values):
        return [
            values[:, j : j + width].reshape(size, values.shape[0] // size, width)
            for j in range(0, values.shape[1], width)
        ]

    tall = half_width // size
    tall_ff = half_ff // size
    grad_ff_part = by_rows(active, grad_out_pair)
    grad_in_part = by_rows(normed_pair, grad_pre)
    branch_other = swap_pair(
        jnp.concatenate([part_of(attn_b, 1 - pair, 2, 1), grad_branch], axis=1)
    )
    attn_pair = jnp.concatenate([part_of(attn_b, pair, 2, 1), branch_other[:, :half_width]], axis=0)
    branch_pair = jnp.concatenate([grad_branch, branch_other[:, half_width:]], axis=0)
    grad_out_part = by_rows(attn_pair, branch_pair)
    in_blocks = blocks_of(part_of(grad_in_part, pair, 2, 0)) + blocks_of(
        part_of(grad_in_part, 1 - pair, 2, 0)
    )
    ff_blocks = jnp.concatenate(
        blocks_of(grad_ff_part) + in_blocks + blocks_of(grad_out_part), axis=1
    )
    ff_tall = ff_blocks.shape[1]

    far = gather_far(payload)
    *far, above, ff_blocks, payload = tied(*far, swap_ctx(far[0], 2), ff_blocks, payload)
    above = [above] + [swap_ctx(piece, 2) for piece in far[1:]]
    above[1], payload = tied(above[1], payload)
    *grad_scores, grad_q = query_back(
        probs, mades, lows, payload, delta.reshape(pairs, 1, 2 * rows), lse, chunk_keys
    )
    above[1], above[2], above[3], grad_scores = tied(*above[1:], grad_scores)
    pieces = with_other_core(far[:2] + above[:2]) + with_other_core(far[2:] + above[2:])
    grad_tab = sum(
        jnp.einsum(
            "hkq,kqb->hb",
            member,
            (where[:, :, None] == jnp.arange(BUCKETS, dtype=jnp.int32)).astype(bf16),
            preferred_element_type=f32,
        )
        for member, where in zip(grad_scores, indexes)
    )
    ff_sum = lax.psum_scatter(
        ff_blocks.reshape(size * ff_tall, width), "ctx", scatter_dimension=0, tiled=True
    )
    pieces[-1], grad_tab = tied(pieces[-1], grad_tab)
    active, normed_one, grad_tab = tied(active, normed_one, grad_tab)
    grads_kv = key_back(
        ([payload] if size == 16 else [pieces[0].reshape(-1, width + 128)])
        + [piece.reshape(-1, width + 128) for piece in pieces[1:]],
        (made_one, made_two),
        (index_one, index_two),
        tables[1],
    )
    out_part = dot_f32(active, w_ff)
    out_other = swap_pair(out_part[rows:].astype(bf16))
    kv_other = swap_pair(grads_kv)
    normed_halves = halves(normed_one)
    q_other = swap_pair(grad_q)
    inputs = tokens[0].astype(f32)
    inv_one = lax.rsqrt(jnp.mean(inputs * inputs, axis=1, keepdims=True) + EPS)
    grad_normed_one = sum(
        jnp.einsum("te,de->td", member, w_qkv[j], preferred_element_type=f32)
        for j, member in enumerate((grad_q, grads_kv[0], grads_kv[1]))
    )
    grad_gain_one, grad_input_norm = norm_back(inputs, inv_one, gain32_one, grad_normed_one)
    grad_tokens = grad_resid + grad_input_norm
    kv_other, out_other = tied(kv_other, out_other)
    output = resid + out_part[:rows] + out_other.astype(f32)

    small_grads = jnp.concatenate(
        [
            grad_gain_one.reshape(2, half_width),
            grad_gain_two.reshape(2, half_width),
            jnp.transpose(grad_tab).reshape(2, rel_table.size),
        ],
        axis=1,
    )
    n_small = small_grads.shape[1]
    each = -(-n_small // size)
    small_grads = jnp.pad(small_grads, ((0, 0), (0, size * each - n_small)))
    small_pair = part_of(small_grads, pair, 2, 0) + swap_pair(part_of(small_grads, 1 - pair, 2, 0))
    small_blocks = jnp.pad(
        small_pair.astype(bf16).reshape(size, 1, each), ((0, 0), (0, 7), (0, width - each))
    )
    rights = [jnp.concatenate([grad_q, q_other])] + [
        jnp.concatenate([grads_kv[j], kv_other[j]]) for j in range(2)
    ]

    def core_blocks(side):
        left = part_of(normed_halves, side, 2, 1)
        made = [by_rows(left, right).reshape(size // 2, tall, width) for right in rights]
        return jnp.concatenate(made + [part_of(small_blocks, side, 2, 0)], axis=1)

    send = core_blocks(1 - spot[1])
    qkv_sum, ff_sum = scatter_sum(core_blocks(spot[1]), send, ff_sum)
    first_in, last_in = tall_ff, tall_ff + 4 * tall
    moved = swap_pair(ff_sum[tall_ff + 2 * tall : last_in])
    ff_sum = jnp.concatenate([ff_sum[: tall_ff + 2 * tall], moved, ff_sum[last_in:]], axis=0)
    ff_full = lax.all_gather(ff_sum, "ctx", axis=0, tiled=True).reshape(size, ff_tall, width)
    near_sum, far_sum = gather_back(qkv_sum)
    *grad_qkv, small_mine = unpack(spot, near_sum, far_sum, tall, 3)
    grad_qkv[0], ff_full = tied(grad_qkv[0], ff_full)
    grad_ff, grad_in, grad_out_w = spread(spot, ff_full, tall_ff, tall)
    grad_qkv = [member.reshape(half_width, width) for member in grad_qkv]
    small_mine = small_mine[:, 0, :each].reshape(-1)
    return (
        output.astype(bf16)[None],
        grad_tokens[None],
        small_mine[:half_width],
        *grad_qkv,
        grad_out_w.reshape(half_width, width),
        small_mine[half_width : 2 * half_width],
        grad_in.reshape(half_width, 4 * width),
        grad_ff.reshape(half_ff, width),
        small_mine[2 * half_width : n_small].reshape(rel_table.shape),
    )


def solution(mesh):
    spread = P("fsdp", "ctx", None)
    rows_of = P("fsdp", None)
    return jax.shard_map(
        shards,
        mesh=mesh,
        in_specs=(
            spread,
            spread,
            rows_of,
            P("fsdp", "ctx"),
            P("fsdp"),
            rows_of,
            rows_of,
            rows_of,
            rows_of,
            P("fsdp"),
            rows_of,
            rows_of,
            rows_of,
        ),
        out_specs=(
            spread,
            spread,
            P("fsdp"),
            rows_of,
            rows_of,
            rows_of,
            rows_of,
            P("fsdp"),
            rows_of,
            rows_of,
            rows_of,
        ),
        check_vma=False,
    )
```

```python
import functools
import jax
import jax.numpy as jnp
from jax import lax
from jax.experimental import pallas as pl
from jax.experimental.pallas import tpu as pltpu
from jax.sharding import PartitionSpec as P

BUCKETS = 32
PIECES = 8
EPS = 1e-06
NEG = -1000000000.0
THRESHOLDS = (1, 2, 3, 4, 5, 6, 7, 8, 12, 16, 23, 32, 46, 64, 91)
VMEM_BYTES = 32 * 1024 * 1024
VMEM_MOST = 63 * 1024 * 1024


def cost_of(micros):
    return pl.CostEstimate(flops=int(micros * 8e8), bytes_accessed=int(micros * 2.5e6), transcendentals=0)


def dot_nt(left, right):
    return lax.dot_general(left, right, (((1,), (1,)), ((), ())), preferred_element_type=jnp.float32)


def dot_tn(left, right):
    return lax.dot_general(left, right, (((0,), (0,)), ((), ())), preferred_element_type=jnp.float32)


def pair_rows(block, half):
    lane = lax.broadcasted_iota(jnp.int32, block.shape, 1)
    zero = jnp.zeros_like(block)
    return jnp.concatenate(
        [jnp.where(lane < half, block, zero), jnp.where(lane < half, zero, block)], axis=0
    )


def pair_blocks(acc, half, rows):
    return jnp.concatenate([acc[:half, :rows], acc[half:, rows:]], axis=0)


def bias_of(row, index):
    return jnp.take_along_axis(jnp.broadcast_to(row, index.shape), index, axis=1)


def fill_rows(out_ref, j, own, got, more, spot_ref):
    rows, part = own.shape[0], got.shape[0]
    other = (1 - spot_ref[0]) * rows
    out_ref[j, pl.ds(pl.multiple_of(spot_ref[0] * rows, 64), rows), :] = own
    out_ref[j, pl.ds(pl.multiple_of(other + spot_ref[1] * part, 64), part), :] = got
    out_ref[j, pl.ds(pl.multiple_of(other + (1 - spot_ref[1]) * part, 64), part), :] = more


def marks_of(places, total, seqs, spot_ref):
    rows = places.shape[1] // 2
    spots = places[:, :rows] * 128.0 + places[:, rows:]
    end = 0
    begin, segment = jnp.zeros_like(spots), jnp.zeros_like(spots)
    for j in range(seqs):
        end = end + spot_ref[2 + j]
        passed = spots >= end.astype(jnp.float32)
        begin = jnp.where(passed, end.astype(jnp.float32), begin)
        segment = jnp.where(passed, segment + 1.0, segment)
    return spots - begin + segment * (2.0 * total)


def project_kernel(count, total, seqs, first, spot_ref, *refs):
    pieces, refs = refs[:PIECES], refs[PIECES:]
    if first:
        gain_ref, place_ref, wq_ref, wk_ref, wv_ref, got_ref, more_ref = refs[:7]
        made_ref, idx_ref, full_ref, normed_ref, rows_scr, place_scr = refs[7:]
    else:
        gain_ref, place_ref, full_ref, made_ref, idx_ref, rows_scr, place_scr = refs
    width = gain_ref.shape[1]
    rows = idx_ref.shape[2]
    outer, inner = pl.program_id(0), pl.program_id(1)

    for group in range(PIECES // count):

        @pl.when(inner == group)
        def _():
            for j in range(count):
                held = pieces[group * count + j][0]
                rows_scr[j * rows : (j + 1) * rows, :] = held[:rows]
                place_scr[j : j + 1, :] = held[rows:].astype(jnp.float32)[:1, : 2 * rows]

    if first:

        @pl.when((outer == 0) & (inner == 0))
        def _():
            for j, ref in enumerate((wq_ref, wk_ref, wv_ref)):
                fill_rows(full_ref, j, ref[...], got_ref[j], more_ref[j], spot_ref)

    values = rows_scr[...].astype(jnp.float32)
    inverse = lax.rsqrt(jnp.mean(values * values, axis=1, keepdims=True) + EPS)
    normed = (values * inverse * gain_ref[...]).astype(jnp.bfloat16)
    shape = (count, rows, width)
    for j in range(3):
        made = jnp.dot(normed, full_ref[j], preferred_element_type=jnp.float32)
        made_ref[:, :, j * width : (j + 1) * width] = made.astype(jnp.bfloat16).reshape(shape)

    if first:

        @pl.when((outer == 0) & (inner == 0))
        def _():
            normed_ref[...] = normed[:rows]

    own = marks_of(place_ref[...].astype(jnp.float32)[:1, : 2 * rows], total, seqs, spot_ref)
    turned = jnp.transpose(marks_of(place_scr[...], total, seqs, spot_ref))
    for j in range(count):
        offset = turned[:, j : j + 1] - own
        distance = jnp.abs(offset)
        bucket = jnp.where(offset > 0, BUCKETS // 2, 0)
        for threshold in THRESHOLDS:
            bucket = bucket + (distance >= threshold).astype(jnp.int32)
        idx_ref[j] = jnp.where(distance >= total, BUCKETS, bucket)


def project(spot, pieces, gain, places, weights, rows, total, seqs, count=4):
    devices, tall, width = pieces[0].shape
    first = len(weights) > 1
    fixed = lambda rank: (lambda i, j, spot: (0,) * rank)
    moving = lambda i, j, spot: (j, i, 0)
    outputs = [
        (
            pl.BlockSpec((count, rows, 3 * width), moving),
            jax.ShapeDtypeStruct((PIECES, devices * rows, 3 * width), jnp.bfloat16),
        ),
        (
            pl.BlockSpec((count, rows, rows), moving),
            jax.ShapeDtypeStruct((PIECES, devices * rows, rows), jnp.int32),
        ),
    ]
    if first:
        outputs += [
            (
                pl.BlockSpec((3, width, width), fixed(3)),
                jax.ShapeDtypeStruct((3, width, width), jnp.bfloat16),
            ),
            (
                pl.BlockSpec((rows, width), fixed(2)),
                jax.ShapeDtypeStruct((rows, width), jnp.bfloat16),
            ),
        ]
    operands = (gain, places) + tuple(weights)
    return pl.pallas_call(
        functools.partial(project_kernel, count, total, seqs, first),
        grid_spec=pltpu.PrefetchScalarGridSpec(
            num_scalar_prefetch=1,
            grid=(devices, PIECES // count),
            in_specs=[pl.BlockSpec((1, tall, width), lambda i, j, spot: (i, 0, 0))] * PIECES
            + [pl.BlockSpec(member.shape, fixed(member.ndim)) for member in operands],
            out_specs=[spec for spec, _ in outputs],
            scratch_shapes=[
                pltpu.VMEM((count * rows, width), jnp.bfloat16),
                pltpu.VMEM((8, 2 * rows), jnp.float32),
            ],
        ),
        out_shape=[shape for _, shape in outputs],
        compiler_params=pltpu.CompilerParams(vmem_limit_bytes=VMEM_BYTES),
        cost_estimate=cost_of(0.7 * PIECES * devices),
        name="project",
    )(spot, *pieces, *operands)


def close_kernel(spot_ref, attn_ref, x_ref, gain_ref, w_ref, got_ref, more_ref, resid_ref, normed_ref, attn_b_ref, full_ref):
    fill_rows(full_ref, 0, w_ref[...], got_ref[0], more_ref[0], spot_ref)
    attn = attn_ref[...].astype(jnp.bfloat16)
    attn_b_ref[...] = attn
    resid = x_ref[...].astype(jnp.float32) + jnp.dot(
        attn, full_ref[0], preferred_element_type=jnp.float32
    )
    resid_ref[...] = resid
    inverse = lax.rsqrt(jnp.mean(resid * resid, axis=1, keepdims=True) + EPS)
    normed_ref[...] = (resid * inverse * gain_ref[...]).astype(jnp.bfloat16)


def close(spot, attn, tokens, gain, weight, got, more):
    rows, width = attn.shape
    held, part = weight.shape[0], got.shape[1]
    whole = lambda i, spot: (0, 0)
    first = lambda i, spot: (0, 0, 0)
    return pl.pallas_call(
        close_kernel,
        grid_spec=pltpu.PrefetchScalarGridSpec(
            num_scalar_prefetch=1,
            grid=(1,),
            in_specs=[
                pl.BlockSpec((rows, width), whole),
                pl.BlockSpec((rows, width), whole),
                pl.BlockSpec((1, width), whole),
                pl.BlockSpec((held, width), whole),
                pl.BlockSpec((1, part, width), first),
                pl.BlockSpec((1, part, width), first),
            ],
            out_specs=[
                pl.BlockSpec((rows, width), whole),
                pl.BlockSpec((rows, width), whole),
                pl.BlockSpec((rows, width), whole),
                pl.BlockSpec((1, width, width), first),
            ],
        ),
        out_shape=[
            jax.ShapeDtypeStruct((rows, width), jnp.float32),
            jax.ShapeDtypeStruct((rows, width), jnp.bfloat16),
            jax.ShapeDtypeStruct((rows, width), jnp.bfloat16),
            jax.ShapeDtypeStruct((1, width, width), jnp.bfloat16),
        ],
        compiler_params=pltpu.CompilerParams(vmem_limit_bytes=VMEM_BYTES),
        cost_estimate=cost_of(2),
        name="close",
    )(spot, attn, tokens, gain, weight, got, more)


def branch_kernel(part_ref, got_ref, resid_ref, cot_ref, gain_ref, out_ref, attn_ref, lse_ref, payload_ref, delta_ref, grad_ref, branch_ref, gain_grad_ref):
    f32, bf16 = jnp.float32, jnp.bfloat16
    rows, width = resid_ref.shape
    heads = lse_ref.shape[0]
    size = width // heads
    resid = resid_ref[...]
    normed_grad = part_ref[...] + got_ref[...].astype(f32)
    inverse = lax.rsqrt(jnp.mean(resid * resid, axis=1, keepdims=True) + EPS)
    gain_grad_ref[...] = jnp.sum(normed_grad * resid * inverse, axis=0, keepdims=True)
    scaled = normed_grad * gain_ref[...]
    mean = jnp.mean(scaled * resid, axis=1, keepdims=True)
    grad = cot_ref[...].astype(f32) + inverse * (scaled - resid * (inverse * inverse * mean))
    grad_ref[...] = grad
    branch = grad.astype(bf16)
    branch_ref[...] = branch
    attn_grad = dot_nt(branch, out_ref[0]).astype(bf16)
    payload_ref[:, :width] = attn_grad
    product = attn_grad.astype(f32) * attn_ref[...]
    high = product.astype(bf16)
    low = (product - high.astype(f32)).astype(bf16)

    def member(shape, at_row, at_col):
        row = lax.broadcasted_iota(jnp.int32, shape, 0)
        col = lax.broadcasted_iota(jnp.int32, shape, 1)
        return jnp.where(at_row(row) == at_col(col), 1.0, 0.0).astype(bf16)

    padded = 16
    by_head = member((padded, width), lambda r: r, lambda c: c // size)
    delta = (dot_nt(by_head, high) + dot_nt(by_head, low))[:heads]
    delta_ref[...] = delta
    col = lax.broadcasted_iota(jnp.int32, (rows, 128), 1)
    aux = jnp.zeros((rows, 128), f32)
    for first, values in ((0, lse_ref[...]), (64, delta)):
        values = jnp.concatenate([values, jnp.zeros((padded - heads, rows), f32)], axis=0)
        high = values.astype(bf16)
        low = (values - high.astype(f32)).astype(bf16)
        for odd, half in ((0, high), (1, low)):
            to_col = member((padded, 128), lambda r: first + odd + 2 * r, lambda c: c)
            aux = aux + dot_tn(half, to_col)
    payload_ref[:, width:] = aux.astype(bf16)


def branch(part, got, resid, cotangent, gain, full_out, attn, lse):
    rows, width = resid.shape
    heads = lse.shape[0]
    return pl.pallas_call(
        branch_kernel,
        grid=(1,),
        in_specs=[
            pl.BlockSpec((rows, width), lambda i: (0, 0)),
            pl.BlockSpec((rows, width), lambda i: (0, 0)),
            pl.BlockSpec((rows, width), lambda i: (0, 0)),
            pl.BlockSpec((rows, width), lambda i: (0, 0)),
            pl.BlockSpec((1, width), lambda i: (0, 0)),
            pl.BlockSpec((1, width, width), lambda i: (0, 0, 0)),
            pl.BlockSpec((rows, width), lambda i: (0, 0)),
            pl.BlockSpec((heads, rows), lambda i: (0, 0)),
        ],
        out_specs=[
            pl.BlockSpec((rows, width + 128), lambda i: (0, 0)),
            pl.BlockSpec((heads, rows), lambda i: (0, 0)),
            pl.BlockSpec((rows, width), lambda i: (0, 0)),
            pl.BlockSpec((rows, width), lambda i: (0, 0)),
            pl.BlockSpec((1, width), lambda i: (0, 0)),
        ],
        out_shape=[
            jax.ShapeDtypeStruct((rows, width + 128), jnp.bfloat16),
            jax.ShapeDtypeStruct((heads, rows), jnp.float32),
            jax.ShapeDtypeStruct((rows, width), jnp.float32),
            jax.ShapeDtypeStruct((rows, width), jnp.bfloat16),
            jax.ShapeDtypeStruct((1, width), jnp.float32),
        ],
        compiler_params=pltpu.CompilerParams(vmem_limit_bytes=VMEM_BYTES),
        cost_estimate=cost_of(3),
        name="branch",
    )(part, got, resid, cotangent, gain, full_out, attn, lse)


def unpack_kernel(tall, spot_ref, near_ref, far_ref, *out_refs):
    values = jnp.where(pl.program_id(0) == 0, near_ref[...], far_ref[...]).astype(jnp.float32)
    for j, ref in enumerate(out_refs[:-1]):
        ref[...] = values[:, j * tall : (j + 1) * tall, :]
    out_refs[-1][...] = values[:, (len(out_refs) - 1) * tall :, :128]


def unpack(spot, near, far, tall, outputs):
    half, high, width = near.shape
    step = min(4, half)
    steps = half // step

    def place(j, i, spot):
        return (jnp.bitwise_xor(j, spot[1]) * steps + i, 0, 0)

    return pl.pallas_call(
        functools.partial(unpack_kernel, tall),
        grid_spec=pltpu.PrefetchScalarGridSpec(
            num_scalar_prefetch=1,
            grid=(2, steps),
            in_specs=[
                pl.BlockSpec(
                    (step, high, width), lambda j, i, spot: (jnp.where(j == 0, i, steps - 1), 0, 0)
                ),
                pl.BlockSpec(
                    (step, high, width), lambda j, i, spot: (jnp.where(j == 0, 0, i), 0, 0)
                ),
            ],
            out_specs=[pl.BlockSpec((step, tall, width), place)] * outputs
            + [pl.BlockSpec((step, high - outputs * tall, 128), place)],
        ),
        out_shape=[jax.ShapeDtypeStruct((2 * half, tall, width), jnp.float32)] * outputs
        + [jax.ShapeDtypeStruct((2 * half, high - outputs * tall, 128), jnp.float32)],
        compiler_params=pltpu.CompilerParams(vmem_limit_bytes=VMEM_BYTES),
        cost_estimate=cost_of(4),
        name="unpack",
    )(spot, near, far)


def spread_kernel(tall_ff, tall, spot_ref, full_ref, ff_ref, in_ref, out_ref):
    width = out_ref.shape[2]
    values = full_ref[...].astype(jnp.float32)
    ff_ref[...] = values[:, :tall_ff, :]
    parts = [values[:, tall_ff + j * tall : tall_ff + (j + 1) * tall, :] for j in range(5)]
    for j in range(2):
        in_ref[:, :, j * width : (j + 1) * width] = jnp.where(
            spot_ref[0] == 0, parts[j], parts[2 + j]
        )
        in_ref[:, :, (2 + j) * width : (3 + j) * width] = jnp.where(
            spot_ref[0] == 0, parts[2 + j], parts[j]
        )
    out_ref[...] = parts[4]


def spread(spot, full, tall_ff, tall):
    size, high, width = full.shape
    step = 4
    return pl.pallas_call(
        functools.partial(spread_kernel, tall_ff, tall),
        grid_spec=pltpu.PrefetchScalarGridSpec(
            num_scalar_prefetch=1,
            grid=(size // step,),
            in_specs=[pl.BlockSpec((step, high, width), lambda i, spot: (i, 0, 0))],
            out_specs=[
                pl.BlockSpec((step, tall_ff, width), lambda i, spot: (i, 0, 0)),
                pl.BlockSpec((step, tall, 4 * width), lambda i, spot: (i, 0, 0)),
                pl.BlockSpec((step, tall, width), lambda i, spot: (i, 0, 0)),
            ],
        ),
        out_shape=[
            jax.ShapeDtypeStruct((size, tall_ff, width), jnp.float32),
            jax.ShapeDtypeStruct((size, tall, 4 * width), jnp.float32),
            jax.ShapeDtypeStruct((size, tall, width), jnp.float32),
        ],
        compiler_params=pltpu.CompilerParams(vmem_limit_bytes=VMEM_BYTES),
        cost_estimate=cost_of(6),
        name="spread",
    )(spot, full)


def attend_kernel(tile, first, q_ref, k_ref, v_ref, idx_ref, tab_ref, *refs):
    if first:
        outs, m_out, p_ref, s_scr, m_scr, l_scr, acc_scr = refs[:3], *refs[3:]
    else:
        kept, outs, m_out, p_ref, s_scr, m_scr, l_scr, acc_scr = refs[:3], refs[3:5], *refs[5:]
    chunk, n_chunks = pl.program_id(1), pl.num_programs(1)
    rows = q_ref.shape[0]
    half = q_ref.shape[1] // 2
    keys = k_ref.shape[0]

    @pl.when(chunk == 0)
    def _():
        if first:
            m_scr[...] = jnp.full_like(m_scr, -3.0e38)
            l_scr[...] = jnp.zeros_like(l_scr)
            acc_scr[...] = jnp.zeros_like(acc_scr)
        else:
            m_scr[...] = kept[0][0]
            l_scr[...] = kept[1][0]
            acc_scr[...] = kept[2][0]

    q_cat = pair_rows(q_ref[...], half)
    m_old = m_scr[...]
    m_tiles = jnp.full((8, 2 * rows), -3.0e38, jnp.float32)
    for t in range(keys // tile):
        rng = slice(t * tile, (t + 1) * tile)
        s = dot_nt(k_ref[rng, :], q_cat)
        index = idx_ref[rng, :]
        s = s + jnp.concatenate(
            [bias_of(tab_ref[0, j : j + 1, :], index) for j in range(2)], axis=1
        )
        s_scr[rng, :] = s
        m_tiles = jnp.maximum(m_tiles, jnp.max(s.reshape(tile // 8, 8, 2 * rows), axis=0))
    m_new = jnp.maximum(m_old, jnp.max(m_tiles, axis=0, keepdims=True))
    fade = jnp.exp(m_old - m_new)
    sums = jnp.zeros((8, 2 * rows), jnp.float32)
    acc = acc_scr[...] * fade
    for t in range(keys // tile):
        rng = slice(t * tile, (t + 1) * tile)
        p = jnp.exp(s_scr[rng, :] - m_new)
        sums = sums + jnp.sum(p.reshape(tile // 8, 8, 2 * rows), axis=0)
        p_low = p.astype(jnp.bfloat16)
        p_ref[0, rng, :] = p_low[:, :rows]
        p_ref[1, rng, :] = p_low[:, rows:]
        acc = acc + dot_tn(v_ref[rng, :], p_low)
    acc_scr[...] = acc
    l_new = l_scr[...] * fade + jnp.sum(sums, axis=0, keepdims=True)
    l_scr[...] = l_new
    m_scr[...] = m_new
    m_out[0, 0] = m_new

    @pl.when(chunk == n_chunks - 1)
    def _():
        if first:
            outs[0][0], outs[1][0], outs[2][0] = m_new, l_new, acc
        else:
            outs[0][...] = jnp.transpose(pair_blocks(acc / l_new, half, rows))
            outs[1][0] = m_new + jnp.log(l_new)


def attend(made_own, made, index, table, chunk_keys, kept=None, tile=512):
    total, rows = index.shape
    width = made.shape[1] // 3
    heads = table.shape[0] * 2
    pairs = table.shape[0]
    wide = width // pairs
    n_chunks = total // chunk_keys
    first = kept is None
    line = (
        pl.BlockSpec((1, 1, 2 * rows), lambda p, c: (p, 0, 0)),
        jax.ShapeDtypeStruct((pairs, 1, 2 * rows), jnp.float32),
    )
    square = (
        pl.BlockSpec((1, wide, 2 * rows), lambda p, c: (p, 0, 0)),
        jax.ShapeDtypeStruct((pairs, wide, 2 * rows), jnp.float32),
    )
    result = (
        pl.BlockSpec((rows, wide), lambda p, c: (0, p)),
        jax.ShapeDtypeStruct((rows, width), jnp.float32),
    )
    outputs = [line, line, square] if first else [result, line]
    outputs += [
        (
            pl.BlockSpec((1, 1, 1, 2 * rows), lambda p, c: (p, c, 0, 0)),
            jax.ShapeDtypeStruct((pairs, n_chunks, 1, 2 * rows), jnp.float32),
        ),
        (
            pl.BlockSpec((2, chunk_keys, rows), lambda p, c: (p, c, 0)),
            jax.ShapeDtypeStruct((heads, total, rows), jnp.bfloat16),
        ),
    ]
    return pl.pallas_call(
        functools.partial(attend_kernel, tile, first),
        grid=(pairs, n_chunks),
        in_specs=[
            pl.BlockSpec((rows, wide), lambda p, c: (0, p)),
            pl.BlockSpec((chunk_keys, wide), lambda p, c: (c, pairs + p)),
            pl.BlockSpec((chunk_keys, wide), lambda p, c: (c, 2 * pairs + p)),
            pl.BlockSpec((chunk_keys, rows), lambda p, c: (c, 0)),
            pl.BlockSpec((1, 2, 128), lambda p, c: (p, 0, 0)),
        ]
        + ([] if first else [line[0], line[0], square[0]]),
        out_specs=[spec for spec, _ in outputs],
        out_shape=[shape for _, shape in outputs],
        scratch_shapes=[
            pltpu.VMEM((chunk_keys, 2 * rows), jnp.float32),
            pltpu.VMEM((1, 2 * rows), jnp.float32),
            pltpu.VMEM((1, 2 * rows), jnp.float32),
            pltpu.VMEM((wide, 2 * rows), jnp.float32),
        ],
        compiler_params=pltpu.CompilerParams(vmem_limit_bytes=VMEM_BYTES),
        cost_estimate=cost_of(0.008 * total),
        name="attend",
    )(made_own, made, made, index, table, *([] if first else kept))


def query_back_kernel(tile, *refs):
    groups, refs = (refs[0:4], refs[4:8]), refs[8:]
    da_ref, delta_ref, lse_ref, dq_ref, acc_scr = refs[:3] + refs[5:]
    chunk, n_chunks = pl.program_id(1), pl.num_programs(1)
    rows = da_ref.shape[0]
    half = da_ref.shape[1] // 2

    @pl.when(chunk == 0)
    def _():
        acc_scr[...] = jnp.zeros_like(acc_scr)

    delta = delta_ref[0]
    da_cat = pair_rows(da_ref[...], half)
    acc = acc_scr[...]
    for (p_ref, v_ref, k_ref, m_ref), ds_ref in zip(groups, refs[3:5]):
        factor = jnp.exp(m_ref[0, 0] - lse_ref[0])
        for t in range(v_ref.shape[0] // tile):
            rng = slice(t * tile, (t + 1) * tile)
            dp = dot_nt(v_ref[rng, :], da_cat)
            p = jnp.concatenate([p_ref[0, rng, :], p_ref[1, rng, :]], axis=1).astype(jnp.float32)
            ds = ((p * factor) * (dp - delta)).astype(jnp.bfloat16)
            ds_ref[0, rng, :] = ds[:, :rows]
            ds_ref[1, rng, :] = ds[:, rows:]
            acc = acc + dot_tn(k_ref[rng, :], ds)
    acc_scr[...] = acc

    @pl.when(chunk == n_chunks - 1)
    def _():
        dq_ref[...] = jnp.transpose(pair_blocks(acc, half, rows)).astype(jnp.bfloat16)


def query_back(probs, mades, lows, payload, delta, lse, chunk_keys, tile=512):
    heads, total, rows = probs[0].shape
    pairs = heads // 2
    width = mades[0].shape[1] // 3
    wide = width // pairs
    n_chunks = total // chunk_keys
    prob = pl.BlockSpec((2, chunk_keys, rows), lambda p, c: (p, c, 0))
    line = pl.BlockSpec((1, 1, 2 * rows), lambda p, c: (p, 0, 0))
    group = [
        prob,
        pl.BlockSpec((chunk_keys, wide), lambda p, c: (c, 2 * pairs + p)),
        pl.BlockSpec((chunk_keys, wide), lambda p, c: (c, pairs + p)),
        pl.BlockSpec((1, 1, 1, 2 * rows), lambda p, c: (p, c, 0, 0)),
    ]
    members = [(probs[j], mades[j], mades[j], lows[j]) for j in range(2)]
    return pl.pallas_call(
        functools.partial(query_back_kernel, tile),
        grid=(pairs, n_chunks),
        in_specs=group + group + [pl.BlockSpec((rows, wide), lambda p, c: (0, p)), line, line],
        out_specs=[prob, prob, pl.BlockSpec((rows, wide), lambda p, c: (0, p))],
        out_shape=[
            jax.ShapeDtypeStruct((heads, total, rows), jnp.bfloat16),
            jax.ShapeDtypeStruct((heads, total, rows), jnp.bfloat16),
            jax.ShapeDtypeStruct((rows, width), jnp.bfloat16),
        ],
        scratch_shapes=[pltpu.VMEM((wide, 2 * rows), jnp.float32)],
        input_output_aliases={0: 0, 4: 1},
        compiler_params=pltpu.CompilerParams(vmem_limit_bytes=VMEM_BYTES),
        cost_estimate=cost_of(0.01 * total),
        name="query_back",
    )(*members[0], *members[1], payload, delta, lse)


def key_back_kernel(count, *refs):
    n_pieces = 2 * PIECES
    grads, auxes, refs = refs[:n_pieces], refs[n_pieces : 2 * n_pieces], refs[2 * n_pieces :]
    q_refs, idx_refs, refs = refs[:2], refs[2:4], refs[4:]
    k_ref, v_ref, tab_ref, out_ref, dk_scr, dv_scr = refs
    pair, chunk, n_chunks = pl.program_id(0), pl.program_id(1), pl.num_programs(1)
    rows = k_ref.shape[0]
    wide = k_ref.shape[1]
    half = wide // 2

    @pl.when(chunk == 0)
    def _():
        dk_scr[...] = jnp.zeros_like(dk_scr)
        dv_scr[...] = jnp.zeros_like(dv_scr)

    lane = lax.broadcasted_iota(jnp.int32, (2 * rows, 128), 1)
    head = 2 * pair + (lax.broadcasted_iota(jnp.int32, (2 * rows, 128), 0) >= rows).astype(jnp.int32)
    early = (lane >= 2 * head) & (lane < 2 * head + 2)
    late = (lane >= 64 + 2 * head) & (lane < 64 + 2 * head + 2)
    take_lse = jnp.where(early, -1.0, 0.0).astype(jnp.bfloat16)
    take_delta = jnp.where(late, -1.0, 0.0).astype(jnp.bfloat16)
    k_cat = jnp.concatenate([pair_rows(k_ref[...], half), take_lse], axis=1)
    v_cat = jnp.concatenate([pair_rows(v_ref[...], half), take_delta], axis=1)
    dk, dv = dk_scr[...], dv_scr[...]
    for t in range(0, n_pieces, count):
        group, at = t // PIECES, t % PIECES
        da = jnp.concatenate([ref[...] for ref in grads[t : t + count]], axis=0)
        aux = jnp.concatenate([ref[...] for ref in auxes[t : t + count]], axis=0)
        q = q_refs[group][at : at + count].reshape(count * rows, wide)
        index = idx_refs[group][at : at + count].reshape(count * rows, rows)
        s = dot_nt(jnp.concatenate([q, aux], axis=1), k_cat)
        bias = jnp.concatenate(
            [bias_of(tab_ref[0, j : j + 1, :], index) for j in range(2)], axis=1
        )
        p = jnp.exp(s + bias)
        ds = p * dot_nt(jnp.concatenate([da, aux], axis=1), v_cat)
        dv = dv + dot_tn(da, p.astype(jnp.bfloat16))
        dk = dk + dot_tn(q, ds.astype(jnp.bfloat16))
    dk_scr[...] = dk
    dv_scr[...] = dv

    @pl.when(chunk == n_chunks - 1)
    def _():
        for j, acc in enumerate((dk, dv)):
            out_ref[j] = jnp.transpose(pair_blocks(acc, half, rows)).astype(jnp.bfloat16)


def key_back(pieces, mades, indexes, table, count=4):
    rows = indexes[0].shape[2]
    side, width = mades[0].shape[1], mades[0].shape[2] // 3
    pairs = table.shape[0]
    wide = width // pairs
    n_chunks = side // rows
    return pl.pallas_call(
        functools.partial(key_back_kernel, count),
        grid=(pairs, n_chunks),
        in_specs=[pl.BlockSpec((rows, wide), lambda p, c: (c, p))] * len(pieces)
        + [pl.BlockSpec((rows, 128), lambda p, c: (c, pairs))] * len(pieces)
        + [pl.BlockSpec((PIECES, rows, wide), lambda p, c: (0, c, p))] * 2
        + [pl.BlockSpec((PIECES, rows, rows), lambda p, c: (0, c, 0))] * 2
        + [
            pl.BlockSpec((None, rows, wide), lambda p, c: (0, 0, pairs + p)),
            pl.BlockSpec((None, rows, wide), lambda p, c: (0, 0, 2 * pairs + p)),
            pl.BlockSpec((1, 2, 128), lambda p, c: (p, 0, 0)),
        ],
        out_specs=pl.BlockSpec((2, rows, wide), lambda p, c: (0, 0, p)),
        out_shape=jax.ShapeDtypeStruct((2, rows, width), jnp.bfloat16),
        scratch_shapes=[pltpu.VMEM((wide, 2 * rows), jnp.float32)] * 2,
        compiler_params=pltpu.CompilerParams(vmem_limit_bytes=VMEM_MOST),
        cost_estimate=cost_of(15 * n_chunks),
        name="key_back",
    )(*pieces, *pieces, *mades, *indexes, mades[0], mades[0], table)


def norm_back(values, inverse, scale_gain, grad_normed):
    grad_gain = jnp.sum(grad_normed * values * inverse, axis=0)
    scaled = grad_normed * scale_gain
    grad_values = inverse * (
        scaled - values * inverse * inverse * jnp.mean(scaled * values, axis=1, keepdims=True)
    )
    return (grad_gain, grad_values)


def smooth_gate(values):
    return jax.nn.gelu(values, approximate=True)


def dot_f32(left, right):
    return jnp.dot(left, right, preferred_element_type=jnp.float32)


def swap_ctx(values, distance):
    size = lax.axis_size("ctx")
    return lax.ppermute(values, "ctx", [(i, i ^ distance) for i in range(size)])


def swap_pair(values):
    return lax.ppermute(values, "fsdp", [(0, 1), (1, 0)])


def in_order(where, mine, other, axis=0):
    return jnp.where(
        where == 0,
        jnp.concatenate([mine, other], axis=axis),
        jnp.concatenate([other, mine], axis=axis),
    )


def part_of(values, index, parts, axis):
    size = values.shape[axis] // parts
    return lax.dynamic_slice_in_dim(values, index * size, size, axis)


def tied(*members):
    return lax.optimization_barrier(members)


def gather_far(block):
    size = lax.axis_size("ctx")
    quarter = size // 4
    block = block[None]
    distance = 2 * 2
    while distance < quarter:
        block = jnp.concatenate([block, swap_ctx(block, distance)], axis=0)
        distance *= 2
    return [block] + [swap_ctx(block, quarter * j) for j in (1, 2, 3)]


def with_other_core(members):
    return members + [swap_ctx(piece, 1) for piece in members]


def scatter_sum(keep, send, tie):
    here, size = lax.axis_index("ctx"), lax.axis_size("ctx")
    f32, low, distance = jnp.float32, keep.dtype, 1
    got = swap_ctx(send, distance)
    while distance < size // 8:
        blocks = (keep.astype(f32) + got.astype(f32)).astype(low)
        distance *= 2
        mine = (here // distance) % 2
        send = part_of(blocks, 1 - mine, 2, 0)
        if distance == 2:
            send, tie = tied(send, tie)
        got = swap_ctx(send, distance)
        keep = part_of(blocks, mine, 2, 0)
    blocks = (keep.astype(f32) + got.astype(f32)).astype(low)
    distance *= 2
    mine = here // distance
    got = [swap_ctx(part_of(blocks, mine ^ j, 4, 0), distance * j) for j in (1, 2, 3)]
    added = part_of(blocks, mine, 4, 0).astype(f32) + sum(member.astype(f32) for member in got)
    return added.astype(low), tie


def gather_back(block):
    here, size = lax.axis_index("ctx"), lax.axis_size("ctx")
    distance = size // 4
    got = [swap_ctx(block, distance * j) for j in (1, 2, 3)]
    low_bit, high_bit = (here // distance) % 2, here // (2 * distance)
    blocks = in_order(high_bit, in_order(low_bit, block, got[0]), in_order(low_bit, got[1], got[2]))
    while distance > 2:
        distance //= 2
        blocks = in_order((here // distance) % 2, blocks, swap_ctx(blocks, distance))
    return blocks, swap_ctx(blocks, 1)


def sent_weights(*members):
    core = lax.axis_index("ctx") % 2
    return swap_pair(jnp.stack([part_of(member, core, 2, 0) for member in members]))


def shards(
    tokens,
    cotangent,
    lengths,
    dealing,
    gain_one,
    w_query,
    w_key,
    w_value,
    w_out,
    gain_two,
    w_in,
    w_ff,
    rel_table,
):
    bf16, f32 = jnp.bfloat16, jnp.float32
    size = lax.axis_size("ctx")
    pair = lax.axis_index("fsdp")
    rows, width = tokens.shape[1], tokens.shape[2]
    heads = rel_table.shape[1]
    head_size = width // heads
    pairs = heads // 2
    total = size * rows
    half_ff = w_ff.shape[0]
    half_width = w_query.shape[0]
    chunk_keys = min(total // 2, 1024)

    spot = jnp.concatenate(
        [jnp.stack([pair, lax.axis_index("ctx") % 2]).astype(jnp.int32), lengths[0]]
    )

    dealt = dealing[0]
    place_row = jnp.concatenate([dealt // 128, dealt % 128]).astype(bf16)
    place_rows = jnp.pad(place_row[None], ((0, 7), (0, width - 2 * rows)))
    far = gather_far(jnp.concatenate([tokens[0], place_rows], axis=0))
    *far, above = tied(*far, swap_ctx(far[0], 2))
    above = [above] + [swap_ctx(piece, 2) for piece in far[1:]]

    small = jnp.concatenate([gain_one, gain_two, rel_table.reshape(-1)])
    small = jnp.pad(small, (0, 1024 - small.shape[0])).reshape(8, 128)
    small_other = swap_pair(small)
    small_full = jnp.stack([small.reshape(-1), small_other.reshape(-1)])
    small_full = jnp.where(pair == 0, small_full, small_full[::-1])
    gain32_one = small_full[:, :half_width].reshape(width).astype(f32)
    gain32_two = small_full[:, half_width : 2 * half_width].reshape(width).astype(f32)
    full_table = small_full[:, 2 * half_width : 2 * half_width + rel_table.size]
    full_table = full_table.reshape(2 * rel_table.shape[0], heads).astype(f32)
    got_one = sent_weights(w_query, w_key, w_value)
    got_one, above[1] = tied(got_one, above[1])
    more_one = swap_ctx(got_one, 1)
    more_one, w_out, w_in, cotangent = tied(more_one, w_out, w_in, cotangent)
    mine_in, other_in = (part_of(w_in, index, 2, 1) for index in (pair, 1 - pair))
    got_two = sent_weights(w_out, other_in[:, :width], other_in[:, width:])
    grad_out = cotangent[0]
    grad_out_pair = jnp.concatenate([grad_out, swap_pair(grad_out)], axis=0)

    table_t = jnp.transpose(full_table)
    back_t = jnp.concatenate(
        [table_t[:, :1], table_t[:, 17:], table_t[:, :1], table_t[:, 1:16]], axis=1
    )
    tables = [
        jnp.pad(tab, ((0, 0), (0, 128 - BUCKETS)), constant_values=NEG).reshape(pairs, 2, 128)
        for tab in (table_t, back_t)
    ]
    fixed = (rows, total, lengths.shape[1])
    weights = (w_query, w_key, w_value, got_one, more_one)
    gain_row = gain32_one[None]
    made_one, index_one, w_qkv, normed_one = project(
        spot, with_other_core(far[:2] + above[:2]), gain_row, place_rows, weights, *fixed
    )
    above[2], above[3], made_one = tied(above[2], above[3], made_one)
    pieces = with_other_core(far[2:] + above[2:])
    mades, indexes = [made_one.reshape(total // 2, -1)], [index_one.reshape(total // 2, rows)]
    *kept, low_one, prob_one = attend(mades[0], mades[0], indexes[0], tables[0], chunk_keys)
    pieces, kept, got_two = tied(pieces, kept, got_two)
    more_two = swap_ctx(got_two, 1)
    made_two, index_two = project(spot, pieces, gain_row, place_rows, (w_qkv,), *fixed)
    mades.append(made_two.reshape(total // 2, -1))
    indexes.append(index_two.reshape(total // 2, rows))
    attn_f32, lse, low_two, prob_two = attend(
        mades[0], mades[1], indexes[1], tables[0], chunk_keys, kept
    )
    lows, probs = (low_one, low_two), (prob_one, prob_two)

    resid, normed_two, attn_b, full_out = close(
        spot, attn_f32, tokens[0], gain32_two[None], w_out, got_two, more_two
    )
    normed_pair = jnp.concatenate([normed_two, swap_pair(normed_two)], axis=0)
    core = lax.axis_index("ctx") % 2
    half_in = jnp.concatenate(
        [
            in_order(
                pair,
                mine_in[:, j * width : (j + 1) * width],
                in_order(core, got_two[1 + j], more_two[1 + j]),
            )
            for j in range(2)
        ],
        axis=1,
    )
    gate_pre = dot_f32(normed_pair, half_in)
    gate_val, gate_pull = jax.vjp(smooth_gate, gate_pre)
    active = gate_val.astype(bf16)
    grad_active = jnp.einsum("td,fd->tf", grad_out_pair, w_ff, preferred_element_type=f32)
    grad_pre = gate_pull(grad_active)[0].astype(bf16)
    grad_normed_part = jnp.einsum("tf,df->td", grad_pre, half_in, preferred_element_type=f32)
    payload, delta, grad_resid, grad_branch, grad_gain_two = branch(
        grad_normed_part,
        swap_pair(grad_normed_part[rows:].astype(bf16)),
        resid,
        grad_out,
        gain32_two[None],
        full_out,
        attn_f32,
        lse.reshape(heads, rows),
    )
    payload, active, normed_pair, grad_pre, attn_b = tied(
        payload, active, normed_pair, grad_pre, attn_b
    )

    def halves(values):
        other = swap_pair(part_of(values, 1 - pair, 2, 1))
        return jnp.concatenate([part_of(values, pair, 2, 1), other], axis=0)

    def both(values):
        return jnp.concatenate([values, swap_pair(values)], axis=0)

    def by_rows(left, right):
        return jnp.einsum("td,te->de", left, right, preferred_element_type=f32).astype(bf16)

    def blocks_of(values):
        return [
            values[:, j : j + width].reshape(size, values.shape[0] // size, width)
            for j in range(0, values.shape[1], width)
        ]

    tall = half_width // size
    tall_ff = half_ff // size
    grad_ff_part = by_rows(active, grad_out_pair)
    grad_in_part = by_rows(normed_pair, grad_pre)
    branch_other = swap_pair(
        jnp.concatenate([part_of(attn_b, 1 - pair, 2, 1), grad_branch], axis=1)
    )
    attn_pair = jnp.concatenate([part_of(attn_b, pair, 2, 1), branch_other[:, :half_width]], axis=0)
    branch_pair = jnp.concatenate([grad_branch, branch_other[:, half_width:]], axis=0)
    grad_out_part = by_rows(attn_pair, branch_pair)
    in_blocks = blocks_of(part_of(grad_in_part, pair, 2, 0)) + blocks_of(
        part_of(grad_in_part, 1 - pair, 2, 0)
    )
    ff_blocks = jnp.concatenate(
        blocks_of(grad_ff_part) + in_blocks + blocks_of(grad_out_part), axis=1
    )
    ff_tall = ff_blocks.shape[1]

    far = gather_far(payload)
    *far, above, ff_blocks, payload = tied(*far, swap_ctx(far[0], 2), ff_blocks, payload)
    above = [above] + [swap_ctx(piece, 2) for piece in far[1:]]
    above[1], payload = tied(above[1], payload)
    *grad_scores, grad_q = query_back(
        probs, mades, lows, payload, delta.reshape(pairs, 1, 2 * rows), lse, chunk_keys
    )
    above[1], above[2], above[3], grad_scores = tied(*above[1:], grad_scores)
    pieces = with_other_core(far[:2] + above[:2]) + with_other_core(far[2:] + above[2:])
    grad_tab = sum(
        jnp.einsum(
            "hkq,kqb->hb",
            member,
            (where[:, :, None] == jnp.arange(BUCKETS, dtype=jnp.int32)).astype(bf16),
            preferred_element_type=f32,
        )
        for member, where in zip(grad_scores, indexes)
    )
    ff_sum = lax.psum_scatter(
        ff_blocks.reshape(size * ff_tall, width), "ctx", scatter_dimension=0, tiled=True
    )
    pieces[-1], grad_tab = tied(pieces[-1], grad_tab)
    active, normed_one, grad_tab = tied(active, normed_one, grad_tab)
    grads_kv = key_back(
        ([payload] if size == 16 else [pieces[0].reshape(-1, width + 128)])
        + [piece.reshape(-1, width + 128) for piece in pieces[1:]],
        (made_one, made_two),
        (index_one, index_two),
        tables[1],
    )
    out_part = dot_f32(active, w_ff)
    out_other = swap_pair(out_part[rows:].astype(bf16))
    kv_other = swap_pair(grads_kv)
    normed_halves = halves(normed_one)
    q_other = swap_pair(grad_q)
    inputs = tokens[0].astype(f32)
    inv_one = lax.rsqrt(jnp.mean(inputs * inputs, axis=1, keepdims=True) + EPS)
    grad_normed_one = sum(
        jnp.einsum("te,de->td", member, w_qkv[j], preferred_element_type=f32)
        for j, member in enumerate((grad_q, grads_kv[0], grads_kv[1]))
    )
    grad_gain_one, grad_input_norm = norm_back(inputs, inv_one, gain32_one, grad_normed_one)
    grad_tokens = grad_resid + grad_input_norm
    kv_other, out_other = tied(kv_other, out_other)
    output = resid + out_part[:rows] + out_other.astype(f32)

    small_grads = jnp.concatenate(
        [
            grad_gain_one.reshape(2, half_width),
            grad_gain_two.reshape(2, half_width),
            jnp.transpose(grad_tab).reshape(2, rel_table.size),
        ],
        axis=1,
    )
    n_small = small_grads.shape[1]
    each = -(-n_small // size)
    small_grads = jnp.pad(small_grads, ((0, 0), (0, size * each - n_small)))
    small_pair = part_of(small_grads, pair, 2, 0) + swap_pair(part_of(small_grads, 1 - pair, 2, 0))
    small_blocks = jnp.pad(
        small_pair.astype(bf16).reshape(size, 1, each), ((0, 0), (0, 7), (0, width - each))
    )
    rights = [jnp.concatenate([grad_q, q_other])] + [
        jnp.concatenate([grads_kv[j], kv_other[j]]) for j in range(2)
    ]

    def core_blocks(side):
        left = part_of(normed_halves, side, 2, 1)
        made = [by_rows(left, right).reshape(size // 2, tall, width) for right in rights]
        return jnp.concatenate(made + [part_of(small_blocks, side, 2, 0)], axis=1)

    send = core_blocks(1 - spot[1])
    qkv_sum, ff_sum = scatter_sum(core_blocks(spot[1]), send, ff_sum)
    first_in, last_in = tall_ff, tall_ff + 4 * tall
    moved = swap_pair(ff_sum[tall_ff + 2 * tall : last_in])
    ff_sum = jnp.concatenate([ff_sum[: tall_ff + 2 * tall], moved, ff_sum[last_in:]], axis=0)
    ff_full = lax.all_gather(ff_sum, "ctx", axis=0, tiled=True).reshape(size, ff_tall, width)
    near_sum, far_sum = gather_back(qkv_sum)
    *grad_qkv, small_mine = unpack(spot, near_sum, far_sum, tall, 3)
    grad_qkv[0], ff_full = tied(grad_qkv[0], ff_full)
    grad_ff, grad_in, grad_out_w = spread(spot, ff_full, tall_ff, tall)
    grad_qkv = [member.reshape(half_width, width) for member in grad_qkv]
    small_mine = small_mine[:, 0, :each].reshape(-1)
    return (
        output.astype(bf16)[None],
        grad_tokens[None],
        small_mine[:half_width],
        *grad_qkv,
        grad_out_w.reshape(half_width, width),
        small_mine[half_width : 2 * half_width],
        grad_in.reshape(half_width, 4 * width),
        grad_ff.reshape(half_ff, width),
        small_mine[2 * half_width : n_small].reshape(rel_table.shape),
    )


def solution(mesh):
    spread = P("fsdp", "ctx", None)
    rows_of = P("fsdp", None)
    return jax.shard_map(
        shards,
        mesh=mesh,
        in_specs=(
            spread,
            spread,
            rows_of,
            P("fsdp", "ctx"),
            P("fsdp"),
            rows_of,
            rows_of,
            rows_of,
            rows_of,
            P("fsdp"),
            rows_of,
            rows_of,
            rows_of,
        ),
        out_specs=(
            spread,
            spread,
            P("fsdp"),
            rows_of,
            rows_of,
            rows_of,
            rows_of,
            P("fsdp"),
            rows_of,
            rows_of,
            rows_of,
        ),
        check_vma=False,
    )
```

```python
import functools
import jax
import jax.numpy as jnp
from jax import lax
from jax.experimental import pallas as pl
from jax.experimental.pallas import tpu as pltpu
from jax.sharding import PartitionSpec as P

BUCKETS = 32
PIECES = 8
EPS = 1e-06
NEG = -1000000000.0
THRESHOLDS = (1, 2, 3, 4, 5, 6, 7, 8, 12, 16, 23, 32, 46, 64, 91)
VMEM_BYTES = 50 * 1024 * 1024
VMEM_LAST = 32 * 1024 * 1024
VMEM_MOST = 63 * 1024 * 1024


def cost_of(micros):
    return pl.CostEstimate(flops=int(micros * 8e8), bytes_accessed=int(micros * 2.5e6), transcendentals=0)


def dot_nt(left, right):
    return lax.dot_general(left, right, (((1,), (1,)), ((), ())), preferred_element_type=jnp.float32)


def dot_tn(left, right):
    return lax.dot_general(left, right, (((0,), (0,)), ((), ())), preferred_element_type=jnp.float32)


def pair_rows(block, half):
    lane = lax.broadcasted_iota(jnp.int32, block.shape, 1)
    zero = jnp.zeros_like(block)
    return jnp.concatenate(
        [jnp.where(lane < half, block, zero), jnp.where(lane < half, zero, block)], axis=0
    )


def pair_blocks(acc, half, rows):
    return jnp.concatenate([acc[:half, :rows], acc[half:, rows:]], axis=0)


def bias_of(row, index):
    return jnp.take_along_axis(jnp.broadcast_to(row, index.shape), index, axis=1)


def fill_rows(out_ref, j, own, got, more, spot_ref):
    rows, part = own.shape[0], got.shape[0]
    other = (1 - spot_ref[0]) * rows
    out_ref[j, pl.ds(pl.multiple_of(spot_ref[0] * rows, 64), rows), :] = own
    out_ref[j, pl.ds(pl.multiple_of(other + spot_ref[1] * part, 64), part), :] = got
    out_ref[j, pl.ds(pl.multiple_of(other + (1 - spot_ref[1]) * part, 64), part), :] = more


def marks_of(places, total, seqs, spot_ref):
    rows = places.shape[1] // 2
    spots = places[:, :rows] * 128.0 + places[:, rows:]
    end = 0
    begin, segment = jnp.zeros_like(spots), jnp.zeros_like(spots)
    for j in range(seqs):
        end = end + spot_ref[2 + j]
        passed = spots >= end.astype(jnp.float32)
        begin = jnp.where(passed, end.astype(jnp.float32), begin)
        segment = jnp.where(passed, segment + 1.0, segment)
    return spots - begin + segment * (2.0 * total)


def project_kernel(count, total, seqs, first, spot_ref, *refs):
    pieces, refs = refs[:PIECES], refs[PIECES:]
    if first:
        gain_ref, place_ref, wq_ref, wk_ref, wv_ref, got_ref, more_ref = refs[:7]
        made_ref, idx_ref, full_ref, normed_ref, rows_scr, place_scr = refs[7:]
    else:
        gain_ref, place_ref, full_ref, made_ref, idx_ref, rows_scr, place_scr = refs
    width = gain_ref.shape[1]
    rows = idx_ref.shape[2]
    outer, inner = pl.program_id(0), pl.program_id(1)

    for group in range(PIECES // count):

        @pl.when(inner == group)
        def _():
            for j in range(count):
                held = pieces[group * count + j][0]
                rows_scr[j * rows : (j + 1) * rows, :] = held[:rows]
                place_scr[j : j + 1, :] = held[rows:].astype(jnp.float32)[:1, : 2 * rows]

    if first:

        @pl.when((outer == 0) & (inner == 0))
        def _():
            for j, ref in enumerate((wq_ref, wk_ref, wv_ref)):
                fill_rows(full_ref, j, ref[...], got_ref[j], more_ref[j], spot_ref)

    values = rows_scr[...].astype(jnp.float32)
    inverse = lax.rsqrt(jnp.mean(values * values, axis=1, keepdims=True) + EPS)
    normed = (values * inverse * gain_ref[...]).astype(jnp.bfloat16)
    shape = (count, rows, width)
    for j in range(3):
        made = jnp.dot(normed, full_ref[j], preferred_element_type=jnp.float32)
        made_ref[:, :, j * width : (j + 1) * width] = made.astype(jnp.bfloat16).reshape(shape)

    if first:

        @pl.when((outer == 0) & (inner == 0))
        def _():
            normed_ref[...] = normed[:rows]

    own = marks_of(place_ref[...].astype(jnp.float32)[:1, : 2 * rows], total, seqs, spot_ref)
    turned = jnp.transpose(marks_of(place_scr[...], total, seqs, spot_ref))
    for j in range(count):
        offset = turned[:, j : j + 1] - own
        distance = jnp.abs(offset)
        bucket = jnp.where(offset > 0, BUCKETS // 2, 0)
        for threshold in THRESHOLDS:
            bucket = bucket + (distance >= threshold).astype(jnp.int32)
        idx_ref[j] = jnp.where(distance >= total, BUCKETS, bucket)


def project(spot, pieces, gain, places, weights, rows, total, seqs, count=4):
    devices, tall, width = pieces[0].shape
    first = len(weights) > 1
    fixed = lambda rank: (lambda i, j, spot: (0,) * rank)
    moving = lambda i, j, spot: (j, i, 0)
    outputs = [
        (
            pl.BlockSpec((count, rows, 3 * width), moving),
            jax.ShapeDtypeStruct((PIECES, devices * rows, 3 * width), jnp.bfloat16),
        ),
        (
            pl.BlockSpec((count, rows, rows), moving),
            jax.ShapeDtypeStruct((PIECES, devices * rows, rows), jnp.int32),
        ),
    ]
    if first:
        outputs += [
            (
                pl.BlockSpec((3, width, width), fixed(3)),
                jax.ShapeDtypeStruct((3, width, width), jnp.bfloat16),
            ),
            (
                pl.BlockSpec((rows, width), fixed(2)),
                jax.ShapeDtypeStruct((rows, width), jnp.bfloat16),
            ),
        ]
    operands = (gain, places) + tuple(weights)
    return pl.pallas_call(
        functools.partial(project_kernel, count, total, seqs, first),
        grid_spec=pltpu.PrefetchScalarGridSpec(
            num_scalar_prefetch=1,
            grid=(devices, PIECES // count),
            in_specs=[pl.BlockSpec((1, tall, width), lambda i, j, spot: (i, 0, 0))] * PIECES
            + [pl.BlockSpec(member.shape, fixed(member.ndim)) for member in operands],
            out_specs=[spec for spec, _ in outputs],
            scratch_shapes=[
                pltpu.VMEM((count * rows, width), jnp.bfloat16),
                pltpu.VMEM((8, 2 * rows), jnp.float32),
            ],
        ),
        out_shape=[shape for _, shape in outputs],
        compiler_params=pltpu.CompilerParams(vmem_limit_bytes=VMEM_BYTES),
        cost_estimate=cost_of(0.7 * PIECES * devices),
        name="project",
    )(spot, *pieces, *operands)


def close_kernel(spot_ref, attn_ref, x_ref, gain_ref, w_ref, got_ref, more_ref, resid_ref, normed_ref, attn_b_ref, full_ref):
    fill_rows(full_ref, 0, w_ref[...], got_ref[0], more_ref[0], spot_ref)
    attn = attn_ref[...].astype(jnp.bfloat16)
    attn_b_ref[...] = attn
    resid = x_ref[...].astype(jnp.float32) + jnp.dot(
        attn, full_ref[0], preferred_element_type=jnp.float32
    )
    resid_ref[...] = resid
    inverse = lax.rsqrt(jnp.mean(resid * resid, axis=1, keepdims=True) + EPS)
    normed_ref[...] = (resid * inverse * gain_ref[...]).astype(jnp.bfloat16)


def close(spot, attn, tokens, gain, weight, got, more):
    rows, width = attn.shape
    held, part = weight.shape[0], got.shape[1]
    whole = lambda i, spot: (0, 0)
    first = lambda i, spot: (0, 0, 0)
    return pl.pallas_call(
        close_kernel,
        grid_spec=pltpu.PrefetchScalarGridSpec(
            num_scalar_prefetch=1,
            grid=(1,),
            in_specs=[
                pl.BlockSpec((rows, width), whole),
                pl.BlockSpec((rows, width), whole),
                pl.BlockSpec((1, width), whole),
                pl.BlockSpec((held, width), whole),
                pl.BlockSpec((1, part, width), first),
                pl.BlockSpec((1, part, width), first),
            ],
            out_specs=[
                pl.BlockSpec((rows, width), whole),
                pl.BlockSpec((rows, width), whole),
                pl.BlockSpec((rows, width), whole),
                pl.BlockSpec((1, width, width), first),
            ],
        ),
        out_shape=[
            jax.ShapeDtypeStruct((rows, width), jnp.float32),
            jax.ShapeDtypeStruct((rows, width), jnp.bfloat16),
            jax.ShapeDtypeStruct((rows, width), jnp.bfloat16),
            jax.ShapeDtypeStruct((1, width, width), jnp.bfloat16),
        ],
        compiler_params=pltpu.CompilerParams(vmem_limit_bytes=VMEM_BYTES),
        cost_estimate=cost_of(2),
        name="close",
    )(spot, attn, tokens, gain, weight, got, more)


def branch_kernel(part_ref, got_ref, resid_ref, cot_ref, gain_ref, out_ref, attn_ref, lse_ref, payload_ref, delta_ref, grad_ref, branch_ref, gain_grad_ref):
    f32, bf16 = jnp.float32, jnp.bfloat16
    rows, width = resid_ref.shape
    heads = lse_ref.shape[0]
    size = width // heads
    resid = resid_ref[...]
    normed_grad = part_ref[...] + got_ref[...].astype(f32)
    inverse = lax.rsqrt(jnp.mean(resid * resid, axis=1, keepdims=True) + EPS)
    gain_grad_ref[...] = jnp.sum(normed_grad * resid * inverse, axis=0, keepdims=True)
    scaled = normed_grad * gain_ref[...]
    mean = jnp.mean(scaled * resid, axis=1, keepdims=True)
    grad = cot_ref[...].astype(f32) + inverse * (scaled - resid * (inverse * inverse * mean))
    grad_ref[...] = grad
    branch = grad.astype(bf16)
    branch_ref[...] = branch
    attn_grad = dot_nt(branch, out_ref[0]).astype(bf16)
    payload_ref[:, :width] = attn_grad
    product = attn_grad.astype(f32) * attn_ref[...]
    high = product.astype(bf16)
    low = (product - high.astype(f32)).astype(bf16)

    def member(shape, at_row, at_col):
        row = lax.broadcasted_iota(jnp.int32, shape, 0)
        col = lax.broadcasted_iota(jnp.int32, shape, 1)
        return jnp.where(at_row(row) == at_col(col), 1.0, 0.0).astype(bf16)

    padded = 16
    by_head = member((padded, width), lambda r: r, lambda c: c // size)
    delta = (dot_nt(by_head, high) + dot_nt(by_head, low))[:heads]
    delta_ref[...] = delta
    col = lax.broadcasted_iota(jnp.int32, (rows, 128), 1)
    aux = jnp.zeros((rows, 128), f32)
    for first, values in ((0, lse_ref[...]), (64, delta)):
        values = jnp.concatenate([values, jnp.zeros((padded - heads, rows), f32)], axis=0)
        high = values.astype(bf16)
        low = (values - high.astype(f32)).astype(bf16)
        for odd, half in ((0, high), (1, low)):
            to_col = member((padded, 128), lambda r: first + odd + 2 * r, lambda c: c)
            aux = aux + dot_tn(half, to_col)
    payload_ref[:, width:] = aux.astype(bf16)


def branch(part, got, resid, cotangent, gain, full_out, attn, lse):
    rows, width = resid.shape
    heads = lse.shape[0]
    return pl.pallas_call(
        branch_kernel,
        grid=(1,),
        in_specs=[
            pl.BlockSpec((rows, width), lambda i: (0, 0)),
            pl.BlockSpec((rows, width), lambda i: (0, 0)),
            pl.BlockSpec((rows, width), lambda i: (0, 0)),
            pl.BlockSpec((rows, width), lambda i: (0, 0)),
            pl.BlockSpec((1, width), lambda i: (0, 0)),
            pl.BlockSpec((1, width, width), lambda i: (0, 0, 0)),
            pl.BlockSpec((rows, width), lambda i: (0, 0)),
            pl.BlockSpec((heads, rows), lambda i: (0, 0)),
        ],
        out_specs=[
            pl.BlockSpec((rows, width + 128), lambda i: (0, 0)),
            pl.BlockSpec((heads, rows), lambda i: (0, 0)),
            pl.BlockSpec((rows, width), lambda i: (0, 0)),
            pl.BlockSpec((rows, width), lambda i: (0, 0)),
            pl.BlockSpec((1, width), lambda i: (0, 0)),
        ],
        out_shape=[
            jax.ShapeDtypeStruct((rows, width + 128), jnp.bfloat16),
            jax.ShapeDtypeStruct((heads, rows), jnp.float32),
            jax.ShapeDtypeStruct((rows, width), jnp.float32),
            jax.ShapeDtypeStruct((rows, width), jnp.bfloat16),
            jax.ShapeDtypeStruct((1, width), jnp.float32),
        ],
        compiler_params=pltpu.CompilerParams(vmem_limit_bytes=VMEM_BYTES),
        cost_estimate=cost_of(3),
        name="branch",
    )(part, got, resid, cotangent, gain, full_out, attn, lse)


def unpack_kernel(tall, spot_ref, near_ref, far_ref, *out_refs):
    values = jnp.where(pl.program_id(0) == 0, near_ref[...], far_ref[...]).astype(jnp.float32)
    for j, ref in enumerate(out_refs[:-1]):
        ref[...] = values[:, j * tall : (j + 1) * tall, :]
    out_refs[-1][...] = values[:, (len(out_refs) - 1) * tall :, :128]


def unpack(spot, near, far, tall, outputs):
    half, high, width = near.shape
    step = min(4, half)
    steps = half // step

    def place(j, i, spot):
        return (jnp.bitwise_xor(j, spot[1]) * steps + i, 0, 0)

    return pl.pallas_call(
        functools.partial(unpack_kernel, tall),
        grid_spec=pltpu.PrefetchScalarGridSpec(
            num_scalar_prefetch=1,
            grid=(2, steps),
            in_specs=[
                pl.BlockSpec(
                    (step, high, width), lambda j, i, spot: (jnp.where(j == 0, i, steps - 1), 0, 0)
                ),
                pl.BlockSpec(
                    (step, high, width), lambda j, i, spot: (jnp.where(j == 0, 0, i), 0, 0)
                ),
            ],
            out_specs=[pl.BlockSpec((step, tall, width), place)] * outputs
            + [pl.BlockSpec((step, high - outputs * tall, 128), place)],
        ),
        out_shape=[jax.ShapeDtypeStruct((2 * half, tall, width), jnp.float32)] * outputs
        + [jax.ShapeDtypeStruct((2 * half, high - outputs * tall, 128), jnp.float32)],
        compiler_params=pltpu.CompilerParams(vmem_limit_bytes=VMEM_BYTES),
        cost_estimate=cost_of(4),
        name="unpack",
    )(spot, near, far)


def spread_kernel(tall_ff, tall, spot_ref, full_ref, ff_ref, in_ref, out_ref):
    width = out_ref.shape[2]
    values = full_ref[...].astype(jnp.float32)
    ff_ref[...] = values[:, :tall_ff, :]
    parts = [values[:, tall_ff + j * tall : tall_ff + (j + 1) * tall, :] for j in range(5)]
    for j in range(2):
        in_ref[:, :, j * width : (j + 1) * width] = jnp.where(
            spot_ref[0] == 0, parts[j], parts[2 + j]
        )
        in_ref[:, :, (2 + j) * width : (3 + j) * width] = jnp.where(
            spot_ref[0] == 0, parts[2 + j], parts[j]
        )
    out_ref[...] = parts[4]


def spread(spot, full, tall_ff, tall):
    size, high, width = full.shape
    step = 4
    return pl.pallas_call(
        functools.partial(spread_kernel, tall_ff, tall),
        grid_spec=pltpu.PrefetchScalarGridSpec(
            num_scalar_prefetch=1,
            grid=(size // step,),
            in_specs=[pl.BlockSpec((step, high, width), lambda i, spot: (i, 0, 0))],
            out_specs=[
                pl.BlockSpec((step, tall_ff, width), lambda i, spot: (i, 0, 0)),
                pl.BlockSpec((step, tall, 4 * width), lambda i, spot: (i, 0, 0)),
                pl.BlockSpec((step, tall, width), lambda i, spot: (i, 0, 0)),
            ],
        ),
        out_shape=[
            jax.ShapeDtypeStruct((size, tall_ff, width), jnp.float32),
            jax.ShapeDtypeStruct((size, tall, 4 * width), jnp.float32),
            jax.ShapeDtypeStruct((size, tall, width), jnp.float32),
        ],
        compiler_params=pltpu.CompilerParams(vmem_limit_bytes=VMEM_LAST),
        cost_estimate=cost_of(6),
        name="spread",
    )(spot, full)


def attend_kernel(tile, first, q_ref, k_ref, v_ref, idx_ref, tab_ref, *refs):
    if first:
        outs, m_out, p_ref, s_scr, m_scr, l_scr, acc_scr = refs[:3], *refs[3:]
    else:
        kept, outs, m_out, p_ref, s_scr, m_scr, l_scr, acc_scr = refs[:3], refs[3:5], *refs[5:]
    chunk, n_chunks = pl.program_id(1), pl.num_programs(1)
    rows = q_ref.shape[0]
    half = q_ref.shape[1] // 2
    keys = k_ref.shape[0]

    @pl.when(chunk == 0)
    def _():
        if first:
            m_scr[...] = jnp.full_like(m_scr, -3.0e38)
            l_scr[...] = jnp.zeros_like(l_scr)
            acc_scr[...] = jnp.zeros_like(acc_scr)
        else:
            m_scr[...] = kept[0][0]
            l_scr[...] = kept[1][0]
            acc_scr[...] = kept[2][0]

    q_cat = pair_rows(q_ref[...], half)
    m_old = m_scr[...]
    m_tiles = jnp.full((8, 2 * rows), -3.0e38, jnp.float32)
    for t in range(keys // tile):
        rng = slice(t * tile, (t + 1) * tile)
        s = dot_nt(k_ref[rng, :], q_cat)
        index = idx_ref[rng, :]
        s = s + jnp.concatenate(
            [bias_of(tab_ref[0, j : j + 1, :], index) for j in range(2)], axis=1
        )
        s_scr[rng, :] = s
        m_tiles = jnp.maximum(m_tiles, jnp.max(s.reshape(tile // 8, 8, 2 * rows), axis=0))
    m_new = jnp.maximum(m_old, jnp.max(m_tiles, axis=0, keepdims=True))
    fade = jnp.exp(m_old - m_new)
    sums = jnp.zeros((8, 2 * rows), jnp.float32)
    acc = acc_scr[...] * fade
    for t in range(keys // tile):
        rng = slice(t * tile, (t + 1) * tile)
        p = jnp.exp(s_scr[rng, :] - m_new)
        sums = sums + jnp.sum(p.reshape(tile // 8, 8, 2 * rows), axis=0)
        p_low = p.astype(jnp.bfloat16)
        p_ref[0, rng, :] = p_low[:, :rows]
        p_ref[1, rng, :] = p_low[:, rows:]
        acc = acc + dot_tn(v_ref[rng, :], p_low)
    acc_scr[...] = acc
    l_new = l_scr[...] * fade + jnp.sum(sums, axis=0, keepdims=True)
    l_scr[...] = l_new
    m_scr[...] = m_new
    m_out[0, 0] = m_new

    @pl.when(chunk == n_chunks - 1)
    def _():
        if first:
            outs[0][0], outs[1][0], outs[2][0] = m_new, l_new, acc
        else:
            outs[0][...] = jnp.transpose(pair_blocks(acc / l_new, half, rows))
            outs[1][0] = m_new + jnp.log(l_new)


def attend(made_own, made, index, table, chunk_keys, kept=None, tile=512):
    total, rows = index.shape
    width = made.shape[1] // 3
    heads = table.shape[0] * 2
    pairs = table.shape[0]
    wide = width // pairs
    n_chunks = total // chunk_keys
    first = kept is None
    line = (
        pl.BlockSpec((1, 1, 2 * rows), lambda p, c: (p, 0, 0)),
        jax.ShapeDtypeStruct((pairs, 1, 2 * rows), jnp.float32),
    )
    square = (
        pl.BlockSpec((1, wide, 2 * rows), lambda p, c: (p, 0, 0)),
        jax.ShapeDtypeStruct((pairs, wide, 2 * rows), jnp.float32),
    )
    result = (
        pl.BlockSpec((rows, wide), lambda p, c: (0, p)),
        jax.ShapeDtypeStruct((rows, width), jnp.float32),
    )
    outputs = [line, line, square] if first else [result, line]
    outputs += [
        (
            pl.BlockSpec((1, 1, 1, 2 * rows), lambda p, c: (p, c, 0, 0)),
            jax.ShapeDtypeStruct((pairs, n_chunks, 1, 2 * rows), jnp.float32),
        ),
        (
            pl.BlockSpec((2, chunk_keys, rows), lambda p, c: (p, c, 0)),
            jax.ShapeDtypeStruct((heads, total, rows), jnp.bfloat16),
        ),
    ]
    return pl.pallas_call(
        functools.partial(attend_kernel, tile, first),
        grid=(pairs, n_chunks),
        in_specs=[
            pl.BlockSpec((rows, wide), lambda p, c: (0, p)),
            pl.BlockSpec((chunk_keys, wide), lambda p, c: (c, pairs + p)),
            pl.BlockSpec((chunk_keys, wide), lambda p, c: (c, 2 * pairs + p)),
            pl.BlockSpec((chunk_keys, rows), lambda p, c: (c, 0)),
            pl.BlockSpec((1, 2, 128), lambda p, c: (p, 0, 0)),
        ]
        + ([] if first else [line[0], line[0], square[0]]),
        out_specs=[spec for spec, _ in outputs],
        out_shape=[shape for _, shape in outputs],
        scratch_shapes=[
            pltpu.VMEM((chunk_keys, 2 * rows), jnp.float32),
            pltpu.VMEM((1, 2 * rows), jnp.float32),
            pltpu.VMEM((1, 2 * rows), jnp.float32),
            pltpu.VMEM((wide, 2 * rows), jnp.float32),
        ],
        compiler_params=pltpu.CompilerParams(vmem_limit_bytes=VMEM_BYTES),
        cost_estimate=cost_of(0.008 * total),
        name="attend",
    )(made_own, made, made, index, table, *([] if first else kept))


def query_back_kernel(tile, *refs):
    groups, refs = (refs[0:4], refs[4:8]), refs[8:]
    da_ref, delta_ref, lse_ref, dq_ref, acc_scr = refs[:3] + refs[5:]
    chunk, n_chunks = pl.program_id(1), pl.num_programs(1)
    rows = da_ref.shape[0]
    half = da_ref.shape[1] // 2

    @pl.when(chunk == 0)
    def _():
        acc_scr[...] = jnp.zeros_like(acc_scr)

    delta = delta_ref[0]
    da_cat = pair_rows(da_ref[...], half)
    acc = acc_scr[...]
    for (p_ref, v_ref, k_ref, m_ref), ds_ref in zip(groups, refs[3:5]):
        factor = jnp.exp(m_ref[0, 0] - lse_ref[0])
        for t in range(v_ref.shape[0] // tile):
            rng = slice(t * tile, (t + 1) * tile)
            dp = dot_nt(v_ref[rng, :], da_cat)
            p = jnp.concatenate([p_ref[0, rng, :], p_ref[1, rng, :]], axis=1).astype(jnp.float32)
            ds = ((p * factor) * (dp - delta)).astype(jnp.bfloat16)
            ds_ref[0, rng, :] = ds[:, :rows]
            ds_ref[1, rng, :] = ds[:, rows:]
            acc = acc + dot_tn(k_ref[rng, :], ds)
    acc_scr[...] = acc

    @pl.when(chunk == n_chunks - 1)
    def _():
        dq_ref[...] = jnp.transpose(pair_blocks(acc, half, rows)).astype(jnp.bfloat16)


def query_back(probs, mades, lows, payload, delta, lse, chunk_keys, tile=512):
    heads, total, rows = probs[0].shape
    pairs = heads // 2
    width = mades[0].shape[1] // 3
    wide = width // pairs
    n_chunks = total // chunk_keys
    prob = pl.BlockSpec((2, chunk_keys, rows), lambda p, c: (p, c, 0))
    line = pl.BlockSpec((1, 1, 2 * rows), lambda p, c: (p, 0, 0))
    group = [
        prob,
        pl.BlockSpec((chunk_keys, wide), lambda p, c: (c, 2 * pairs + p)),
        pl.BlockSpec((chunk_keys, wide), lambda p, c: (c, pairs + p)),
        pl.BlockSpec((1, 1, 1, 2 * rows), lambda p, c: (p, c, 0, 0)),
    ]
    members = [(probs[j], mades[j], mades[j], lows[j]) for j in range(2)]
    return pl.pallas_call(
        functools.partial(query_back_kernel, tile),
        grid=(pairs, n_chunks),
        in_specs=group + group + [pl.BlockSpec((rows, wide), lambda p, c: (0, p)), line, line],
        out_specs=[prob, prob, pl.BlockSpec((rows, wide), lambda p, c: (0, p))],
        out_shape=[
            jax.ShapeDtypeStruct((heads, total, rows), jnp.bfloat16),
            jax.ShapeDtypeStruct((heads, total, rows), jnp.bfloat16),
            jax.ShapeDtypeStruct((rows, width), jnp.bfloat16),
        ],
        scratch_shapes=[pltpu.VMEM((wide, 2 * rows), jnp.float32)],
        input_output_aliases={0: 0, 4: 1},
        compiler_params=pltpu.CompilerParams(vmem_limit_bytes=VMEM_BYTES),
        cost_estimate=cost_of(0.01 * total),
        name="query_back",
    )(*members[0], *members[1], payload, delta, lse)


def key_back_kernel(count, *refs):
    n_pieces = 2 * PIECES
    grads, auxes, refs = refs[:n_pieces], refs[n_pieces : 2 * n_pieces], refs[2 * n_pieces :]
    q_refs, idx_refs, refs = refs[:2], refs[2:4], refs[4:]
    k_ref, v_ref, tab_ref, out_ref, dk_scr, dv_scr = refs
    pair, chunk, n_chunks = pl.program_id(0), pl.program_id(1), pl.num_programs(1)
    rows = k_ref.shape[0]
    wide = k_ref.shape[1]
    half = wide // 2

    @pl.when(chunk == 0)
    def _():
        dk_scr[...] = jnp.zeros_like(dk_scr)
        dv_scr[...] = jnp.zeros_like(dv_scr)

    lane = lax.broadcasted_iota(jnp.int32, (2 * rows, 128), 1)
    head = 2 * pair + (lax.broadcasted_iota(jnp.int32, (2 * rows, 128), 0) >= rows).astype(jnp.int32)
    early = (lane >= 2 * head) & (lane < 2 * head + 2)
    late = (lane >= 64 + 2 * head) & (lane < 64 + 2 * head + 2)
    take_lse = jnp.where(early, -1.0, 0.0).astype(jnp.bfloat16)
    take_delta = jnp.where(late, -1.0, 0.0).astype(jnp.bfloat16)
    k_cat = jnp.concatenate([pair_rows(k_ref[...], half), take_lse], axis=1)
    v_cat = jnp.concatenate([pair_rows(v_ref[...], half), take_delta], axis=1)
    dk, dv = dk_scr[...], dv_scr[...]
    for t in range(0, n_pieces, count):
        group, at = t // PIECES, t % PIECES
        da = jnp.concatenate([ref[...] for ref in grads[t : t + count]], axis=0)
        aux = jnp.concatenate([ref[...] for ref in auxes[t : t + count]], axis=0)
        q = q_refs[group][at : at + count].reshape(count * rows, wide)
        index = idx_refs[group][at : at + count].reshape(count * rows, rows)
        s = dot_nt(jnp.concatenate([q, aux], axis=1), k_cat)
        bias = jnp.concatenate(
            [bias_of(tab_ref[0, j : j + 1, :], index) for j in range(2)], axis=1
        )
        p = jnp.exp(s + bias)
        ds = p * dot_nt(jnp.concatenate([da, aux], axis=1), v_cat)
        dv = dv + dot_tn(da, p.astype(jnp.bfloat16))
        dk = dk + dot_tn(q, ds.astype(jnp.bfloat16))
    dk_scr[...] = dk
    dv_scr[...] = dv

    @pl.when(chunk == n_chunks - 1)
    def _():
        for j, acc in enumerate((dk, dv)):
            out_ref[j] = jnp.transpose(pair_blocks(acc, half, rows)).astype(jnp.bfloat16)


def key_back(pieces, mades, indexes, table, count=4):
    rows = indexes[0].shape[2]
    side, width = mades[0].shape[1], mades[0].shape[2] // 3
    pairs = table.shape[0]
    wide = width // pairs
    n_chunks = side // rows
    return pl.pallas_call(
        functools.partial(key_back_kernel, count),
        grid=(pairs, n_chunks),
        in_specs=[pl.BlockSpec((rows, wide), lambda p, c: (c, p))] * len(pieces)
        + [pl.BlockSpec((rows, 128), lambda p, c: (c, pairs))] * len(pieces)
        + [pl.BlockSpec((PIECES, rows, wide), lambda p, c: (0, c, p))] * 2
        + [pl.BlockSpec((PIECES, rows, rows), lambda p, c: (0, c, 0))] * 2
        + [
            pl.BlockSpec((None, rows, wide), lambda p, c: (0, 0, pairs + p)),
            pl.BlockSpec((None, rows, wide), lambda p, c: (0, 0, 2 * pairs + p)),
            pl.BlockSpec((1, 2, 128), lambda p, c: (p, 0, 0)),
        ],
        out_specs=pl.BlockSpec((2, rows, wide), lambda p, c: (0, 0, p)),
        out_shape=jax.ShapeDtypeStruct((2, rows, width), jnp.bfloat16),
        scratch_shapes=[pltpu.VMEM((wide, 2 * rows), jnp.float32)] * 2,
        compiler_params=pltpu.CompilerParams(vmem_limit_bytes=VMEM_MOST),
        cost_estimate=cost_of(15 * n_chunks),
        name="key_back",
    )(*pieces, *pieces, *mades, *indexes, mades[0], mades[0], table)


def norm_back(values, inverse, scale_gain, grad_normed):
    grad_gain = jnp.sum(grad_normed * values * inverse, axis=0)
    scaled = grad_normed * scale_gain
    grad_values = inverse * (
        scaled - values * inverse * inverse * jnp.mean(scaled * values, axis=1, keepdims=True)
    )
    return (grad_gain, grad_values)


def smooth_gate(values):
    return jax.nn.gelu(values, approximate=True)


def dot_f32(left, right):
    return jnp.dot(left, right, preferred_element_type=jnp.float32)


def swap_ctx(values, distance):
    size = lax.axis_size("ctx")
    return lax.ppermute(values, "ctx", [(i, i ^ distance) for i in range(size)])


def swap_pair(values):
    return lax.ppermute(values, "fsdp", [(0, 1), (1, 0)])


def in_order(where, mine, other, axis=0):
    return jnp.where(
        where == 0,
        jnp.concatenate([mine, other], axis=axis),
        jnp.concatenate([other, mine], axis=axis),
    )


def part_of(values, index, parts, axis):
    size = values.shape[axis] // parts
    return lax.dynamic_slice_in_dim(values, index * size, size, axis)


def tied(*members):
    return lax.optimization_barrier(members)


def gather_far(block):
    size = lax.axis_size("ctx")
    quarter = size // 4
    block = block[None]
    distance = 2 * 2
    while distance < quarter:
        block = jnp.concatenate([block, swap_ctx(block, distance)], axis=0)
        distance *= 2
    return [block] + [swap_ctx(block, quarter * j) for j in (1, 2, 3)]


def with_other_core(members):
    return members + [swap_ctx(piece, 1) for piece in members]


def scatter_sum(keep, send, tie):
    here, size = lax.axis_index("ctx"), lax.axis_size("ctx")
    f32, low, distance = jnp.float32, keep.dtype, 1
    got = swap_ctx(send, distance)
    while distance < size // 8:
        blocks = (keep.astype(f32) + got.astype(f32)).astype(low)
        distance *= 2
        mine = (here // distance) % 2
        send = part_of(blocks, 1 - mine, 2, 0)
        if distance == 2:
            send, tie = tied(send, tie)
        got = swap_ctx(send, distance)
        keep = part_of(blocks, mine, 2, 0)
    blocks = (keep.astype(f32) + got.astype(f32)).astype(low)
    distance *= 2
    mine = here // distance
    got = [swap_ctx(part_of(blocks, mine ^ j, 4, 0), distance * j) for j in (1, 2, 3)]
    added = part_of(blocks, mine, 4, 0).astype(f32) + sum(member.astype(f32) for member in got)
    return added.astype(low), tie


def gather_back(block):
    here, size = lax.axis_index("ctx"), lax.axis_size("ctx")
    distance = size // 4
    got = [swap_ctx(block, distance * j) for j in (1, 2, 3)]
    low_bit, high_bit = (here // distance) % 2, here // (2 * distance)
    blocks = in_order(high_bit, in_order(low_bit, block, got[0]), in_order(low_bit, got[1], got[2]))
    while distance > 2:
        distance //= 2
        blocks = in_order((here // distance) % 2, blocks, swap_ctx(blocks, distance))
    return blocks, swap_ctx(blocks, 1)


def sent_weights(*members):
    core = lax.axis_index("ctx") % 2
    return swap_pair(jnp.stack([part_of(member, core, 2, 0) for member in members]))


def shards(
    tokens,
    cotangent,
    lengths,
    dealing,
    gain_one,
    w_query,
    w_key,
    w_value,
    w_out,
    gain_two,
    w_in,
    w_ff,
    rel_table,
):
    bf16, f32 = jnp.bfloat16, jnp.float32
    size = lax.axis_size("ctx")
    pair = lax.axis_index("fsdp")
    rows, width = tokens.shape[1], tokens.shape[2]
    heads = rel_table.shape[1]
    head_size = width // heads
    pairs = heads // 2
    total = size * rows
    half_ff = w_ff.shape[0]
    half_width = w_query.shape[0]
    chunk_keys = min(total // 2, 1024)

    spot = jnp.concatenate(
        [jnp.stack([pair, lax.axis_index("ctx") % 2]).astype(jnp.int32), lengths[0]]
    )

    dealt = dealing[0]
    place_row = jnp.concatenate([dealt // 128, dealt % 128]).astype(bf16)
    place_rows = jnp.pad(place_row[None], ((0, 7), (0, width - 2 * rows)))
    far = gather_far(jnp.concatenate([tokens[0], place_rows], axis=0))
    *far, above = tied(*far, swap_ctx(far[0], 2))
    above = [above] + [swap_ctx(piece, 2) for piece in far[1:]]

    small = jnp.concatenate([gain_one, gain_two, rel_table.reshape(-1)])
    small = jnp.pad(small, (0, 1024 - small.shape[0])).reshape(8, 128)
    small_other = swap_pair(small)
    small_full = jnp.stack([small.reshape(-1), small_other.reshape(-1)])
    small_full = jnp.where(pair == 0, small_full, small_full[::-1])
    gain32_one = small_full[:, :half_width].reshape(width).astype(f32)
    gain32_two = small_full[:, half_width : 2 * half_width].reshape(width).astype(f32)
    full_table = small_full[:, 2 * half_width : 2 * half_width + rel_table.size]
    full_table = full_table.reshape(2 * rel_table.shape[0], heads).astype(f32)
    got_one = sent_weights(w_query, w_key, w_value)
    got_one, above[1] = tied(got_one, above[1])
    more_one = swap_ctx(got_one, 1)
    more_one, w_out, w_in, cotangent = tied(more_one, w_out, w_in, cotangent)
    mine_in, other_in = (part_of(w_in, index, 2, 1) for index in (pair, 1 - pair))
    got_two = sent_weights(w_out, other_in[:, :width], other_in[:, width:])
    grad_out = cotangent[0]
    grad_out_pair = jnp.concatenate([grad_out, swap_pair(grad_out)], axis=0)

    table_t = jnp.transpose(full_table)
    back_t = jnp.concatenate(
        [table_t[:, :1], table_t[:, 17:], table_t[:, :1], table_t[:, 1:16]], axis=1
    )
    tables = [
        jnp.pad(tab, ((0, 0), (0, 128 - BUCKETS)), constant_values=NEG).reshape(pairs, 2, 128)
        for tab in (table_t, back_t)
    ]
    fixed = (rows, total, lengths.shape[1])
    weights = (w_query, w_key, w_value, got_one, more_one)
    gain_row = gain32_one[None]
    made_one, index_one, w_qkv, normed_one = project(
        spot, with_other_core(far[:2] + above[:2]), gain_row, place_rows, weights, *fixed
    )
    above[2], above[3], made_one = tied(above[2], above[3], made_one)
    pieces = with_other_core(far[2:] + above[2:])
    mades, indexes = [made_one.reshape(total // 2, -1)], [index_one.reshape(total // 2, rows)]
    *kept, low_one, prob_one = attend(mades[0], mades[0], indexes[0], tables[0], chunk_keys)
    pieces, kept, got_two = tied(pieces, kept, got_two)
    more_two = swap_ctx(got_two, 1)
    made_two, index_two = project(spot, pieces, gain_row, place_rows, (w_qkv,), *fixed)
    mades.append(made_two.reshape(total // 2, -1))
    indexes.append(index_two.reshape(total // 2, rows))
    attn_f32, lse, low_two, prob_two = attend(
        mades[0], mades[1], indexes[1], tables[0], chunk_keys, kept
    )
    lows, probs = (low_one, low_two), (prob_one, prob_two)

    resid, normed_two, attn_b, full_out = close(
        spot, attn_f32, tokens[0], gain32_two[None], w_out, got_two, more_two
    )
    normed_pair = jnp.concatenate([normed_two, swap_pair(normed_two)], axis=0)
    core = lax.axis_index("ctx") % 2
    half_in = jnp.concatenate(
        [
            in_order(
                pair,
                mine_in[:, j * width : (j + 1) * width],
                in_order(core, got_two[1 + j], more_two[1 + j]),
            )
            for j in range(2)
        ],
        axis=1,
    )
    gate_pre = dot_f32(normed_pair, half_in)
    gate_val, gate_pull = jax.vjp(smooth_gate, gate_pre)
    active = gate_val.astype(bf16)
    grad_active = jnp.einsum("td,fd->tf", grad_out_pair, w_ff, preferred_element_type=f32)
    grad_pre = gate_pull(grad_active)[0].astype(bf16)
    grad_normed_part = jnp.einsum("tf,df->td", grad_pre, half_in, preferred_element_type=f32)
    payload, delta, grad_resid, grad_branch, grad_gain_two = branch(
        grad_normed_part,
        swap_pair(grad_normed_part[rows:].astype(bf16)),
        resid,
        grad_out,
        gain32_two[None],
        full_out,
        attn_f32,
        lse.reshape(heads, rows),
    )
    payload, active, normed_pair, grad_pre, attn_b = tied(
        payload, active, normed_pair, grad_pre, attn_b
    )

    def halves(values):
        other = swap_pair(part_of(values, 1 - pair, 2, 1))
        return jnp.concatenate([part_of(values, pair, 2, 1), other], axis=0)

    def both(values):
        return jnp.concatenate([values, swap_pair(values)], axis=0)

    def by_rows(left, right):
        return jnp.einsum("td,te->de", left, right, preferred_element_type=f32).astype(bf16)

    def blocks_of(values):
        return [
            values[:, j : j + width].reshape(size, values.shape[0] // size, width)
            for j in range(0, values.shape[1], width)
        ]

    tall = half_width // size
    tall_ff = half_ff // size
    grad_ff_part = by_rows(active, grad_out_pair)
    grad_in_part = by_rows(normed_pair, grad_pre)
    branch_other = swap_pair(
        jnp.concatenate([part_of(attn_b, 1 - pair, 2, 1), grad_branch], axis=1)
    )
    attn_pair = jnp.concatenate([part_of(attn_b, pair, 2, 1), branch_other[:, :half_width]], axis=0)
    branch_pair = jnp.concatenate([grad_branch, branch_other[:, half_width:]], axis=0)
    grad_out_part = by_rows(attn_pair, branch_pair)
    in_blocks = blocks_of(part_of(grad_in_part, pair, 2, 0)) + blocks_of(
        part_of(grad_in_part, 1 - pair, 2, 0)
    )
    ff_blocks = jnp.concatenate(
        blocks_of(grad_ff_part) + in_blocks + blocks_of(grad_out_part), axis=1
    )
    ff_tall = ff_blocks.shape[1]

    far = gather_far(payload)
    *far, above, ff_blocks, payload = tied(*far, swap_ctx(far[0], 2), ff_blocks, payload)
    above = [above] + [swap_ctx(piece, 2) for piece in far[1:]]
    above[1], payload = tied(above[1], payload)
    *grad_scores, grad_q = query_back(
        probs, mades, lows, payload, delta.reshape(pairs, 1, 2 * rows), lse, chunk_keys
    )
    above[1], above[2], above[3], grad_scores = tied(*above[1:], grad_scores)
    pieces = with_other_core(far[:2] + above[:2]) + with_other_core(far[2:] + above[2:])
    grad_tab = sum(
        jnp.einsum(
            "hkq,kqb->hb",
            member,
            (where[:, :, None] == jnp.arange(BUCKETS, dtype=jnp.int32)).astype(bf16),
            preferred_element_type=f32,
        )
        for member, where in zip(grad_scores, indexes)
    )
    ff_sum = lax.psum_scatter(
        ff_blocks.reshape(size * ff_tall, width), "ctx", scatter_dimension=0, tiled=True
    )
    pieces[-1], grad_tab = tied(pieces[-1], grad_tab)
    active, normed_one, grad_tab = tied(active, normed_one, grad_tab)
    grads_kv = key_back(
        ([payload] if size == 16 else [pieces[0].reshape(-1, width + 128)])
        + [piece.reshape(-1, width + 128) for piece in pieces[1:]],
        (made_one, made_two),
        (index_one, index_two),
        tables[1],
    )
    out_part = dot_f32(active, w_ff)
    out_other = swap_pair(out_part[rows:].astype(bf16))
    kv_other = swap_pair(grads_kv)
    normed_halves = halves(normed_one)
    q_other = swap_pair(grad_q)
    inputs = tokens[0].astype(f32)
    inv_one = lax.rsqrt(jnp.mean(inputs * inputs, axis=1, keepdims=True) + EPS)
    grad_normed_one = sum(
        jnp.einsum("te,de->td", member, w_qkv[j], preferred_element_type=f32)
        for j, member in enumerate((grad_q, grads_kv[0], grads_kv[1]))
    )
    grad_gain_one, grad_input_norm = norm_back(inputs, inv_one, gain32_one, grad_normed_one)
    grad_tokens = grad_resid + grad_input_norm
    kv_other, out_other = tied(kv_other, out_other)
    output = resid + out_part[:rows] + out_other.astype(f32)

    small_grads = jnp.concatenate(
        [
            grad_gain_one.reshape(2, half_width),
            grad_gain_two.reshape(2, half_width),
            jnp.transpose(grad_tab).reshape(2, rel_table.size),
        ],
        axis=1,
    )
    n_small = small_grads.shape[1]
    each = -(-n_small // size)
    small_grads = jnp.pad(small_grads, ((0, 0), (0, size * each - n_small)))
    small_pair = part_of(small_grads, pair, 2, 0) + swap_pair(part_of(small_grads, 1 - pair, 2, 0))
    small_blocks = jnp.pad(
        small_pair.astype(bf16).reshape(size, 1, each), ((0, 0), (0, 7), (0, width - each))
    )
    rights = [jnp.concatenate([grad_q, q_other])] + [
        jnp.concatenate([grads_kv[j], kv_other[j]]) for j in range(2)
    ]

    def core_blocks(side):
        left = part_of(normed_halves, side, 2, 1)
        made = [by_rows(left, right).reshape(size // 2, tall, width) for right in rights]
        return jnp.concatenate(made + [part_of(small_blocks, side, 2, 0)], axis=1)

    send = core_blocks(1 - spot[1])
    qkv_sum, ff_sum = scatter_sum(core_blocks(spot[1]), send, ff_sum)
    first_in, last_in = tall_ff, tall_ff + 4 * tall
    moved = swap_pair(ff_sum[tall_ff + 2 * tall : last_in])
    ff_sum = jnp.concatenate([ff_sum[: tall_ff + 2 * tall], moved, ff_sum[last_in:]], axis=0)
    ff_full = lax.all_gather(ff_sum, "ctx", axis=0, tiled=True).reshape(size, ff_tall, width)
    near_sum, far_sum = gather_back(qkv_sum)
    *grad_qkv, small_mine = unpack(spot, near_sum, far_sum, tall, 3)
    grad_qkv[0], ff_full = tied(grad_qkv[0], ff_full)
    grad_ff, grad_in, grad_out_w = spread(spot, ff_full, tall_ff, tall)
    grad_qkv = [member.reshape(half_width, width) for member in grad_qkv]
    small_mine = small_mine[:, 0, :each].reshape(-1)
    return (
        output.astype(bf16)[None],
        grad_tokens[None],
        small_mine[:half_width],
        *grad_qkv,
        grad_out_w.reshape(half_width, width),
        small_mine[half_width : 2 * half_width],
        grad_in.reshape(half_width, 4 * width),
        grad_ff.reshape(half_ff, width),
        small_mine[2 * half_width : n_small].reshape(rel_table.shape),
    )


def solution(mesh):
    spread = P("fsdp", "ctx", None)
    rows_of = P("fsdp", None)
    return jax.shard_map(
        shards,
        mesh=mesh,
        in_specs=(
            spread,
            spread,
            rows_of,
            P("fsdp", "ctx"),
            P("fsdp"),
            rows_of,
            rows_of,
            rows_of,
            rows_of,
            P("fsdp"),
            rows_of,
            rows_of,
            rows_of,
        ),
        out_specs=(
            spread,
            spread,
            P("fsdp"),
            rows_of,
            rows_of,
            rows_of,
            rows_of,
            P("fsdp"),
            rows_of,
            rows_of,
            rows_of,
        ),
        check_vma=False,
    )
```
